32 devices in a mesh: region: 2 (over x), range: 8 (over z, y), radial: 2 (over core).
Axes of the slice: x: 2, y: 2, z: 4, core: 2. Of those that a mesh axis runs over, the one named last changes fastest.
Arguments:
- refractivity: bfloat16 [512, 16, 4096], P(('region', 'radial'), None, 'range'), parts along dimension 0, may hold values from -6 to 6
- source: float32 [2, 8192], P(None, 'region'), parts along dimension 1, may hold values from -6 to 6
- terrain: int32 [512, 16], P(('region', 'radial'), 'range'), parts along dimension 0, may hold values from 0 to 511
- tile_map: int32 [512, 16], P(('region', 'radial'), 'range'), parts along dimension 0, may hold values from 0 to 255, as said below
Outputs:
- coverage: float32 [512, 128], P(('region', 'range', 'radial')), parts along dimension 0
The draws below stay inside these ranges and needn't reach their ends.
There are 2 independent parts, one for each index of `region`. The reference program is written for one: setup_inputs(seed, part) draws one part's arguments, and reference() takes and returns one part's arrays. A program takes and returns all parts, laid end to end along the dimension named above; each array names one. Nothing has to cross between parts.
Inputs may be any that keep to these rules, and one draw needn't show every extreme that they name: `tile_map`: every tile number is named by at least one radial and step.
All inputs are finite; a program needn't handle non-finite values.
Results may differ from the reference program's by a relative error of at most 0.0003.
Values may be sent and summed in bfloat16 or wider, within the bound.
No kernel may reach another device: no remote copies, remote signals or barrier semaphores. Data moves between devices by JAX's collectives and lax.ppermute only.
A program may use at most 64 MiB of HBM per device.

```python
import math
import jax
import jax.numpy as jnp
from jax import lax

H = 4096
FA = 64
BIN = 32
RADIALS = 256
STEPS = 16
TILES = 256


def draw_tile_map(key, part):
    key = jax.random.fold_in(key, 11)
    keys = jax.random.split(key, 5)
    total_cells = RADIALS * STEPS
    first_pass = jax.random.permutation(keys[0], TILES).astype(jnp.int32)
    low_pick = jax.random.randint(keys[1], (total_cells - TILES,), 0, TILES, dtype=jnp.int32)
    high_pick = jax.random.randint(keys[2], (total_cells - TILES,), 0, TILES, dtype=jnp.int32)
    relabel = jax.random.permutation(keys[3], TILES).astype(jnp.int32)
    remainder = relabel[jnp.minimum(low_pick, high_pick)]
    combined = jnp.concatenate([first_pass, remainder])
    ordering = jax.random.permutation(keys[4], total_cells)
    return combined[ordering].reshape(RADIALS, STEPS).astype(jnp.int32)


def place_ends(entries, key, low, top_value):
    shape = entries.shape
    spot = [jax.random.randint(jax.random.fold_in(key, axis), (), 0, shape[axis]) for axis in range(len(shape))]
    entries = entries.at[tuple(spot)].set(low)
    longest = shape.index(max(shape))
    spot[longest] = (spot[longest] + 1) % shape[longest]
    return entries.at[tuple(spot)].set(top_value)


def levels(key, shape, pieces, least, high):
    loudness = 1.0
    for dim, blocks in pieces:
        heights = jax.random.uniform(jax.random.fold_in(jax.random.fold_in(key, 6), dim), (blocks,), jnp.float32, least / len(pieces), high / len(pieces))
        loudness = loudness * jnp.repeat(jnp.exp(heights), shape[dim] // blocks).reshape((-1,) + (1,) * (len(shape) - 1 - dim))
    return loudness


def centred(own_key, shape, width, bound, cuts=(), kind=jnp.bfloat16):
    array = jax.random.normal(own_key, shape, jnp.float32) * width
    if len(cuts) > 0:
        array = levels(own_key, shape, cuts, -0.22, 0.18) * array
    return jnp.clip(array, min=-bound, max=bound).astype(kind)


def setup_inputs(seed: int = 0, part: int = 0) -> dict:
    splits = jax.random.split(jax.random.key(seed), 5)
    own_keys = jax.random.split(jax.random.fold_in(splits[4], part), 5)
    refractivity = centred(own_keys[0], (RADIALS, STEPS, H), 1.0, 6.0, ((0, 2), (2, 8)))
    source = centred(own_keys[1], (2, H), 1.0, 6.0, (), jnp.float32)
    terrain = place_ends(jax.random.randint(own_keys[2], (RADIALS, STEPS), 0, H // 8), jax.random.fold_in(own_keys[2], 1), 0, (H // 8) - 1).astype(jnp.int32)
    tile_map = draw_tile_map(jax.random.fold_in(jax.random.fold_in(splits[4], part), 71), part)
    return {"refractivity": refractivity, "source": source, "terrain": terrain, "tile_map": tile_map}


TILT_SLOPE = 2.0
SPREAD_RATE = 0.5
ABSORB_RATE = 0.05
PRECISE = lax.Precision.HIGHEST


def dft_table(extent):
    indices = jnp.arange(extent, dtype=jnp.int32)
    product = (indices[:, None] * indices[None, :]) % extent
    angles = (-2.0 * math.pi / extent) * product.astype(jnp.float32)
    return jnp.cos(angles), jnp.sin(angles)


def make_tables(height, factor):
    factor_b = height // factor
    inner_table = dft_table(factor_b)
    outer_table = dft_table(factor)
    q_second = jnp.arange(factor_b, dtype=jnp.int32)[:, None]
    n_first = jnp.arange(factor, dtype=jnp.int32)[None, :]
    twiddle_angle = (-2.0 * math.pi / height) * (q_second * n_first).astype(jnp.float32)
    twiddle = (jnp.cos(twiddle_angle), jnp.sin(twiddle_angle))
    frequency = n_first * factor_b + q_second
    signed = jnp.where(frequency >= height // 2, frequency - height, frequency).astype(jnp.float32)
    wavenumber = (2.0 * math.pi / height) * signed
    turning = -SPREAD_RATE * wavenumber * wavenumber
    spreading = (jnp.cos(turning), jnp.sin(turning))
    return inner_table, outer_table, twiddle, spreading


def complex_mix(pattern, real_part, imag_part, matrix_real, matrix_imag):
    def single(operand, matrix):
        return jnp.einsum(pattern, operand, matrix, precision=PRECISE)
    return (single(real_part, matrix_real) - single(imag_part, matrix_imag),
            single(real_part, matrix_imag) + single(imag_part, matrix_real))


def propagate(wave_field, tables):
    inner_table, outer_table, twiddle, spreading = tables
    batch_rows = wave_field.shape[1]
    height = wave_field.shape[2]
    factor = outer_table[0].shape[0]
    factor_b = inner_table[0].shape[0]
    real_part = wave_field[0].reshape(batch_rows, factor_b, factor)
    imag_part = wave_field[1].reshape(batch_rows, factor_b, factor)
    real_part, imag_part = complex_mix("bkn,kq->bqn", real_part, imag_part, inner_table[0], inner_table[1])
    real_part, imag_part = (real_part * twiddle[0] - imag_part * twiddle[1],
                            real_part * twiddle[1] + imag_part * twiddle[0])
    real_part, imag_part = complex_mix("bqn,nm->bqm", real_part, imag_part, outer_table[0], outer_table[1])
    real_part, imag_part = (real_part * spreading[0] - imag_part * spreading[1],
                            real_part * spreading[1] + imag_part * spreading[0])
    real_part, imag_part = complex_mix("bqm,mn->bqn", real_part, imag_part, outer_table[0], -outer_table[1])
    real_part, imag_part = (real_part * twiddle[0] + imag_part * twiddle[1],
                            imag_part * twiddle[0] - real_part * twiddle[1])
    real_part, imag_part = complex_mix("bqn,qk->bkn", real_part, imag_part, inner_table[0], -inner_table[1])
    normalize = 1.0 / height
    return real_part.reshape(batch_rows, height) * normalize, imag_part.reshape(batch_rows, height) * normalize


def advance(wave_field, refract_rows, terrain_rows, tables):
    height = wave_field.shape[2]
    real_part, imag_part = propagate(wave_field, tables)
    height_index = jnp.arange(height, dtype=jnp.int32)
    relative = height_index.astype(jnp.float32) / height
    top_depth = jnp.maximum(relative - 0.75, 0.0) * 4.0
    phase_angle = refract_rows.astype(jnp.float32) + TILT_SLOPE * relative
    retained = jnp.where(height_index[None, :] >= terrain_rows[:, None],
                         jnp.exp(-ABSORB_RATE * top_depth * top_depth), 0.0)
    cosine = jnp.cos(phase_angle)
    sine_part = jnp.sin(phase_angle)
    new_real = (real_part * cosine - imag_part * sine_part) * retained
    new_imag = (real_part * sine_part + imag_part * cosine) * retained
    return jnp.stack([new_real, new_imag])


def bin_power(wave_field, bin_width):
    energy = wave_field[0] * wave_field[0] + wave_field[1] * wave_field[1]
    return jnp.mean(energy.reshape(energy.shape[0], -1, bin_width), axis=2)


def reference(refractivity, source, terrain, tile_map):
    tables = make_tables(H, FA)
    launch = jnp.broadcast_to(source[:, None, :], (2, RADIALS, H)).astype(jnp.float32)

    def advance_once(wave_field, inputs):
        refract_rows, terrain_rows = inputs
        wave_field = advance(wave_field, refract_rows, terrain_rows, tables)
        return wave_field, bin_power(wave_field, BIN)

    refract_steps = jnp.swapaxes(refractivity, 0, 1)
    terrain_steps = jnp.swapaxes(terrain, 0, 1)
    _, powers = lax.scan(advance_once, launch, (refract_steps, terrain_steps))
    cell_tiles = jnp.swapaxes(tile_map, 0, 1).reshape(-1).astype(jnp.int32)
    tile_totals = jax.ops.segment_sum(powers.reshape(-1, powers.shape[2]), cell_tiles, num_segments=TILES)
    tile_counts = jax.ops.segment_sum(jnp.ones(cell_tiles.shape, jnp.float32), cell_tiles, num_segments=TILES)
    return tile_totals / tile_counts[:, None]
```

```python
import functools
import math

import jax
import jax.numpy as jnp
import ml_dtypes
import numpy as np
from jax import lax
from jax.experimental import pallas as pl
from jax.experimental.pallas import tpu as pltpu
from jax.sharding import PartitionSpec as P

H = 4096
BIN = 32
LANES = 128
ROWS = H // LANES
FOUR = 4
EIGHT = 8
BINS = H // BIN
TILE_DEV = 16
TILT_SLOPE = 2.0
SPREAD_RATE = 0.5
ABSORB_RATE = 0.05
TERRAIN_ROWS = 4
CHUNKS = (1.0,)
GROUP = 2

F32 = jnp.float32
BF16 = jnp.bfloat16


def split_np(table):
    high = table.astype(np.float32).astype(ml_dtypes.bfloat16)
    low = (table - high.astype(np.float64)).astype(ml_dtypes.bfloat16)
    return high, low


def tables():
    n = np.arange(LANES)
    angle = -2.0 * np.pi / LANES * (n[:, None] * n[None, :] % LANES)
    c, s = np.cos(angle), np.sin(angle)
    forward = np.block([[c, s], [-s, c]])
    inverse = np.block([[c, -s], [s, c]])
    weights = []
    for matrix in (forward, inverse):
        high, low = split_np(matrix)
        weights.append(np.concatenate([high, high, low], axis=0))
    q = np.arange(ROWS)
    angle = -2.0 * np.pi / H * (q[:, None] * n[None, :])
    twiddle = np.stack([np.cos(angle), np.sin(angle)]).astype(np.float32)
    frequency = q[:, None] + ROWS * n[None, :]
    signed = np.where(frequency >= H // 2, frequency - H, frequency)
    turning = -SPREAD_RATE * (2.0 * np.pi / H * signed) ** 2
    spread = (np.stack([np.cos(turning), np.sin(turning)]) / H).astype(np.float32)
    rel = np.arange(H).reshape(ROWS, LANES) / H
    tilt = (TILT_SLOPE * rel - 1.0).astype(np.float32)
    depth = np.maximum(rel - 0.75, 0.0) * 4.0
    absorb = np.exp(-ABSORB_RATE * depth * depth).astype(np.float32)
    bins = np.zeros((2 * LANES, BINS), np.float64)
    for lane in range(2 * LANES):
        bins[lane, (lane % LANES) // BIN :: LANES // BIN] = 1.0 / BIN
    return weights[0], weights[1], twiddle, spread, tilt, absorb, bins.astype(ml_dtypes.bfloat16)


def phase_polynomials():
    root = 2.0 ** 0.25
    sin_scale = root * math.sqrt(2.0)
    cos_scale = 2.0 * math.sqrt(2.0) / sin_scale
    limit = 7.001
    nodes = 0.5 * limit * limit * (1.0 + np.cos(np.pi * (np.arange(64) + 0.5) / 64))
    phi = np.sqrt(nodes)
    sine = np.polynomial.chebyshev.Chebyshev.fit(
        nodes, sin_scale * np.sin(phi / 4) / phi, 4, domain=[0, limit * limit]
    ).convert(kind=np.polynomial.Polynomial)
    cosine = np.polynomial.chebyshev.Chebyshev.fit(
        nodes, cos_scale * np.cos(phi / 4), 4, domain=[0, limit * limit]
    ).convert(kind=np.polynomial.Polynomial)
    return [float(v) for v in sine.coef], [float(v) for v in cosine.coef]


def unit(number, extent):
    angle = -2.0 * math.pi * (number % extent) / extent
    return math.cos(angle), math.sin(angle)


def cmul_const(value, factor):
    re, im = value
    c, s = factor
    if abs(s) < 1e-12 and c > 0:
        return value
    if abs(c) < 1e-12:
        return (im, -re) if s < 0 else (-im, re)
    return re * c - im * s, re * s + im * c


def add(a, b):
    return a[0] + b[0], a[1] + b[1]


def sub(a, b):
    return a[0] - b[0], a[1] - b[1]


def turn(a, sign):
    return (a[1], -a[0]) if sign < 0 else (-a[1], a[0])


def dft4(x, sign):
    a, b = add(x[0], x[2]), sub(x[0], x[2])
    c, d = add(x[1], x[3]), turn(sub(x[1], x[3]), sign)
    return [add(a, c), add(b, d), sub(a, c), sub(b, d)]


def eighth(a, sign):
    h = math.sqrt(0.5)
    re, im = a
    if sign < 0:
        return (re + im) * h, (im - re) * h
    return (re - im) * h, (re + im) * h


def dft8(x, sign):
    even = dft4(x[0::2], sign)
    odd = dft4(x[1::2], sign)
    odd = [odd[0], eighth(odd[1], sign), turn(odd[2], sign), turn(eighth(odd[3], sign), sign)]
    return [add(even[i], odd[i]) for i in range(4)] + [sub(even[i], odd[i]) for i in range(4)]


def split(value):
    high = value.astype(BF16)
    low = (value - high.astype(F32)).astype(BF16)
    return high, low


def march_kernel(
    steps, batch, heights, first,
    levels, terrain, cells, start_re, start_im, totals_in,
    w_forward, w_inverse, twiddle, spread, tilt, absorb, bins,
    end_re, end_im, totals,
    back_re, back_im, energy, power,
):
    sine, cosine = phase_polynomials()

    def enter(columns, jl, put_re, put_im):
        parts = dft4(columns, -1)
        for ql in range(FOUR):
            re, im = cmul_const(parts[ql], unit(ql * jl, ROWS))
            put_re[ql * EIGHT + jl] = re
            put_im[ql * EIGHT + jl] = im

    if first:
        for jl in range(EIGHT):
            columns = []
            for jh in range(FOUR):
                j = EIGHT * jh + jl
                shape = (batch, LANES)
                columns.append((
                    jnp.broadcast_to(start_re[j : j + 1, :], shape),
                    jnp.broadcast_to(start_im[j : j + 1, :], shape),
                ))
            enter(columns, jl, end_re, end_im)
    else:
        end_re[...] = start_re[...]
        end_im[...] = start_im[...]

    lane = lax.broadcasted_iota(jnp.int32, (batch, LANES), 1)

    def joined(pieces):
        re_high, re_low = split(jnp.concatenate([p[0] for p in pieces], axis=0))
        im_high, im_low = split(jnp.concatenate([p[1] for p in pieces], axis=0))
        return jnp.concatenate([re_high, im_high, re_low, im_low, re_high, im_high], axis=1)

    def parted(product, count):
        return [
            (product[i * batch : (i + 1) * batch, :LANES], product[i * batch : (i + 1) * batch, LANES:])
            for i in range(count)
        ]

    def step(t, carry):
        for base in range(0, FOUR, GROUP):
            qs = [ql + FOUR * qh for ql in range(base, base + GROUP) for qh in range(EIGHT)]
            pieces = []
            for ql in range(base, base + GROUP):
                column = [(end_re[ql * EIGHT + jl], end_im[ql * EIGHT + jl]) for jl in range(EIGHT)]
                for qh, (re, im) in enumerate(dft8(column, -1)):
                    q = ql + FOUR * qh
                    c, s = twiddle[0, q : q + 1, :], twiddle[1, q : q + 1, :]
                    pieces.append((re * c - im * s, re * s + im * c))
            product = jnp.dot(joined(pieces), w_forward[...], preferred_element_type=F32)
            pieces = []
            for q, (re, im) in zip(qs, parted(product, len(qs))):
                c, s = spread[0, q : q + 1, :], spread[1, q : q + 1, :]
                pieces.append((re * c - im * s, re * s + im * c))
            product = jnp.dot(joined(pieces), w_inverse[...], preferred_element_type=F32)
            pieces = []
            for q, (re, im) in zip(qs, parted(product, len(qs))):
                c, s = twiddle[0, q : q + 1, :], twiddle[1, q : q + 1, :]
                pieces.append((re * c + im * s, im * c - re * s))
            for i in range(GROUP):
                column = dft8(pieces[i * EIGHT : (i + 1) * EIGHT], 1)
                for jl in range(EIGHT):
                    back_re[(base + i) * EIGHT + jl] = column[jl][0]
                    back_im[(base + i) * EIGHT + jl] = column[jl][1]

        for jl in range(EIGHT):
            column = []
            for ql in range(FOUR):
                c, s = unit(ql * jl, ROWS)
                column.append(cmul_const((back_re[ql * EIGHT + jl], back_im[ql * EIGHT + jl]), (c, -s)))
            column = dft4(column, 1)
            moved = []
            for jh in range(FOUR):
                j = EIGHT * jh + jl
                place = j * LANES
                raw = levels[place // heights, t, :, place % heights : place % heights + LANES]
                phi = raw.astype(F32) + tilt[j : j + 1, :]
                u = phi * phi
                sin_poly, cos_poly = sine[-1], cosine[-1]
                for a, b in zip(sine[-2::-1], cosine[-2::-1]):
                    sin_poly = sin_poly * u + a
                    cos_poly = cos_poly * u + b
                small = sin_poly * phi
                double = small * cos_poly
                turned_c = 1.0 - double * double
                turned_s = double * (math.sqrt(2.0) - small * small)
                re, im = column[jh]
                if (j + 1) * LANES > 3 * H // 4:
                    loss = absorb[j : j + 1, :]
                    re, im = re * loss, im * loss
                re, im = re * turned_c - im * turned_s, re * turned_s + im * turned_c
                if j < TERRAIN_ROWS:
                    open_air = lane + j * LANES >= terrain[t]
                    re, im = jnp.where(open_air, re, 0.0), jnp.where(open_air, im, 0.0)
                high, low = split(re * re + im * im)
                energy[j * batch : (j + 1) * batch, :] = jnp.concatenate([high, low], axis=1)
                moved.append((re, im))
            enter(moved, jl, end_re, end_im)

        summed = jnp.dot(energy[...], bins[...], preferred_element_type=F32)
        row = summed[:batch]
        for j in range(1, ROWS):
            row = jnp.where(lane // (LANES // BIN) == j, summed[j * batch : (j + 1) * batch], row)
        power[pl.ds(pl.multiple_of(t * batch, batch), batch), :] = row
        return carry

    lax.fori_loop(0, steps, step, 0)

    count = steps * batch
    tiles = totals.shape[0]
    hot = (lax.broadcasted_iota(jnp.int32, (tiles, count), 0) == cells[...]).astype(F32).astype(BF16)
    value = power[...]
    high, rest = value.astype(BF16), None
    rest = value - high.astype(F32)
    middle = rest.astype(BF16)
    low = (rest - middle.astype(F32)).astype(BF16)
    gain = jnp.dot(hot, high, preferred_element_type=F32)
    gain += jnp.dot(hot, middle, preferred_element_type=F32)
    gain += jnp.dot(hot, low, preferred_element_type=F32)
    if first:
        totals[...] = gain
    else:
        totals[...] = totals_in[...] + gain


def march(levels, terrain, cells, start, totals, consts, tiles, first):
    sources, steps, batch, heights = levels.shape
    state = jax.ShapeDtypeStruct((ROWS, batch, LANES), F32)
    vmem = pl.BlockSpec(memory_space=pltpu.VMEM)
    call = pl.pallas_call(
        functools.partial(march_kernel, steps, batch, heights, first),
        out_shape=(state, state, jax.ShapeDtypeStruct((tiles, BINS), F32)),
        in_specs=[vmem] * 13,
        out_specs=(vmem, vmem, vmem),
        scratch_shapes=[
            pltpu.VMEM((ROWS, batch, LANES), F32),
            pltpu.VMEM((ROWS, batch, LANES), F32),
            pltpu.VMEM((ROWS * batch, 2 * LANES), BF16),
            pltpu.VMEM((steps * batch, BINS), F32),
        ],
        compiler_params=pltpu.CompilerParams(vmem_limit_bytes=48 * 1024 * 1024),
        cost_estimate=pl.CostEstimate(
            flops=steps * batch * H * 3 * 8 * LANES, bytes_accessed=4 * 1024 * 1024, transcendentals=0
        ),
    )
    return call(levels, terrain, cells, *start, totals, *consts)


def local(refractivity, source, terrain, tile_map):
    sections = lax.axis_size("range")
    owners = sections * lax.axis_size("radial")
    tiles = TILE_DEV * owners
    radials, steps, heights = refractivity.shape
    own = radials // sections
    batch = -(-own // 16) * 16

    small = jnp.stack([terrain, tile_map])
    everyone = lax.all_gather(small, ("range", "radial"))
    everyone = everyone.reshape(sections, lax.axis_size("radial"), *small.shape)
    my_ids = (lax.axis_index("range") * lax.axis_size("radial") + lax.axis_index("radial")) * TILE_DEV
    my_ids = my_ids + jnp.arange(TILE_DEV, dtype=jnp.int32)
    counts = jnp.sum(
        (my_ids[:, None] == everyone[:, :, 1].reshape(1, -1)).astype(F32), axis=1
    )
    mine = lax.dynamic_index_in_dim(everyone, lax.axis_index("radial"), 1, keepdims=False)
    mine = lax.dynamic_slice_in_dim(mine, lax.axis_index("range") * own, own, 2)
    mine = jnp.transpose(mine, (1, 0, 3, 2)).reshape(2, steps, own)
    pad = ((0, 0), (0, batch - own))
    terrain_all = jnp.pad(mine[0], pad)
    cells_all = jnp.pad(mine[1], pad, constant_values=-1)
    terrain_all = jnp.broadcast_to(terrain_all[:, :, None], (steps, batch, LANES))

    consts = [jnp.asarray(v) for v in tables()]
    edges = [0]
    for share in CHUNKS:
        edges.append(edges[-1] + max(1, round(share * steps)))
    start = (source[0].reshape(ROWS, LANES), source[1].reshape(ROWS, LANES))
    totals = jnp.zeros((tiles, BINS), F32)
    pieces = []
    for begin, end in zip(edges[:-1], edges[1:]):
        piece = refractivity[:, begin:end].reshape(sections, own, end - begin, heights)
        piece = jnp.transpose(piece, (0, 2, 1, 3))
        pieces.append(lax.all_to_all(piece, "range", 0, 0, tiled=True))
    for piece, begin, end in zip(pieces, edges[:-1], edges[1:]):
        piece = jnp.pad(piece, ((0, 0), (0, 0), (0, batch - own), (0, 0)))
        *start, totals = march(
            piece, terrain_all[begin:end], cells_all[begin:end].reshape(1, -1),
            start, totals, consts, tiles, begin == 0,
        )
    sent = lax.all_to_all(
        totals.reshape(owners, TILE_DEV, BINS), ("range", "radial"), 0, 0, tiled=True
    )
    return jnp.sum(sent, axis=0) / counts[:, None]


def solution(mesh):
    in_specs = (
        P(("region", "radial"), None, "range"),
        P(None, "region"),
        P(("region", "radial"), "range"),
        P(("region", "radial"), "range"),
    )
    out_specs = P(("region", "range", "radial"), None)
    return jax.shard_map(local, mesh=mesh, in_specs=in_specs, out_specs=out_specs, check_vma=False)
```

```python
import functools
import math

import jax
import jax.numpy as jnp
import ml_dtypes
import numpy as np
from jax import lax
from jax.experimental import pallas as pl
from jax.experimental.pallas import tpu as pltpu
from jax.sharding import PartitionSpec as P

H = 4096
BIN = 32
LANES = 128
ROWS = H // LANES
FOUR = 4
EIGHT = 8
BINS = H // BIN
TILE_DEV = 16
TILT_SLOPE = 2.0
SPREAD_RATE = 0.5
ABSORB_RATE = 0.05
TERRAIN_ROWS = 4
CHUNKS = (0.3125, 0.4375, 0.25)
GROUP = 2

F32 = jnp.float32
BF16 = jnp.bfloat16


def split_np(table):
    high = table.astype(np.float32).astype(ml_dtypes.bfloat16)
    low = (table - high.astype(np.float64)).astype(ml_dtypes.bfloat16)
    return high, low


def tables():
    n = np.arange(LANES)
    angle = -2.0 * np.pi / LANES * (n[:, None] * n[None, :] % LANES)
    c, s = np.cos(angle), np.sin(angle)
    forward = np.block([[c, s], [-s, c]])
    inverse = np.block([[c, -s], [s, c]])
    weights = []
    for matrix in (forward, inverse):
        high, low = split_np(matrix)
        weights.append(np.concatenate([high, high, low], axis=0))
    q = np.arange(ROWS)
    angle = -2.0 * np.pi / H * (q[:, None] * n[None, :])
    twiddle = np.stack([np.cos(angle), np.sin(angle)]).astype(np.float32)
    frequency = q[:, None] + ROWS * n[None, :]
    signed = np.where(frequency >= H // 2, frequency - H, frequency)
    turning = -SPREAD_RATE * (2.0 * np.pi / H * signed) ** 2
    spread = (np.stack([np.cos(turning), np.sin(turning)]) / H).astype(np.float32)
    rel = np.arange(H).reshape(ROWS, LANES) / H
    tilt = (TILT_SLOPE * rel - 1.0).astype(np.float32)
    depth = np.maximum(rel - 0.75, 0.0) * 4.0
    absorb = np.exp(-ABSORB_RATE * depth * depth).astype(np.float32)
    bins = np.zeros((2 * LANES, BINS), np.float64)
    for lane in range(2 * LANES):
        bins[lane, (lane % LANES) // BIN :: LANES // BIN] = 1.0 / BIN
    return weights[0], weights[1], twiddle, spread, tilt, absorb, bins.astype(ml_dtypes.bfloat16)


def phase_polynomials():
    root = 2.0 ** 0.25
    sin_scale = root * math.sqrt(2.0)
    cos_scale = 2.0 * math.sqrt(2.0) / sin_scale
    limit = 7.001
    nodes = 0.5 * limit * limit * (1.0 + np.cos(np.pi * (np.arange(64) + 0.5) / 64))
    phi = np.sqrt(nodes)
    sine = np.polynomial.chebyshev.Chebyshev.fit(
        nodes, sin_scale * np.sin(phi / 4) / phi, 4, domain=[0, limit * limit]
    ).convert(kind=np.polynomial.Polynomial)
    cosine = np.polynomial.chebyshev.Chebyshev.fit(
        nodes, cos_scale * np.cos(phi / 4), 4, domain=[0, limit * limit]
    ).convert(kind=np.polynomial.Polynomial)
    return [float(v) for v in sine.coef], [float(v) for v in cosine.coef]


def unit(number, extent):
    angle = -2.0 * math.pi * (number % extent) / extent
    return math.cos(angle), math.sin(angle)


def cmul_const(value, factor):
    re, im = value
    c, s = factor
    if abs(s) < 1e-12 and c > 0:
        return value
    if abs(c) < 1e-12:
        return (im, -re) if s < 0 else (-im, re)
    return re * c - im * s, re * s + im * c


def add(a, b):
    return a[0] + b[0], a[1] + b[1]


def sub(a, b):
    return a[0] - b[0], a[1] - b[1]


def turn(a, sign):
    return (a[1], -a[0]) if sign < 0 else (-a[1], a[0])


def dft4(x, sign):
    a, b = add(x[0], x[2]), sub(x[0], x[2])
    c, d = add(x[1], x[3]), turn(sub(x[1], x[3]), sign)
    return [add(a, c), add(b, d), sub(a, c), sub(b, d)]


def eighth(a, sign):
    h = math.sqrt(0.5)
    re, im = a
    if sign < 0:
        return (re + im) * h, (im - re) * h
    return (re - im) * h, (re + im) * h


def dft8(x, sign):
    even = dft4(x[0::2], sign)
    odd = dft4(x[1::2], sign)
    odd = [odd[0], eighth(odd[1], sign), turn(odd[2], sign), turn(eighth(odd[3], sign), sign)]
    return [add(even[i], odd[i]) for i in range(4)] + [sub(even[i], odd[i]) for i in range(4)]


def split(value):
    high = value.astype(BF16)
    low = (value - high.astype(F32)).astype(BF16)
    return high, low


def march_kernel(steps, batch, heights, first, sections, section, *refs):
    slabs, refs = refs[:sections], refs[sections:]
    (
        terrain, cells, start_re, start_im, totals_in,
        w_forward, w_inverse, twiddle, spread, tilt, absorb, bins,
        end_re, end_im, totals,
        levels, back_re, back_im, energy, power,
    ) = refs
    sine, cosine = phase_polynomials()
    for d in range(sections):
        levels[section[0] ^ d] = slabs[d][...]

    def enter(columns, jl, put_re, put_im):
        parts = dft4(columns, -1)
        for ql in range(FOUR):
            re, im = cmul_const(parts[ql], unit(ql * jl, ROWS))
            put_re[ql * EIGHT + jl] = re
            put_im[ql * EIGHT + jl] = im

    if first:
        for jl in range(EIGHT):
            columns = []
            for jh in range(FOUR):
                j = EIGHT * jh + jl
                shape = (batch, LANES)
                columns.append((
                    jnp.broadcast_to(start_re[j : j + 1, :], shape),
                    jnp.broadcast_to(start_im[j : j + 1, :], shape),
                ))
            enter(columns, jl, end_re, end_im)
    else:
        end_re[...] = start_re[...]
        end_im[...] = start_im[...]

    lane = lax.broadcasted_iota(jnp.int32, (batch, LANES), 1)

    def joined(pieces):
        re_high, re_low = split(jnp.concatenate([p[0] for p in pieces], axis=0))
        im_high, im_low = split(jnp.concatenate([p[1] for p in pieces], axis=0))
        return jnp.concatenate([re_high, im_high, re_low, im_low, re_high, im_high], axis=1)

    def parted(product, count):
        return [
            (product[i * batch : (i + 1) * batch, :LANES], product[i * batch : (i + 1) * batch, LANES:])
            for i in range(count)
        ]

    def step(t, carry):
        for base in range(0, FOUR, GROUP):
            qs = [ql + FOUR * qh for ql in range(base, base + GROUP) for qh in range(EIGHT)]
            pieces = []
            for ql in range(base, base + GROUP):
                column = [(end_re[ql * EIGHT + jl], end_im[ql * EIGHT + jl]) for jl in range(EIGHT)]
                for qh, (re, im) in enumerate(dft8(column, -1)):
                    q = ql + FOUR * qh
                    c, s = twiddle[0, q : q + 1, :], twiddle[1, q : q + 1, :]
                    pieces.append((re * c - im * s, re * s + im * c))
            product = jnp.dot(joined(pieces), w_forward[...], preferred_element_type=F32)
            pieces = []
            for q, (re, im) in zip(qs, parted(product, len(qs))):
                c, s = spread[0, q : q + 1, :], spread[1, q : q + 1, :]
                pieces.append((re * c - im * s, re * s + im * c))
            product = jnp.dot(joined(pieces), w_inverse[...], preferred_element_type=F32)
            pieces = []
            for q, (re, im) in zip(qs, parted(product, len(qs))):
                c, s = twiddle[0, q : q + 1, :], twiddle[1, q : q + 1, :]
                pieces.append((re * c + im * s, im * c - re * s))
            for i in range(GROUP):
                column = dft8(pieces[i * EIGHT : (i + 1) * EIGHT], 1)
                for jl in range(EIGHT):
                    back_re[(base + i) * EIGHT + jl] = column[jl][0]
                    back_im[(base + i) * EIGHT + jl] = column[jl][1]

        for jl in range(EIGHT):
            column = []
            for ql in range(FOUR):
                c, s = unit(ql * jl, ROWS)
                column.append(cmul_const((back_re[ql * EIGHT + jl], back_im[ql * EIGHT + jl]), (c, -s)))
            column = dft4(column, 1)
            moved = []
            for jh in range(FOUR):
                j = EIGHT * jh + jl
                place = j * LANES
                raw = levels[place // heights, t, :, place % heights : place % heights + LANES]
                phi = raw.astype(F32) + tilt[j : j + 1, :]
                u = phi * phi
                sin_poly, cos_poly = sine[-1], cosine[-1]
                for a, b in zip(sine[-2::-1], cosine[-2::-1]):
                    sin_poly = sin_poly * u + a
                    cos_poly = cos_poly * u + b
                small = sin_poly * phi
                double = small * cos_poly
                turned_c = 1.0 - double * double
                turned_s = double * (math.sqrt(2.0) - small * small)
                re, im = column[jh]
                if (j + 1) * LANES > 3 * H // 4:
                    loss = absorb[j : j + 1, :]
                    re, im = re * loss, im * loss
                re, im = re * turned_c - im * turned_s, re * turned_s + im * turned_c
                if j < TERRAIN_ROWS:
                    open_air = lane + j * LANES >= terrain[t]
                    re, im = jnp.where(open_air, re, 0.0), jnp.where(open_air, im, 0.0)
                high, low = split(re * re + im * im)
                energy[j * batch : (j + 1) * batch, :] = jnp.concatenate([high, low], axis=1)
                moved.append((re, im))
            enter(moved, jl, end_re, end_im)

        summed = jnp.dot(energy[...], bins[...], preferred_element_type=F32)
        row = summed[:batch]
        for j in range(1, ROWS):
            row = jnp.where(lane // (LANES // BIN) == j, summed[j * batch : (j + 1) * batch], row)
        power[pl.ds(pl.multiple_of(t * batch, batch), batch), :] = row
        return carry

    lax.fori_loop(0, steps, step, 0)

    count = steps * batch
    tiles = totals.shape[0]
    hot = (lax.broadcasted_iota(jnp.int32, (tiles, count), 0) == cells[...]).astype(F32).astype(BF16)
    value = power[...]
    high, rest = value.astype(BF16), None
    rest = value - high.astype(F32)
    middle = rest.astype(BF16)
    low = (rest - middle.astype(F32)).astype(BF16)
    gain = jnp.dot(hot, high, preferred_element_type=F32)
    gain += jnp.dot(hot, middle, preferred_element_type=F32)
    gain += jnp.dot(hot, low, preferred_element_type=F32)
    if first:
        totals[...] = gain
    else:
        totals[...] = totals_in[...] + gain


def march(section, slabs, terrain, cells, start, totals, consts, tiles, first):
    sections = len(slabs)
    steps, batch, heights = slabs[0].shape
    state = jax.ShapeDtypeStruct((ROWS, batch, LANES), F32)
    vmem = pl.BlockSpec(memory_space=pltpu.VMEM)
    smem = pl.BlockSpec(memory_space=pltpu.SMEM)
    call = pl.pallas_call(
        functools.partial(march_kernel, steps, batch, heights, first, sections),
        out_shape=(state, state, jax.ShapeDtypeStruct((tiles, BINS), F32)),
        in_specs=[smem] + [vmem] * (sections + 12),
        out_specs=(vmem, vmem, vmem),
        scratch_shapes=[
            pltpu.VMEM((sections, steps, batch, heights), BF16),
            pltpu.VMEM((ROWS, batch, LANES), F32),
            pltpu.VMEM((ROWS, batch, LANES), F32),
            pltpu.VMEM((ROWS * batch, 2 * LANES), BF16),
            pltpu.VMEM((steps * batch, BINS), F32),
        ],
        compiler_params=pltpu.CompilerParams(vmem_limit_bytes=48 * 1024 * 1024),
        cost_estimate=pl.CostEstimate(
            flops=steps * 1_600_000_000, bytes_accessed=4 * 1024 * 1024, transcendentals=0
        ),
        name="march",
    )
    return call(section, *slabs, terrain, cells, *start, totals, *consts)


def cut_kernel(begin, end, own, section, levels, *refs):
    slabs, rows = refs[:-1], refs[-1]
    steps, heights = levels.shape[1:]
    columns = [slice(c * LANES, (c + 1) * LANES) for c in range(heights // LANES)]
    for d, slab in enumerate(slabs):
        base = (section[0] ^ d) * own
        for b in range(own):
            for c, column in enumerate(columns):
                rows[c, b * steps : (b + 1) * steps, :] = levels[base + b, :, column].astype(F32)
        for t in range(begin, end):
            for c, column in enumerate(columns):
                taken = rows[c, pl.ds(t, own, stride=steps), :].astype(BF16)
                if own < slab.shape[1]:
                    taken = jnp.pad(taken, ((0, slab.shape[1] - own), (0, 0)))
                slab[t - begin, :, column] = taken


def cut(section, levels, begin, end, sections, own, batch):
    steps, heights = levels.shape[1:]
    slab = jax.ShapeDtypeStruct((end - begin, batch, heights), BF16)
    vmem = pl.BlockSpec(memory_space=pltpu.VMEM)
    smem = pl.BlockSpec(memory_space=pltpu.SMEM)
    call = pl.pallas_call(
        functools.partial(cut_kernel, begin, end, own),
        out_shape=(slab,) * sections,
        in_specs=[smem, vmem],
        out_specs=(vmem,) * sections,
        scratch_shapes=[pltpu.VMEM((heights // LANES, own * steps, LANES), F32)],
        compiler_params=pltpu.CompilerParams(vmem_limit_bytes=32 * 1024 * 1024),
        cost_estimate=pl.CostEstimate(flops=1_000_000_000, bytes_accessed=4 * 1024 * 1024, transcendentals=0),
        name="cut",
    )
    return call(section, levels)


def local(refractivity, source, terrain, tile_map):
    sections = lax.axis_size("range")
    owners = sections * lax.axis_size("radial")
    tiles = TILE_DEV * owners
    radials, steps, heights = refractivity.shape
    own = radials // sections
    batch = -(-own // 16) * 16

    small = jnp.concatenate([terrain.T, tile_map.T])
    edges = [0]
    for share in CHUNKS:
        edges.append(edges[-1] + max(1, round(share * steps)))
    section = lax.axis_index("range").astype(jnp.int32).reshape(1)
    pieces = []
    for begin, end in zip(edges[:-1], edges[1:]):
        slabs = list(cut(section, refractivity, begin, end, sections, own, batch))
        for d in reversed(range(1, sections)):
            slabs[d] = lax.ppermute(slabs[d], "range", [(i, i ^ d) for i in range(sections)])
        pieces.append(slabs)
    everyone = lax.all_to_all(
        jnp.broadcast_to(small, (owners, *small.shape)), ("range", "radial"), 0, 0, tiled=True
    )
    everyone = everyone.reshape(sections, lax.axis_size("radial"), 2, -1, radials)
    my_ids = (lax.axis_index("range") * lax.axis_size("radial") + lax.axis_index("radial")) * TILE_DEV
    my_ids = my_ids + jnp.arange(TILE_DEV, dtype=jnp.int32)
    counts = jnp.sum(
        (my_ids[:, None] == everyone[:, :, 1].reshape(1, -1)).astype(F32), axis=1
    )
    mine = lax.dynamic_index_in_dim(everyone, lax.axis_index("radial"), 1, keepdims=False)
    mine = lax.dynamic_slice_in_dim(mine, lax.axis_index("range") * own, own, 3)
    mine = jnp.transpose(mine, (1, 0, 2, 3)).reshape(2, steps, own)
    pad = ((0, 0), (0, batch - own))
    terrain_all = jnp.pad(mine[0], pad)
    cells_all = jnp.pad(mine[1], pad, constant_values=-1)
    terrain_all = jnp.broadcast_to(terrain_all[:, :, None], (steps, batch, LANES))

    consts = [jnp.asarray(v) for v in tables()]
    start = (source[0].reshape(ROWS, LANES), source[1].reshape(ROWS, LANES))
    totals = jnp.zeros((tiles, BINS), F32)
    for piece, begin, end in zip(pieces, edges[:-1], edges[1:]):
        *start, totals = march(
            section, piece, terrain_all[begin:end], cells_all[begin:end].reshape(1, -1),
            start, totals, consts, tiles, begin == 0,
        )
    sent = lax.all_to_all(
        totals.reshape(owners, TILE_DEV, BINS), ("range", "radial"), 0, 0, tiled=True
    )
    return jnp.sum(sent, axis=0) / counts[:, None]


def solution(mesh):
    in_specs = (
        P(("region", "radial"), None, "range"),
        P(None, "region"),
        P(("region", "radial"), "range"),
        P(("region", "radial"), "range"),
    )
    out_specs = P(("region", "range", "radial"), None)
    return jax.shard_map(local, mesh=mesh, in_specs=in_specs, out_specs=out_specs, check_vma=False)
```

```python
import functools
import math

import jax
import jax.numpy as jnp
import ml_dtypes
import numpy as np
from jax import lax
from jax.experimental import pallas as pl
from jax.experimental.pallas import tpu as pltpu
from jax.sharding import PartitionSpec as P

H = 4096
BIN = 32
LANES = 128
ROWS = H // LANES
FOUR = 4
EIGHT = 8
BINS = H // BIN
TILE_DEV = 16
TILT_SLOPE = 2.0
SPREAD_RATE = 0.5
ABSORB_RATE = 0.05
TERRAIN_ROWS = 4
WHOLE_SHARE = 0.6875
GROUP = 2

F32 = jnp.float32
BF16 = jnp.bfloat16


def split_np(table):
    high = table.astype(np.float32).astype(ml_dtypes.bfloat16)
    low = (table - high.astype(np.float64)).astype(ml_dtypes.bfloat16)
    return high, low


def tables():
    n = np.arange(LANES)
    angle = -2.0 * np.pi / LANES * (n[:, None] * n[None, :] % LANES)
    c, s = np.cos(angle), np.sin(angle)
    forward = np.block([[c, s], [-s, c]])
    inverse = np.block([[c, -s], [s, c]])
    weights = []
    for matrix in (forward, inverse):
        high, low = split_np(matrix)
        weights.append(np.concatenate([high, high, low], axis=0))
    q = np.arange(ROWS)
    angle = -2.0 * np.pi / H * (q[:, None] * n[None, :])
    twiddle = np.stack([np.cos(angle), np.sin(angle)]).astype(np.float32)
    frequency = q[:, None] + ROWS * n[None, :]
    signed = np.where(frequency >= H // 2, frequency - H, frequency)
    turning = -SPREAD_RATE * (2.0 * np.pi / H * signed) ** 2
    spread = (np.stack([np.cos(turning), np.sin(turning)]) / H).astype(np.float32)
    rel = np.arange(H).reshape(ROWS, LANES) / H
    tilt = (TILT_SLOPE * rel - 1.0).astype(np.float32)
    depth = np.maximum(rel - 0.75, 0.0) * 4.0
    absorb = np.exp(-ABSORB_RATE * depth * depth).astype(np.float32)
    bins = np.zeros((2 * LANES, BINS), np.float64)
    for lane in range(2 * LANES):
        bins[lane, (lane % LANES) // BIN :: LANES // BIN] = 1.0 / BIN
    return weights[0], weights[1], twiddle, spread, tilt, absorb, bins.astype(ml_dtypes.bfloat16)


def phase_polynomials():
    root = 2.0 ** 0.25
    sin_scale = root * math.sqrt(2.0)
    cos_scale = 2.0 * math.sqrt(2.0) / sin_scale
    limit = 7.001
    nodes = 0.5 * limit * limit * (1.0 + np.cos(np.pi * (np.arange(64) + 0.5) / 64))
    phi = np.sqrt(nodes)
    sine = np.polynomial.chebyshev.Chebyshev.fit(
        nodes, sin_scale * np.sin(phi / 4) / phi, 4, domain=[0, limit * limit]
    ).convert(kind=np.polynomial.Polynomial)
    cosine = np.polynomial.chebyshev.Chebyshev.fit(
        nodes, cos_scale * np.cos(phi / 4), 4, domain=[0, limit * limit]
    ).convert(kind=np.polynomial.Polynomial)
    return [float(v) for v in sine.coef], [float(v) for v in cosine.coef]


def unit(number, extent):
    angle = -2.0 * math.pi * (number % extent) / extent
    return math.cos(angle), math.sin(angle)


def cmul_const(value, factor):
    re, im = value
    c, s = factor
    if abs(s) < 1e-12 and c > 0:
        return value
    if abs(c) < 1e-12:
        return (im, -re) if s < 0 else (-im, re)
    return re * c - im * s, re * s + im * c


def add(a, b):
    return a[0] + b[0], a[1] + b[1]


def sub(a, b):
    return a[0] - b[0], a[1] - b[1]


def turn(a, sign):
    return (a[1], -a[0]) if sign < 0 else (-a[1], a[0])


def dft4(x, sign):
    a, b = add(x[0], x[2]), sub(x[0], x[2])
    c, d = add(x[1], x[3]), turn(sub(x[1], x[3]), sign)
    return [add(a, c), add(b, d), sub(a, c), sub(b, d)]


def eighth(a, sign):
    h = math.sqrt(0.5)
    re, im = a
    if sign < 0:
        return (re + im) * h, (im - re) * h
    return (re - im) * h, (re + im) * h


def dft8(x, sign):
    even = dft4(x[0::2], sign)
    odd = dft4(x[1::2], sign)
    odd = [odd[0], eighth(odd[1], sign), turn(odd[2], sign), turn(eighth(odd[3], sign), sign)]
    return [add(even[i], odd[i]) for i in range(4)] + [sub(even[i], odd[i]) for i in range(4)]


def split(value):
    high = value.astype(BF16)
    low = (value - high.astype(F32)).astype(BF16)
    return high, low


def march_kernel(steps, batch, heights, first, count, section, *refs):
    slabs, refs = refs[:count], refs[count:]
    (
        terrain, cells, start_re, start_im, totals_in,
        w_forward, w_inverse, twiddle, spread, tilt, absorb, bins,
        end_re, end_im, totals,
        levels, arrived, back_re, back_im, energy, power,
    ) = refs
    sine, cosine = phase_polynomials()
    copies = []
    for d, slab in enumerate(slabs):
        place = levels if count == 1 else levels.at[section[0] ^ d]
        copies.append(pltpu.make_async_copy(slab, place, arrived.at[d]))
        copies[-1].start()

    def enter(columns, jl, put_re, put_im):
        parts = dft4(columns, -1)
        for ql in range(FOUR):
            re, im = cmul_const(parts[ql], unit(ql * jl, ROWS))
            put_re[ql * EIGHT + jl] = re
            put_im[ql * EIGHT + jl] = im

    if first:
        for jl in range(EIGHT):
            columns = []
            for jh in range(FOUR):
                j = EIGHT * jh + jl
                shape = (batch, LANES)
                columns.append((
                    jnp.broadcast_to(start_re[j : j + 1, :], shape),
                    jnp.broadcast_to(start_im[j : j + 1, :], shape),
                ))
            enter(columns, jl, end_re, end_im)
    else:
        end_re[...] = start_re[...]
        end_im[...] = start_im[...]

    lane = lax.broadcasted_iota(jnp.int32, (batch, LANES), 1)

    def joined(pieces):
        re_high, re_low = split(jnp.concatenate([p[0] for p in pieces], axis=0))
        im_high, im_low = split(jnp.concatenate([p[1] for p in pieces], axis=0))
        return jnp.concatenate([re_high, im_high, re_low, im_low, re_high, im_high], axis=1)

    def parted(product, count):
        return [
            (product[i * batch : (i + 1) * batch, :LANES], product[i * batch : (i + 1) * batch, LANES:])
            for i in range(count)
        ]

    def binned(t):
        summed = jnp.dot(energy[...], bins[...], preferred_element_type=F32)
        row = summed[:batch]
        for j in range(1, ROWS):
            row = jnp.where(lane // (LANES // BIN) == j, summed[j * batch : (j + 1) * batch], row)
        power[pl.ds(pl.multiple_of(t * batch, batch), batch), :] = row

    def step(t, carry):
        groups = [list(range(base, base + GROUP)) for base in range(0, FOUR, GROUP)]
        rows = [[ql + FOUR * qh for ql in group for qh in range(EIGHT)] for group in groups]
        products = []
        for group in groups:
            pieces = []
            for ql in group:
                column = [(end_re[ql * EIGHT + jl], end_im[ql * EIGHT + jl]) for jl in range(EIGHT)]
                for qh, (re, im) in enumerate(dft8(column, -1)):
                    q = ql + FOUR * qh
                    c, s = twiddle[0, q : q + 1, :], twiddle[1, q : q + 1, :]
                    pieces.append((re * c - im * s, re * s + im * c))
            products.append(jnp.dot(joined(pieces), w_forward[...], preferred_element_type=F32))
        binned(jnp.maximum(t - 1, 0))
        for i, qs in enumerate(rows):
            pieces = []
            for q, (re, im) in zip(qs, parted(products[i], len(qs))):
                c, s = spread[0, q : q + 1, :], spread[1, q : q + 1, :]
                pieces.append((re * c - im * s, re * s + im * c))
            products[i] = jnp.dot(joined(pieces), w_inverse[...], preferred_element_type=F32)
        for i, qs in enumerate(rows):
            pieces = []
            for q, (re, im) in zip(qs, parted(products[i], len(qs))):
                c, s = twiddle[0, q : q + 1, :], twiddle[1, q : q + 1, :]
                pieces.append((re * c + im * s, im * c - re * s))
            for k, ql in enumerate(groups[i]):
                column = dft8(pieces[k * EIGHT : (k + 1) * EIGHT], 1)
                for jl in range(EIGHT):
                    back_re[ql * EIGHT + jl] = column[jl][0]
                    back_im[ql * EIGHT + jl] = column[jl][1]

        for jl in range(EIGHT):
            column = []
            for ql in range(FOUR):
                c, s = unit(ql * jl, ROWS)
                column.append(cmul_const((back_re[ql * EIGHT + jl], back_im[ql * EIGHT + jl]), (c, -s)))
            column = dft4(column, 1)
            moved = []
            for jh in range(FOUR):
                j = EIGHT * jh + jl
                place = j * LANES
                raw = levels[place // heights, t, :, place % heights : place % heights + LANES]
                phi = raw.astype(F32) + tilt[j : j + 1, :]
                u = phi * phi
                sin_poly, cos_poly = sine[-1], cosine[-1]
                for a, b in zip(sine[-2::-1], cosine[-2::-1]):
                    sin_poly = sin_poly * u + a
                    cos_poly = cos_poly * u + b
                small = sin_poly * phi
                double = small * cos_poly
                turned_c = 1.0 - double * double
                turned_s = double * (math.sqrt(2.0) - small * small)
                re, im = column[jh]
                if (j + 1) * LANES > 3 * H // 4:
                    loss = absorb[j : j + 1, :]
                    re, im = re * loss, im * loss
                re, im = re * turned_c - im * turned_s, re * turned_s + im * turned_c
                if j < TERRAIN_ROWS:
                    open_air = lane + j * LANES >= terrain[t]
                    re, im = jnp.where(open_air, re, 0.0), jnp.where(open_air, im, 0.0)
                high, low = split(re * re + im * im)
                energy[j * batch : (j + 1) * batch, :] = jnp.concatenate([high, low], axis=1)
                moved.append((re, im))
            enter(moved, jl, end_re, end_im)
        return carry

    energy[...] = jnp.zeros_like(energy)
    for copy in copies:
        copy.wait()
    lax.fori_loop(0, steps, step, 0)
    binned(steps - 1)

    tiles = totals.shape[0]
    hot = (lax.broadcasted_iota(jnp.int32, (tiles, steps * batch), 0) == cells[...]).astype(F32).astype(BF16)
    value = power[...]
    high = value.astype(BF16)
    rest = value - high.astype(F32)
    middle = rest.astype(BF16)
    low = (rest - middle.astype(F32)).astype(BF16)
    gain = jnp.dot(hot, high, preferred_element_type=F32)
    gain += jnp.dot(hot, middle, preferred_element_type=F32)
    gain += jnp.dot(hot, low, preferred_element_type=F32)
    if first:
        totals[...] = gain
    else:
        totals[...] = totals_in[...] + gain


def march(section, slabs, terrain, cells, start, totals, consts, tiles, first):
    steps, batch, heights = slabs[0].shape[-3:]
    sections = H // heights
    state = jax.ShapeDtypeStruct((ROWS, batch, LANES), F32)
    vmem = pl.BlockSpec(memory_space=pltpu.VMEM)
    smem = pl.BlockSpec(memory_space=pltpu.SMEM)
    anywhere = pl.BlockSpec(memory_space=pl.ANY)
    call = pl.pallas_call(
        functools.partial(march_kernel, steps, batch, heights, first, len(slabs)),
        out_shape=(state, state, jax.ShapeDtypeStruct((tiles, BINS), F32)),
        in_specs=[smem] + [anywhere] * len(slabs) + [vmem] * 12,
        out_specs=(vmem, vmem, vmem),
        scratch_shapes=[
            pltpu.VMEM((sections, steps, batch, heights), BF16),
            pltpu.SemaphoreType.DMA((len(slabs),)),
            pltpu.VMEM((ROWS, batch, LANES), F32),
            pltpu.VMEM((ROWS, batch, LANES), F32),
            pltpu.VMEM((ROWS * batch, 2 * LANES), BF16),
            pltpu.VMEM((steps * batch, BINS), F32),
        ],
        compiler_params=pltpu.CompilerParams(vmem_limit_bytes=48 * 1024 * 1024),
        cost_estimate=pl.CostEstimate(
            flops=steps * 1_600_000_000, bytes_accessed=4 * 1024 * 1024, transcendentals=0
        ),
        name="march",
    )
    return call(section, *slabs, terrain, cells, *start, totals, *consts)


def turned(levels, base, rows, begin, end, own, put):
    steps, heights = levels.shape[1:]
    columns = [slice(c * LANES, (c + 1) * LANES) for c in range(heights // LANES)]
    for b in range(own):
        for c, column in enumerate(columns):
            rows[c, b * steps : (b + 1) * steps, :] = levels[base + b, :, column].astype(F32)
    for t in range(begin, end):
        for c, column in enumerate(columns):
            put(t - begin, column, rows[c, pl.ds(t, own, stride=steps), :].astype(BF16))


def filled(taken, batch):
    if taken.shape[0] < batch:
        return jnp.pad(taken, ((0, batch - taken.shape[0]), (0, 0)))
    return taken


def deal_kernel(begin, end, levels, out, rows):
    def put(t, column, taken):
        out[0, t, :, column] = filled(taken, out.shape[2])

    turned(levels, 0, rows, begin, end, levels.shape[0], put)


def deal(levels, begin, end, sections, own, batch):
    steps, heights = levels.shape[1:]
    return pl.pallas_call(
        functools.partial(deal_kernel, begin, end),
        grid=(sections,),
        out_shape=jax.ShapeDtypeStruct((sections, end - begin, batch, heights), BF16),
        in_specs=[pl.BlockSpec((own, steps, heights), lambda d: (d, 0, 0))],
        out_specs=pl.BlockSpec((1, end - begin, batch, heights), lambda d: (d, 0, 0, 0)),
        scratch_shapes=[pltpu.VMEM((heights // LANES, own * steps, LANES), F32)],
        compiler_params=pltpu.CompilerParams(vmem_limit_bytes=32 * 1024 * 1024),
        cost_estimate=pl.CostEstimate(flops=1_000_000_000, bytes_accessed=4 * 1024 * 1024, transcendentals=0),
        name="deal",
    )(levels)


def cut_kernel(begin, end, own, section, levels, *refs):
    slabs, rows = refs[:-1], refs[-1]
    for d, slab in enumerate(slabs):
        def put(t, column, taken, slab=slab):
            slab[t, :, column] = filled(taken, slab.shape[1])

        turned(levels, (section[0] ^ d) * own, rows, begin, end, own, put)


def cut(section, levels, begin, end, sections, own, batch):
    steps, heights = levels.shape[1:]
    slab = jax.ShapeDtypeStruct((end - begin, batch, heights), BF16)
    vmem = pl.BlockSpec(memory_space=pltpu.VMEM)
    smem = pl.BlockSpec(memory_space=pltpu.SMEM)
    call = pl.pallas_call(
        functools.partial(cut_kernel, begin, end, own),
        out_shape=(slab,) * sections,
        in_specs=[smem, vmem],
        out_specs=(vmem,) * sections,
        scratch_shapes=[pltpu.VMEM((heights // LANES, own * steps, LANES), F32)],
        compiler_params=pltpu.CompilerParams(vmem_limit_bytes=32 * 1024 * 1024),
        cost_estimate=pl.CostEstimate(flops=1_000_000_000, bytes_accessed=4 * 1024 * 1024, transcendentals=0),
        name="cut",
    )
    return call(section, levels)


def gather_small(value):
    radial, sections = lax.axis_index("radial"), lax.axis_size("range")
    other = lax.ppermute(value, "radial", [(0, 1), (1, 0)])
    pair = jnp.stack([jnp.where(radial == 0, value, other), jnp.where(radial == 0, other, value)])
    section = lax.axis_index("range")
    held = jnp.zeros((sections, *pair.shape), pair.dtype)
    held = lax.dynamic_update_index_in_dim(held, pair, section, 0)
    width = 1
    while width < sections:
        base = section // width * width
        part = lax.dynamic_slice_in_dim(held, base, width, 0)
        part = lax.ppermute(part, "range", [(i, i ^ width) for i in range(sections)])
        held = lax.dynamic_update_slice_in_dim(held, part, base ^ width, 0)
        width *= 2
    return held


def local(refractivity, source, terrain, tile_map):
    sections = lax.axis_size("range")
    owners = sections * lax.axis_size("radial")
    tiles = TILE_DEV * owners
    radials, steps, heights = refractivity.shape
    own = radials // sections
    batch = -(-own // 16) * 16

    small = jnp.concatenate([terrain.T, tile_map.T])
    middle = round(WHOLE_SHARE * steps)
    section = lax.axis_index("range").astype(jnp.int32).reshape(1)
    dealt = deal(refractivity, 0, middle, sections, own, batch)
    refractivity, dealt = lax.optimization_barrier((refractivity, dealt))
    whole = lax.all_to_all(dealt, "range", 0, 0, tiled=True)
    slabs = list(cut(section, refractivity, middle, steps, sections, own, batch))
    small, slabs[0] = lax.optimization_barrier((small, slabs[0]))
    everyone = gather_small(small)
    for d in reversed(range(1, sections)):
        slabs[d] = lax.ppermute(slabs[d], "range", [(i, i ^ d) for i in range(sections)])
    everyone = everyone.reshape(*everyone.shape[:2], 2, -1, radials)
    my_ids = (lax.axis_index("range") * lax.axis_size("radial") + lax.axis_index("radial")) * TILE_DEV
    my_ids = my_ids + jnp.arange(TILE_DEV, dtype=jnp.int32)
    counts = jnp.sum(
        (my_ids[:, None] == everyone[:, :, 1].reshape(1, -1)).astype(F32), axis=1
    )
    mine = lax.dynamic_index_in_dim(everyone, lax.axis_index("radial"), 1, keepdims=False)
    mine = lax.dynamic_slice_in_dim(mine, lax.axis_index("range") * own, own, 3)
    mine = jnp.transpose(mine, (1, 0, 2, 3)).reshape(2, steps, own)
    pad = ((0, 0), (0, batch - own))
    terrain_all = jnp.pad(mine[0], pad)
    cells_all = jnp.pad(mine[1], pad, constant_values=-1)
    terrain_all = jnp.broadcast_to(terrain_all[:, :, None], (steps, batch, LANES))

    consts = [jnp.asarray(v) for v in tables()]
    start = (source[0].reshape(ROWS, LANES), source[1].reshape(ROWS, LANES))
    totals = jnp.zeros((tiles, BINS), F32)
    for piece, begin, end in (([whole], 0, middle), (slabs, middle, steps)):
        *start, totals = march(
            section, piece, terrain_all[begin:end], cells_all[begin:end].reshape(1, -1),
            start, totals, consts, tiles, begin == 0,
        )
    sent = lax.all_to_all(
        totals.reshape(owners, TILE_DEV, BINS), ("range", "radial"), 0, 0, tiled=True
    )
    return jnp.sum(sent, axis=0) / counts[:, None]


def solution(mesh):
    in_specs = (
        P(("region", "radial"), None, "range"),
        P(None, "region"),
        P(("region", "radial"), "range"),
        P(("region", "radial"), "range"),
    )
    out_specs = P(("region", "range", "radial"), None)
    return jax.shard_map(local, mesh=mesh, in_specs=in_specs, out_specs=out_specs, check_vma=False)
```

```python
import functools
import math

import jax
import jax.numpy as jnp
import ml_dtypes
import numpy as np
from jax import lax
from jax.experimental import pallas as pl
from jax.experimental.pallas import tpu as pltpu
from jax.sharding import PartitionSpec as P

H = 4096
BIN = 32
LANES = 128
ROWS = H // LANES
FOUR = 4
EIGHT = 8
BINS = H // BIN
TILE_DEV = 16
TILT_SLOPE = 2.0
SPREAD_RATE = 0.5
ABSORB_RATE = 0.05
TERRAIN_ROWS = 4
WHOLE_SHARE = 0.6875
GROUP = 2
DIGIT = 32
DIGIT_ROWS = 8

F32 = jnp.float32
BF16 = jnp.bfloat16


def split_np(table):
    high = table.astype(np.float32).astype(ml_dtypes.bfloat16)
    low = (table - high.astype(np.float64)).astype(ml_dtypes.bfloat16)
    return high, low


def tables():
    n = np.arange(LANES)
    angle = -2.0 * np.pi / LANES * (n[:, None] * n[None, :] % LANES)
    c, s = np.cos(angle), np.sin(angle)
    forward = np.block([[c, s], [-s, c]])
    inverse = np.block([[c, -s], [s, c]])
    weights = []
    for matrix in (forward, inverse):
        high, low = split_np(matrix)
        weights.append(np.concatenate([high, high, low], axis=0))
    q = np.arange(ROWS)
    angle = -2.0 * np.pi / H * (q[:, None] * n[None, :])
    twiddle = np.stack([np.cos(angle), np.sin(angle)]).astype(np.float32)
    frequency = q[:, None] + ROWS * n[None, :]
    signed = np.where(frequency >= H // 2, frequency - H, frequency)
    turning = -SPREAD_RATE * (2.0 * np.pi / H * signed) ** 2
    spread = (np.stack([np.cos(turning), np.sin(turning)]) / H).astype(np.float32)
    rel = np.arange(H).reshape(ROWS, LANES) / H
    tilt = (TILT_SLOPE * rel - 1.0).astype(np.float32)
    depth = np.maximum(rel - 0.75, 0.0) * 4.0
    absorb = np.exp(-ABSORB_RATE * depth * depth).astype(np.float32)
    bins = np.zeros((2 * LANES, BINS), np.float64)
    for lane in range(2 * LANES):
        bins[lane, (lane % LANES) // BIN :: LANES // BIN] = 1.0 / BIN
    return weights[0], weights[1], twiddle, spread, tilt, absorb, bins.astype(ml_dtypes.bfloat16)


def phase_polynomials():
    root = 2.0 ** 0.25
    sin_scale = root * math.sqrt(2.0)
    cos_scale = 2.0 * math.sqrt(2.0) / sin_scale
    limit = 7.001
    nodes = 0.5 * limit * limit * (1.0 + np.cos(np.pi * (np.arange(64) + 0.5) / 64))
    phi = np.sqrt(nodes)
    sine = np.polynomial.chebyshev.Chebyshev.fit(
        nodes, sin_scale * np.sin(phi / 4) / phi, 4, domain=[0, limit * limit]
    ).convert(kind=np.polynomial.Polynomial)
    cosine = np.polynomial.chebyshev.Chebyshev.fit(
        nodes, cos_scale * np.cos(phi / 4), 4, domain=[0, limit * limit]
    ).convert(kind=np.polynomial.Polynomial)
    return [float(v) for v in sine.coef], [float(v) for v in cosine.coef]


def unit(number, extent):
    angle = -2.0 * math.pi * (number % extent) / extent
    return math.cos(angle), math.sin(angle)


def cmul_const(value, factor):
    re, im = value
    c, s = factor
    if abs(s) < 1e-12 and c > 0:
        return value
    if abs(c) < 1e-12:
        return (im, -re) if s < 0 else (-im, re)
    return re * c - im * s, re * s + im * c


def add(a, b):
    return a[0] + b[0], a[1] + b[1]


def sub(a, b):
    return a[0] - b[0], a[1] - b[1]


def turn(a, sign):
    return (a[1], -a[0]) if sign < 0 else (-a[1], a[0])


def dft4(x, sign):
    a, b = add(x[0], x[2]), sub(x[0], x[2])
    c, d = add(x[1], x[3]), turn(sub(x[1], x[3]), sign)
    return [add(a, c), add(b, d), sub(a, c), sub(b, d)]


def eighth(a, sign):
    h = math.sqrt(0.5)
    re, im = a
    if sign < 0:
        return (re + im) * h, (im - re) * h
    return (re - im) * h, (re + im) * h


def dft8(x, sign):
    even = dft4(x[0::2], sign)
    odd = dft4(x[1::2], sign)
    odd = [odd[0], eighth(odd[1], sign), turn(odd[2], sign), turn(eighth(odd[3], sign), sign)]
    return [add(even[i], odd[i]) for i in range(4)] + [sub(even[i], odd[i]) for i in range(4)]


def split(value):
    high = value.astype(BF16)
    low = (value - high.astype(F32)).astype(BF16)
    return high, low


def march_kernel(begin, steps, batch, own, first, last, count, section, *refs):
    slabs, refs = refs[:count], refs[count:]
    (start_re, start_im, named, totals_in, w_forward, w_inverse, twiddle, spread, tilt, absorb, bins), refs = (
        refs[:11], refs[11:]
    )
    (totals, end_re, end_im, cells), refs = (refs[:4], refs[4:]) if first else ((*refs[:3], named), refs[3:])
    levels, arrived, back_re, back_im, energy, power = refs
    sine, cosine = phase_polynomials()
    heights = levels.shape[2]
    copies = [(slab, levels if first else levels.at[section[0] ^ d]) for d, slab in enumerate(slabs)]
    if not first:
        copies += [(start_re, end_re), (start_im, end_im)]
    copies = [pltpu.make_async_copy(*pair, arrived.at[i]) for i, pair in enumerate(copies)]
    for copy in copies:
        copy.start()
    lane = lax.broadcasted_iota(jnp.int32, (batch, LANES), 1)
    radial = lax.broadcasted_iota(jnp.int32, (batch, LANES), 0)
    my_lane = lane == section[0] * own + radial
    at_once = cells.shape[1] // 2

    def enter(columns, jl, put_re, put_im):
        parts = dft4(columns, -1)
        for ql in range(FOUR):
            re, im = cmul_const(parts[ql], unit(ql * jl, ROWS))
            put_re[ql * EIGHT + jl] = re
            put_im[ql * EIGHT + jl] = im

    if first:
        for jl in range(EIGHT):
            columns = []
            for jh in range(FOUR):
                j = EIGHT * jh + jl
                shape = (batch, LANES)
                columns.append((
                    jnp.broadcast_to(start_re[j : j + 1, :], shape),
                    jnp.broadcast_to(start_im[j : j + 1, :], shape),
                ))
            enter(columns, jl, end_re, end_im)

    def joined(pieces):
        re_high, re_low = split(jnp.concatenate([p[0] for p in pieces], axis=0))
        im_high, im_low = split(jnp.concatenate([p[1] for p in pieces], axis=0))
        return jnp.concatenate([re_high, im_high, re_low, im_low, re_high, im_high], axis=1)

    def parted(product, count):
        return [
            (product[i * batch : (i + 1) * batch, :LANES], product[i * batch : (i + 1) * batch, LANES:])
            for i in range(count)
        ]

    def binned(t):
        summed = jnp.dot(energy[...], bins[...], preferred_element_type=F32)
        row = summed[:batch]
        for j in range(1, ROWS):
            row = jnp.where(lane // (LANES // BIN) == j, summed[j * batch : (j + 1) * batch], row)
        power[pl.ds(pl.multiple_of(t * batch, batch), batch), :] = row

    def step(t, carry):
        groups = [list(range(base, base + GROUP)) for base in range(0, FOUR, GROUP)]
        rows = [[ql + FOUR * qh for ql in group for qh in range(EIGHT)] for group in groups]
        products = []
        for group in groups:
            pieces = []
            for ql in group:
                column = [(end_re[ql * EIGHT + jl], end_im[ql * EIGHT + jl]) for jl in range(EIGHT)]
                for qh, (re, im) in enumerate(dft8(column, -1)):
                    q = ql + FOUR * qh
                    c, s = twiddle[0, q : q + 1, :], twiddle[1, q : q + 1, :]
                    pieces.append((re * c - im * s, re * s + im * c))
            products.append(jnp.dot(joined(pieces), w_forward[...], preferred_element_type=F32))
        binned(jnp.maximum(t - 1, 0))
        for i, qs in enumerate(rows):
            pieces = []
            for q, (re, im) in zip(qs, parted(products[i], len(qs))):
                c, s = spread[0, q : q + 1, :], spread[1, q : q + 1, :]
                pieces.append((re * c - im * s, re * s + im * c))
            products[i] = jnp.dot(joined(pieces), w_inverse[...], preferred_element_type=F32)
        for i, qs in enumerate(rows):
            pieces = []
            for q, (re, im) in zip(qs, parted(products[i], len(qs))):
                c, s = twiddle[0, q : q + 1, :], twiddle[1, q : q + 1, :]
                pieces.append((re * c + im * s, im * c - re * s))
            for k, ql in enumerate(groups[i]):
                column = dft8(pieces[k * EIGHT : (k + 1) * EIGHT], 1)
                for jl in range(EIGHT):
                    back_re[ql * EIGHT + jl] = column[jl][0]
                    back_im[ql * EIGHT + jl] = column[jl][1]

        row = cells[(begin + t) // at_once, pl.ds((begin + t) % at_once, 1), :]
        ground = jnp.sum(jnp.where(my_lane, row, 0), axis=1, keepdims=True)
        for jl in range(EIGHT):
            column = []
            for ql in range(FOUR):
                c, s = unit(ql * jl, ROWS)
                column.append(cmul_const((back_re[ql * EIGHT + jl], back_im[ql * EIGHT + jl]), (c, -s)))
            column = dft4(column, 1)
            moved = []
            for jh in range(FOUR):
                j = EIGHT * jh + jl
                place = j * LANES
                raw = levels[
                    place // heights, pl.ds(pl.multiple_of(t * batch, batch), batch),
                    place % heights : place % heights + LANES,
                ]
                phi = raw.astype(F32) + tilt[j : j + 1, :]
                u = phi * phi
                sin_poly, cos_poly = sine[-1], cosine[-1]
                for a, b in zip(sine[-2::-1], cosine[-2::-1]):
                    sin_poly = sin_poly * u + a
                    cos_poly = cos_poly * u + b
                small = sin_poly * phi
                double = small * cos_poly
                turned_c = 1.0 - double * double
                turned_s = double * (math.sqrt(2.0) - small * small)
                re, im = column[jh]
                if (j + 1) * LANES > 3 * H // 4:
                    loss = absorb[j : j + 1, :]
                    re, im = re * loss, im * loss
                re, im = re * turned_c - im * turned_s, re * turned_s + im * turned_c
                if j < TERRAIN_ROWS:
                    open_air = lane + j * LANES >= ground
                    re, im = jnp.where(open_air, re, 0.0), jnp.where(open_air, im, 0.0)
                high, low = split(re * re + im * im)
                energy[j * batch : (j + 1) * batch, :] = jnp.concatenate([high, low], axis=1)
                moved.append((re, im))
            enter(moved, jl, end_re, end_im)
        return carry

    energy[...] = jnp.zeros_like(energy)
    power[...] = jnp.zeros_like(power)
    for copy in copies:
        copy.wait()
    if first:
        for source in range(cells.shape[0]):
            rows = levels[source, steps * batch :, :LANES].astype(F32).astype(jnp.int32)
            half = DIGIT_ROWS // 2
            cells[source] = rows[:half] * DIGIT + rows[half:]
    lax.fori_loop(0, steps, step, 0)
    binned(steps - 1)

    lane = lax.broadcasted_iota(jnp.int32, (1, LANES), 1)
    fit = LANES // batch
    tile_rows = []
    for t in range(steps):
        row = cells[(begin + t) // at_once, at_once + (begin + t) % at_once, :].reshape(1, LANES)
        row = pltpu.roll(row, lax.rem(batch * (t % fit) - section[0] * own + LANES, LANES), 1)
        row = jnp.where(lane % batch < own, row, -1)
        if t % fit == 0:
            tile_rows.append(jnp.where(lane < batch, row, -1))
        else:
            tile_rows[-1] = jnp.where(lane // batch == t % fit, row, tile_rows[-1])
    tile_row = jnp.concatenate(tile_rows, axis=1)
    tiles, cell_count = totals.shape[0], tile_row.shape[1]
    hot = (lax.broadcasted_iota(jnp.int32, (tiles, cell_count), 0) == tile_row).astype(F32).astype(BF16)
    value = power[...]
    high = value.astype(BF16)
    rest = value - high.astype(F32)
    middle = rest.astype(BF16)
    low = (rest - middle.astype(F32)).astype(BF16)
    gain = jnp.dot(hot, high, preferred_element_type=F32)
    gain += jnp.dot(hot, middle, preferred_element_type=F32)
    gain += jnp.dot(hot, low, preferred_element_type=F32)
    if first:
        totals[...] = gain
    else:
        totals[...] = totals_in[...] + gain


def march(section, slabs, begin, steps, batch, own, start, named, totals, consts, first, last):
    heights = slabs[0].shape[-1]
    sections = H // heights
    field = jax.ShapeDtypeStruct((ROWS, batch, LANES), F32)
    held = pltpu.VMEM(field.shape, F32)
    vmem = pl.BlockSpec(memory_space=pltpu.VMEM)
    smem = pl.BlockSpec(memory_space=pltpu.SMEM)
    anywhere = pl.BlockSpec(memory_space=pl.ANY)
    outputs = [jax.ShapeDtypeStruct(totals.shape, F32)]
    if not last:
        outputs += [field, field]
    if first:
        outputs += [jax.ShapeDtypeStruct(named.shape, jnp.int32)]
    call = pl.pallas_call(
        functools.partial(march_kernel, begin, steps, batch, own, first, last, len(slabs)),
        out_shape=outputs,
        in_specs=[smem] + [anywhere] * len(slabs) + [vmem if first else anywhere] * 2 + [vmem] * 9,
        out_specs=[vmem] * len(outputs),
        scratch_shapes=([held, held] if last else []) + [
            pltpu.VMEM((sections, *slabs[0].shape[-2:]), BF16),
            pltpu.SemaphoreType.DMA((len(slabs) + 2,)),
            held,
            held,
            pltpu.VMEM((ROWS * batch, 2 * LANES), BF16),
            pltpu.VMEM((-(-steps * batch // LANES) * LANES, BINS), F32),
        ],
        compiler_params=pltpu.CompilerParams(vmem_limit_bytes=20 * 1024 * 1024),
        cost_estimate=pl.CostEstimate(
            flops=steps * 1_600_000_000, bytes_accessed=4 * 1024 * 1024, transcendentals=0
        ),
        name="march",
    )
    return call(section, *slabs, *start, named, totals, *consts)


def turned(levels, base, rows, begin, end, own, put):
    steps, heights = levels.shape[1:]
    columns = [slice(c * LANES, (c + 1) * LANES) for c in range(heights // LANES)]
    for b in range(own):
        for c, column in enumerate(columns):
            rows[c, b * steps : (b + 1) * steps, :] = levels[base + b, :, column].astype(F32)
    for t in range(begin, end):
        for c, column in enumerate(columns):
            put(t - begin, column, rows[c, pl.ds(t, own, stride=steps), :].astype(BF16))


def filled(taken, batch):
    if taken.shape[0] < batch:
        return jnp.pad(taken, ((0, batch - taken.shape[0]), (0, 0)))
    return taken


def deal_kernel(begin, end, own, steps, batch, levels, digits, out):
    count = (end - begin) * batch
    row = lax.broadcasted_iota(jnp.int32, (count, own * steps), 0)
    column = lax.broadcasted_iota(jnp.int32, (count, own * steps), 1)
    wanted = (row % batch) * steps + row // batch + begin
    chosen = jnp.logical_and(column == wanted, row % batch < own)
    moved = jnp.dot(
        chosen.astype(F32).astype(BF16),
        levels[...].reshape(own * steps, levels.shape[2]),
        preferred_element_type=F32,
    )
    out[0, :count, :] = moved.astype(BF16)
    out[0, count:, :] = jnp.zeros((DIGIT_ROWS, levels.shape[2]), BF16)
    out[0, count:, : digits.shape[1]] = digits[...]


def deal(levels, digits, begin, end, sections, own, batch):
    steps, heights = levels.shape[1:]
    count = (end - begin) * batch + DIGIT_ROWS
    return pl.pallas_call(
        functools.partial(deal_kernel, begin, end, own, steps, batch),
        grid=(sections,),
        out_shape=jax.ShapeDtypeStruct((sections, count, heights), BF16),
        in_specs=[
            pl.BlockSpec((own, steps, heights), lambda d: (d, 0, 0)),
            pl.BlockSpec(digits.shape, lambda d: (0, 0)),
        ],
        out_specs=pl.BlockSpec((1, count, heights), lambda d: (d, 0, 0)),
        compiler_params=pltpu.CompilerParams(vmem_limit_bytes=60 * 1024 * 1024),
        cost_estimate=pl.CostEstimate(flops=1_000_000_000, bytes_accessed=4 * 1024 * 1024, transcendentals=0),
        name="deal",
    )(levels, digits)


def cut_kernel(begin, end, own, batch, section, levels, *refs):
    slabs, rows = refs[:-1], refs[-1]
    for d, slab in enumerate(slabs):
        def put(t, column, taken, slab=slab):
            slab[t * batch : (t + 1) * batch, column] = filled(taken, batch)

        turned(levels, (section[0] ^ d) * own, rows, begin, end, own, put)


def cut(section, levels, begin, end, sections, own, batch):
    steps, heights = levels.shape[1:]
    slab = jax.ShapeDtypeStruct(((end - begin) * batch, heights), BF16)
    vmem = pl.BlockSpec(memory_space=pltpu.VMEM)
    smem = pl.BlockSpec(memory_space=pltpu.SMEM)
    call = pl.pallas_call(
        functools.partial(cut_kernel, begin, end, own, batch),
        out_shape=(slab,) * sections,
        in_specs=[smem, vmem],
        out_specs=(vmem,) * sections,
        scratch_shapes=[pltpu.VMEM((heights // LANES, own * steps, LANES), F32)],
        compiler_params=pltpu.CompilerParams(vmem_limit_bytes=60 * 1024 * 1024),
        cost_estimate=pl.CostEstimate(flops=1_000_000_000, bytes_accessed=4 * 1024 * 1024, transcendentals=0),
        name="cut",
    )
    return call(section, levels)


def local(refractivity, source, terrain, tile_map):
    sections = lax.axis_size("range")
    owners = sections * lax.axis_size("radial")
    tiles = TILE_DEV * owners
    radials, steps, heights = refractivity.shape
    own = radials // sections
    batch = -(-own // 16) * 16

    small = jnp.concatenate([terrain.T, tile_map.T])
    digits = jnp.concatenate([small // DIGIT, small % DIGIT]).astype(BF16)
    middle = round(WHOLE_SHARE * steps)
    section = lax.axis_index("range").astype(jnp.int32).reshape(1)
    dealt = deal(refractivity, digits, 0, middle, sections, own, batch)
    refractivity, dealt = lax.optimization_barrier((refractivity, dealt))
    whole = lax.all_to_all(dealt, "range", 0, 0, tiled=True)
    slabs = list(cut(section, refractivity, middle, steps, sections, own, batch))
    for d in range(1, sections):
        slabs[d] = lax.ppermute(slabs[d], "range", [(i, i ^ d) for i in range(sections)])

    consts = [jnp.asarray(v) for v in tables()]
    start = (source[0].reshape(ROWS, LANES), source[1].reshape(ROWS, LANES))
    totals = jnp.zeros((tiles, BINS), F32)
    named = jnp.zeros((sections, DIGIT_ROWS // 2, radials), jnp.int32)
    totals, *start, named = march(
        section, [whole], 0, middle, batch, own, start, named, totals, consts, True, False
    )
    (totals,) = march(
        section, slabs, middle, steps - middle, batch, own, start, named, totals, consts, False, True
    )

    named, totals = lax.optimization_barrier((named, totals))
    sent = lax.all_to_all(
        totals.reshape(owners, TILE_DEV, BINS), ("range", "radial"), 0, 0, tiled=True
    )
    pair = lax.axis_index("range") * lax.axis_size("radial")
    radial = lax.axis_index("radial")
    tile_ids = named[:, DIGIT_ROWS // 4 :].reshape(1, -1)

    def count_of(core):
        ids = (pair + core) * TILE_DEV + jnp.arange(TILE_DEV, dtype=jnp.int32)
        return jnp.sum((ids[:, None] == tile_ids).astype(F32), axis=1)

    counts = count_of(radial) + lax.ppermute(count_of(1 - radial), "radial", [(0, 1), (1, 0)])
    return jnp.sum(sent, axis=0) / counts[:, None]


def solution(mesh):
    in_specs = (
        P(("region", "radial"), None, "range"),
        P(None, "region"),
        P(("region", "radial"), "range"),
        P(("region", "radial"), "range"),
    )
    out_specs = P(("region", "range", "radial"), None)
    return jax.shard_map(local, mesh=mesh, in_specs=in_specs, out_specs=out_specs, check_vma=False)
```

```python
import functools
import math

import jax
import jax.numpy as jnp
import ml_dtypes
import numpy as np
from jax import lax
from jax.experimental import pallas as pl
from jax.experimental.pallas import tpu as pltpu
from jax.sharding import PartitionSpec as P

H = 4096
BIN = 32
LANES = 128
ROWS = H // LANES
FOUR = 4
EIGHT = 8
BINS = H // BIN
TILE_DEV = 16
TILT_SLOPE = 2.0
SPREAD_RATE = 0.5
ABSORB_RATE = 0.05
TERRAIN_ROWS = 4
EARLY_SHARE = 0.6875
GROUP = 2
DIGIT = 32
DIGIT_ROWS = 8

F32 = jnp.float32
BF16 = jnp.bfloat16


def split_np(table):
    high = table.astype(np.float32).astype(ml_dtypes.bfloat16)
    low = (table - high.astype(np.float64)).astype(ml_dtypes.bfloat16)
    return high, low


def tables():
    n = np.arange(LANES)
    angle = -2.0 * np.pi / LANES * (n[:, None] * n[None, :] % LANES)
    c, s = np.cos(angle), np.sin(angle)
    forward = np.block([[c, s], [-s, c]])
    inverse = np.block([[c, -s], [s, c]])
    weights = []
    for matrix in (forward, inverse):
        high, low = split_np(matrix)
        weights.append(np.concatenate([high, high, low], axis=0))
    q = np.arange(ROWS)
    angle = -2.0 * np.pi / H * (q[:, None] * n[None, :])
    twiddle = np.stack([np.cos(angle), np.sin(angle)]).astype(np.float32)
    frequency = q[:, None] + ROWS * n[None, :]
    signed = np.where(frequency >= H // 2, frequency - H, frequency)
    turning = -SPREAD_RATE * (2.0 * np.pi / H * signed) ** 2
    spread = (np.stack([np.cos(turning), np.sin(turning)]) / H).astype(np.float32)
    rel = np.arange(H).reshape(ROWS, LANES) / H
    tilt = (TILT_SLOPE * rel - 1.0).astype(np.float32)
    depth = np.maximum(rel - 0.75, 0.0) * 4.0
    absorb = np.exp(-ABSORB_RATE * depth * depth).astype(np.float32)
    bins = np.zeros((2 * LANES, BINS), np.float64)
    for lane in range(2 * LANES):
        bins[lane, (lane % LANES) // BIN :: LANES // BIN] = 1.0 / BIN
    return weights[0], weights[1], twiddle, spread, tilt, absorb, bins.astype(ml_dtypes.bfloat16)


def phase_polynomials():
    root = 2.0 ** 0.25
    sin_scale = root * math.sqrt(2.0)
    cos_scale = 2.0 * math.sqrt(2.0) / sin_scale
    limit = 7.001
    nodes = 0.5 * limit * limit * (1.0 + np.cos(np.pi * (np.arange(64) + 0.5) / 64))
    phi = np.sqrt(nodes)
    sine = np.polynomial.chebyshev.Chebyshev.fit(
        nodes, sin_scale * np.sin(phi / 4) / phi, 4, domain=[0, limit * limit]
    ).convert(kind=np.polynomial.Polynomial)
    cosine = np.polynomial.chebyshev.Chebyshev.fit(
        nodes, cos_scale * np.cos(phi / 4), 4, domain=[0, limit * limit]
    ).convert(kind=np.polynomial.Polynomial)
    return [float(v) for v in sine.coef], [float(v) for v in cosine.coef]


def unit(number, extent):
    angle = -2.0 * math.pi * (number % extent) / extent
    return math.cos(angle), math.sin(angle)


def cmul_const(value, factor):
    re, im = value
    c, s = factor
    if abs(s) < 1e-12 and c > 0:
        return value
    if abs(c) < 1e-12:
        return (im, -re) if s < 0 else (-im, re)
    return re * c - im * s, re * s + im * c


def add(a, b):
    return a[0] + b[0], a[1] + b[1]


def sub(a, b):
    return a[0] - b[0], a[1] - b[1]


def turn(a, sign):
    return (a[1], -a[0]) if sign < 0 else (-a[1], a[0])


def dft4(x, sign):
    a, b = add(x[0], x[2]), sub(x[0], x[2])
    c, d = add(x[1], x[3]), turn(sub(x[1], x[3]), sign)
    return [add(a, c), add(b, d), sub(a, c), sub(b, d)]


def eighth(a, sign):
    h = math.sqrt(0.5)
    re, im = a
    if sign < 0:
        return (re + im) * h, (im - re) * h
    return (re - im) * h, (re + im) * h


def dft8(x, sign):
    even = dft4(x[0::2], sign)
    odd = dft4(x[1::2], sign)
    odd = [odd[0], eighth(odd[1], sign), turn(odd[2], sign), turn(eighth(odd[3], sign), sign)]
    return [add(even[i], odd[i]) for i in range(4)] + [sub(even[i], odd[i]) for i in range(4)]


def split(value):
    high = value.astype(BF16)
    low = (value - high.astype(F32)).astype(BF16)
    return high, low


def march_kernel(begin, steps, batch, own, first, last, count, section, *refs):
    slabs, refs = refs[:count], refs[count:]
    (start_re, start_im, named, totals_in, w_forward, w_inverse, twiddle, spread, tilt, absorb, bins), refs = (
        refs[:11], refs[11:]
    )
    (totals, end_re, end_im, cells), refs = (refs[:4], refs[4:]) if first else ((*refs[:3], named), refs[3:])
    levels, arrived, back_re, back_im, energy, power = refs
    sine, cosine = phase_polynomials()
    heights = levels.shape[2]
    half = levels.shape[0] // 2
    if first:
        places = [levels.at[pl.ds(section[0] // half * half, half)]]
        places += [levels.at[section[0] ^ d] for d in range(half, 2 * half)]
    else:
        places = [levels]
    copies = list(zip(slabs, places))
    copies = [pltpu.make_async_copy(*pair, arrived.at[i]) for i, pair in enumerate(copies)]
    for copy in copies:
        copy.start()
    lane = lax.broadcasted_iota(jnp.int32, (batch, LANES), 1)
    radial = lax.broadcasted_iota(jnp.int32, (batch, LANES), 0)
    my_lane = lane == section[0] * own + radial
    at_once = cells.shape[1] // 2

    def enter(columns, jl, put_re, put_im):
        parts = dft4(columns, -1)
        for ql in range(FOUR):
            re, im = cmul_const(parts[ql], unit(ql * jl, ROWS))
            put_re[ql * EIGHT + jl] = re
            put_im[ql * EIGHT + jl] = im

    if first:
        for jl in range(EIGHT):
            columns = []
            for jh in range(FOUR):
                j = EIGHT * jh + jl
                shape = (batch, LANES)
                columns.append((
                    jnp.broadcast_to(start_re[j : j + 1, :], shape),
                    jnp.broadcast_to(start_im[j : j + 1, :], shape),
                ))
            enter(columns, jl, end_re, end_im)
    else:
        end_re[...] = start_re[...]
        end_im[...] = start_im[...]

    def joined(pieces):
        re_high, re_low = split(jnp.concatenate([p[0] for p in pieces], axis=0))
        im_high, im_low = split(jnp.concatenate([p[1] for p in pieces], axis=0))
        return jnp.concatenate([re_high, im_high, re_low, im_low, re_high, im_high], axis=1)

    def parted(product, count):
        return [
            (product[i * batch : (i + 1) * batch, :LANES], product[i * batch : (i + 1) * batch, LANES:])
            for i in range(count)
        ]

    def binned(t):
        summed = jnp.dot(energy[...], bins[...], preferred_element_type=F32)
        row = summed[:batch]
        for j in range(1, ROWS):
            row = jnp.where(lane // (LANES // BIN) == j, summed[j * batch : (j + 1) * batch], row)
        power[pl.ds(pl.multiple_of(t * batch, batch), batch), :] = row

    def step(t, carry):
        groups = [list(range(base, base + GROUP)) for base in range(0, FOUR, GROUP)]
        rows = [[ql + FOUR * qh for ql in group for qh in range(EIGHT)] for group in groups]
        products = []
        for group in groups:
            pieces = []
            for ql in group:
                column = [(end_re[ql * EIGHT + jl], end_im[ql * EIGHT + jl]) for jl in range(EIGHT)]
                for qh, (re, im) in enumerate(dft8(column, -1)):
                    q = ql + FOUR * qh
                    c, s = twiddle[0, q : q + 1, :], twiddle[1, q : q + 1, :]
                    pieces.append((re * c - im * s, re * s + im * c))
            products.append(jnp.dot(joined(pieces), w_forward[...], preferred_element_type=F32))
        binned(jnp.maximum(t - 1, 0))
        for i, qs in enumerate(rows):
            pieces = []
            for q, (re, im) in zip(qs, parted(products[i], len(qs))):
                c, s = spread[0, q : q + 1, :], spread[1, q : q + 1, :]
                pieces.append((re * c - im * s, re * s + im * c))
            products[i] = jnp.dot(joined(pieces), w_inverse[...], preferred_element_type=F32)
        for i, qs in enumerate(rows):
            pieces = []
            for q, (re, im) in zip(qs, parted(products[i], len(qs))):
                c, s = twiddle[0, q : q + 1, :], twiddle[1, q : q + 1, :]
                pieces.append((re * c + im * s, im * c - re * s))
            for k, ql in enumerate(groups[i]):
                column = dft8(pieces[k * EIGHT : (k + 1) * EIGHT], 1)
                for jl in range(EIGHT):
                    back_re[ql * EIGHT + jl] = column[jl][0]
                    back_im[ql * EIGHT + jl] = column[jl][1]

        row = cells[(begin + t) // at_once, pl.ds((begin + t) % at_once, 1), :]
        ground = jnp.sum(jnp.where(my_lane, row, 0), axis=1, keepdims=True)
        for jl in range(EIGHT):
            column = []
            for ql in range(FOUR):
                c, s = unit(ql * jl, ROWS)
                column.append(cmul_const((back_re[ql * EIGHT + jl], back_im[ql * EIGHT + jl]), (c, -s)))
            column = dft4(column, 1)
            moved = []
            for jh in range(FOUR):
                j = EIGHT * jh + jl
                place = j * LANES
                raw = levels[
                    place // heights, pl.ds(pl.multiple_of(t * batch, batch), batch),
                    place % heights : place % heights + LANES,
                ]
                phi = raw.astype(F32) + tilt[j : j + 1, :]
                u = phi * phi
                sin_poly, cos_poly = sine[-1], cosine[-1]
                for a, b in zip(sine[-2::-1], cosine[-2::-1]):
                    sin_poly = sin_poly * u + a
                    cos_poly = cos_poly * u + b
                small = sin_poly * phi
                double = small * cos_poly
                turned_c = 1.0 - double * double
                turned_s = double * (math.sqrt(2.0) - small * small)
                re, im = column[jh]
                if (j + 1) * LANES > 3 * H // 4:
                    loss = absorb[j : j + 1, :]
                    re, im = re * loss, im * loss
                re, im = re * turned_c - im * turned_s, re * turned_s + im * turned_c
                if j < TERRAIN_ROWS:
                    open_air = lane + j * LANES >= ground
                    re, im = jnp.where(open_air, re, 0.0), jnp.where(open_air, im, 0.0)
                high, low = split(re * re + im * im)
                energy[j * batch : (j + 1) * batch, :] = jnp.concatenate([high, low], axis=1)
                moved.append((re, im))
            enter(moved, jl, end_re, end_im)
        return carry

    energy[...] = jnp.zeros_like(energy)
    power[...] = jnp.zeros_like(power)
    for copy in copies:
        copy.wait()
    if first:
        for source in range(cells.shape[0]):
            rows = levels[source, steps * batch :, :LANES].astype(F32).astype(jnp.int32)
            half = DIGIT_ROWS // 2
            cells[source] = rows[:half] * DIGIT + rows[half:]
    lax.fori_loop(0, steps, step, 0)
    binned(steps - 1)

    lane = lax.broadcasted_iota(jnp.int32, (1, LANES), 1)
    fit = LANES // batch
    tile_rows = []
    for t in range(steps):
        row = cells[(begin + t) // at_once, at_once + (begin + t) % at_once, :].reshape(1, LANES)
        row = pltpu.roll(row, lax.rem(batch * (t % fit) - section[0] * own + LANES, LANES), 1)
        row = jnp.where(lane % batch < own, row, -1)
        if t % fit == 0:
            tile_rows.append(jnp.where(lane < batch, row, -1))
        else:
            tile_rows[-1] = jnp.where(lane // batch == t % fit, row, tile_rows[-1])
    tile_row = jnp.concatenate(tile_rows, axis=1)
    tiles, cell_count = totals.shape[0], tile_row.shape[1]
    hot = (lax.broadcasted_iota(jnp.int32, (tiles, cell_count), 0) == tile_row).astype(F32).astype(BF16)
    value = power[...]
    high = value.astype(BF16)
    rest = value - high.astype(F32)
    middle = rest.astype(BF16)
    low = (rest - middle.astype(F32)).astype(BF16)
    gain = jnp.dot(hot, high, preferred_element_type=F32)
    gain += jnp.dot(hot, middle, preferred_element_type=F32)
    gain += jnp.dot(hot, low, preferred_element_type=F32)
    if first:
        totals[...] = gain
    else:
        totals[...] = totals_in[...] + gain


def march(section, slabs, begin, steps, batch, own, start, named, totals, consts, first, last):
    heights = slabs[0].shape[-1]
    sections = H // heights
    field = jax.ShapeDtypeStruct((ROWS, batch, LANES), F32)
    held = pltpu.VMEM(field.shape, F32)
    vmem = pl.BlockSpec(memory_space=pltpu.VMEM)
    smem = pl.BlockSpec(memory_space=pltpu.SMEM)
    anywhere = pl.BlockSpec(memory_space=pl.ANY)
    outputs = [jax.ShapeDtypeStruct(totals.shape, F32)]
    if not last:
        outputs += [field, field]
    if first:
        outputs += [jax.ShapeDtypeStruct(named.shape, jnp.int32)]
    call = pl.pallas_call(
        functools.partial(march_kernel, begin, steps, batch, own, first, last, len(slabs)),
        out_shape=outputs,
        in_specs=[smem] + [anywhere] * len(slabs) + [vmem] * 11,
        out_specs=[vmem] * len(outputs),
        scratch_shapes=([held, held] if last else []) + [
            pltpu.VMEM((sections, *slabs[0].shape[-2:]), BF16),
            pltpu.SemaphoreType.DMA((len(slabs),)),
            held,
            held,
            pltpu.VMEM((ROWS * batch, 2 * LANES), BF16),
            pltpu.VMEM((-(-steps * batch // LANES) * LANES, BINS), F32),
        ],
        compiler_params=pltpu.CompilerParams(vmem_limit_bytes=20 * 1024 * 1024),
        cost_estimate=pl.CostEstimate(
            flops=steps * 1_600_000_000, bytes_accessed=4 * 1024 * 1024, transcendentals=0
        ),
        name="march",
    )
    return call(section, *slabs, *start, named, totals, *consts)


def turn_steps(block, rows, begin, end, out):
    own, steps, heights = block.shape
    batch = out.shape[0] // (end - begin)
    for c in range(heights // LANES):
        column = slice(c * LANES, (c + 1) * LANES)
        for b in range(own):
            rows[c, b * steps : (b + 1) * steps, :] = block[b, :, column].astype(F32)
        for t in range(begin, end):
            taken = rows[c, pl.ds(t, own, stride=steps), :].astype(BF16)
            if own < batch:
                taken = jnp.pad(taken, ((0, batch - own), (0, 0)))
            out[(t - begin) * batch : (t - begin + 1) * batch, column] = taken


def fill_slabs(begin, end, own, batch, owners, levels, digits, slabs, blocks, turned, rows, sems):
    count = (end - begin) * batch
    arrive = [
        pltpu.make_async_copy(levels.at[pl.ds(owner * own, own)], blocks.at[i], sems.at[0, i])
        for i, owner in enumerate(owners)
    ]
    leave = [pltpu.make_async_copy(turned.at[i], slab, sems.at[1, i]) for i, slab in enumerate(slabs)]
    for copy in arrive:
        copy.start()
    for i in range(len(slabs)):
        arrive[i].wait()
        turn_steps(blocks.at[i], rows, begin, end, turned.at[i, :count, :])
        if turned.shape[1] > count:
            turned[i, count:, :] = jnp.zeros((DIGIT_ROWS, turned.shape[2]), BF16)
            turned[i, count:, : digits.shape[1]] = digits[...]
        leave[i].start()
    for copy in leave:
        copy.wait()


def slab_scratch(number, own, steps, heights, count):
    return [
        pltpu.VMEM((number, own, steps, heights), BF16),
        pltpu.VMEM((number, count, heights), BF16),
        pltpu.VMEM((heights // LANES, own * steps, LANES), F32),
        pltpu.SemaphoreType.DMA((2, number)),
    ]


def cut(section, levels, digits, begin, end, own, batch, partners, extra):
    steps, heights = levels.shape[1:]
    count = (end - begin) * batch + extra
    vmem = pl.BlockSpec(memory_space=pltpu.VMEM)
    smem = pl.BlockSpec(memory_space=pltpu.SMEM)
    anywhere = pl.BlockSpec(memory_space=pl.ANY)

    def kernel(section, levels, digits, *refs):
        slabs, scratch = refs[: len(partners)], refs[len(partners) :]
        fill_slabs(begin, end, own, batch, [section[0] ^ d for d in partners], levels, digits, slabs, *scratch)

    call = pl.pallas_call(
        kernel,
        out_shape=[jax.ShapeDtypeStruct((count, heights), BF16)] * len(partners),
        in_specs=[smem, anywhere, vmem],
        out_specs=[anywhere] * len(partners),
        scratch_shapes=slab_scratch(len(partners), own, steps, heights, count),
        compiler_params=pltpu.CompilerParams(vmem_limit_bytes=58 * 1024 * 1024),
        cost_estimate=pl.CostEstimate(flops=1_000_000_000, bytes_accessed=4 * 1024 * 1024, transcendentals=0),
        name="cut",
    )
    return call(section, levels, digits)


def deal(section, levels, digits, begin, end, own, batch, group, extra):
    steps, heights = levels.shape[1:]
    count = (end - begin) * batch + extra
    vmem = pl.BlockSpec(memory_space=pltpu.VMEM)
    smem = pl.BlockSpec(memory_space=pltpu.SMEM)
    anywhere = pl.BlockSpec(memory_space=pl.ANY)

    def kernel(section, levels, digits, out, *scratch):
        base = section[0] // group * group
        fill_slabs(begin, end, own, batch, [base + i for i in range(group)], levels, digits,
                   [out.at[i] for i in range(group)], *scratch)

    call = pl.pallas_call(
        kernel,
        out_shape=jax.ShapeDtypeStruct((group, count, heights), BF16),
        in_specs=[smem, anywhere, vmem],
        out_specs=anywhere,
        scratch_shapes=slab_scratch(group, own, steps, heights, count),
        compiler_params=pltpu.CompilerParams(vmem_limit_bytes=58 * 1024 * 1024),
        cost_estimate=pl.CostEstimate(flops=1_000_000_000, bytes_accessed=4 * 1024 * 1024, transcendentals=0),
        name="deal",
    )
    return call(section, levels, digits)


def local(refractivity, source, terrain, tile_map):
    sections = lax.axis_size("range")
    owners = sections * lax.axis_size("radial")
    tiles = TILE_DEV * owners
    radials, steps, heights = refractivity.shape
    own = radials // sections
    batch = -(-own // 16) * 16

    small = jnp.concatenate([terrain.T, tile_map.T])
    digits = jnp.concatenate([small // DIGIT, small % DIGIT]).astype(BF16)
    middle = round(EARLY_SHARE * steps)
    section = lax.axis_index("range").astype(jnp.int32).reshape(1)
    half = sections // 2
    slabs = []
    cuts = cut(section, refractivity, digits, 0, middle, own, batch, range(half, sections), DIGIT_ROWS)
    for d, slab in zip(range(half, sections), cuts):
        slabs.append(lax.ppermute(slab, "range", [(i, i ^ d) for i in range(sections)]))
    refractivity, digits, cuts = lax.optimization_barrier((refractivity, digits, cuts))
    near = deal(section, refractivity, digits, 0, middle, own, batch, half, DIGIT_ROWS)
    groups = [list(range(half)), list(range(half, sections))]
    near = lax.all_to_all(near, "range", 0, 0, axis_index_groups=groups, tiled=True)
    late = deal(section, refractivity, digits, middle, steps, own, batch, sections, 0)
    late, near, slabs[-1] = lax.optimization_barrier((late, near, slabs[-1]))
    late = lax.all_to_all(late, "range", 0, 0, tiled=True)

    consts = [jnp.asarray(v) for v in tables()]
    start = (source[0].reshape(ROWS, LANES), source[1].reshape(ROWS, LANES))
    totals = jnp.zeros((tiles, BINS), F32)
    named = jnp.zeros((sections, DIGIT_ROWS // 2, radials), jnp.int32)
    totals, *start, named = march(
        section, [near] + slabs, 0, middle, batch, own, start, named, totals, consts, True, False
    )
    (totals,) = march(
        section, [late], middle, steps - middle, batch, own, start, named, totals, consts, False, True
    )

    named, totals = lax.optimization_barrier((named, totals))
    sent = lax.all_to_all(
        totals.reshape(owners, TILE_DEV, BINS), ("range", "radial"), 0, 0, tiled=True
    )
    pair = lax.axis_index("range") * lax.axis_size("radial")
    radial = lax.axis_index("radial")
    tile_ids = named[:, DIGIT_ROWS // 4 :].reshape(1, -1)

    def count_of(core):
        ids = (pair + core) * TILE_DEV + jnp.arange(TILE_DEV, dtype=jnp.int32)
        return jnp.sum((ids[:, None] == tile_ids).astype(F32), axis=1)

    counts = count_of(radial) + lax.ppermute(count_of(1 - radial), "radial", [(0, 1), (1, 0)])
    return jnp.sum(sent, axis=0) / counts[:, None]


def solution(mesh):
    in_specs = (
        P(("region", "radial"), None, "range"),
        P(None, "region"),
        P(("region", "radial"), "range"),
        P(("region", "radial"), "range"),
    )
    out_specs = P(("region", "range", "radial"), None)
    return jax.shard_map(local, mesh=mesh, in_specs=in_specs, out_specs=out_specs, check_vma=False)
```

```python
import functools
import math

import jax
import jax.numpy as jnp
import ml_dtypes
import numpy as np
from jax import lax
from jax.experimental import pallas as pl
from jax.experimental.pallas import tpu as pltpu
from jax.sharding import PartitionSpec as P

H = 4096
BIN = 32
LANES = 128
ROWS = H // LANES
FOUR = 4
EIGHT = 8
BINS = H // BIN
TILE_DEV = 16
TILT_SLOPE = 2.0
SPREAD_RATE = 0.5
ABSORB_RATE = 0.05
TERRAIN_ROWS = 4
SUB = 8

F32 = jnp.float32
BF16 = jnp.bfloat16


def split_np(table):
    high = table.astype(np.float32).astype(ml_dtypes.bfloat16)
    low = (table - high.astype(np.float64)).astype(ml_dtypes.bfloat16)
    return high, low


def tables():
    n = np.arange(LANES)
    angle = -2.0 * np.pi / LANES * (n[:, None] * n[None, :] % LANES)
    c, s = np.cos(angle), np.sin(angle)
    forward = np.block([[c, s], [-s, c]])
    inverse = np.block([[c, -s], [s, c]])
    weights = []
    for matrix in (forward, inverse):
        high, low = split_np(matrix)
        weights.append(np.concatenate([high, high, low], axis=0))
    q = np.arange(ROWS)
    angle = -2.0 * np.pi / H * (q[:, None] * n[None, :])
    twiddle = np.stack([np.cos(angle), np.sin(angle)]).astype(np.float32)
    frequency = q[:, None] + ROWS * n[None, :]
    signed = np.where(frequency >= H // 2, frequency - H, frequency)
    turning = -SPREAD_RATE * (2.0 * np.pi / H * signed) ** 2
    spread = (np.stack([np.cos(turning), np.sin(turning)]) / H).astype(np.float32)
    rel = np.arange(H).reshape(ROWS, LANES) / H
    tilt = (TILT_SLOPE * rel - 1.0).astype(np.float32)
    depth = np.maximum(rel - 0.75, 0.0) * 4.0
    absorb = np.exp(-ABSORB_RATE * depth * depth).astype(np.float32)
    bins = np.zeros((2 * LANES, BINS), np.float64)
    for lane in range(2 * LANES):
        bins[lane, (lane % LANES) // BIN :: LANES // BIN] = 1.0 / BIN
    return weights[0], weights[1], twiddle, spread, tilt, absorb, bins.astype(ml_dtypes.bfloat16)


def phase_polynomials():
    root = 2.0 ** 0.25
    sin_scale = root * math.sqrt(2.0)
    cos_scale = 2.0 * math.sqrt(2.0) / sin_scale
    limit = 7.001
    nodes = 0.5 * limit * limit * (1.0 + np.cos(np.pi * (np.arange(64) + 0.5) / 64))
    phi = np.sqrt(nodes)
    sine = np.polynomial.chebyshev.Chebyshev.fit(
        nodes, sin_scale * np.sin(phi / 4) / phi, 4, domain=[0, limit * limit]
    ).convert(kind=np.polynomial.Polynomial)
    cosine = np.polynomial.chebyshev.Chebyshev.fit(
        nodes, cos_scale * np.cos(phi / 4), 4, domain=[0, limit * limit]
    ).convert(kind=np.polynomial.Polynomial)
    return [float(v) for v in sine.coef], [float(v) for v in cosine.coef]


def unit(number, extent):
    angle = -2.0 * math.pi * (number % extent) / extent
    return math.cos(angle), math.sin(angle)


def cmul_const(value, factor):
    re, im = value
    c, s = factor
    if abs(s) < 1e-12 and c > 0:
        return value
    if abs(c) < 1e-12:
        return (im, -re) if s < 0 else (-im, re)
    return re * c - im * s, re * s + im * c


def add(a, b):
    return a[0] + b[0], a[1] + b[1]


def sub(a, b):
    return a[0] - b[0], a[1] - b[1]


def add_turned(a, b, sign):
    if sign < 0:
        return a[0] + b[1], a[1] - b[0]
    return a[0] - b[1], a[1] + b[0]


def dft4(x, sign):
    a, b = add(x[0], x[2]), sub(x[0], x[2])
    c, d = add(x[1], x[3]), sub(x[1], x[3])
    return [add(a, c), add_turned(b, d, sign), sub(a, c), add_turned(b, d, -sign)]


def eighth(a, sign):
    h = math.sqrt(0.5)
    re, im = a
    if sign < 0:
        return (re + im) * h, (im - re) * h
    return (re - im) * h, (re + im) * h


def dft8(x, sign):
    even = dft4(x[0::2], sign)
    odd = dft4(x[1::2], sign)
    odd[1], odd[3] = eighth(odd[1], sign), eighth(odd[3], sign)
    low = [add(even[0], odd[0]), add(even[1], odd[1]), add_turned(even[2], odd[2], sign), add_turned(even[3], odd[3], sign)]
    high = [sub(even[0], odd[0]), sub(even[1], odd[1]), add_turned(even[2], odd[2], -sign), add_turned(even[3], odd[3], -sign)]
    return low + high


def split(value):
    high = value.astype(BF16)
    low = (value - high.astype(F32)).astype(BF16)
    return high, low


def march_kernel(own, received, cells, start, w_forward, w_inverse, twiddle, spread, tilt, absorb, bins, section,
                 totals, levels, arrived, wide, field, back, energy, power):
    sine, cosine = phase_polynomials()
    sections, batch, steps, heights = levels.shape
    halves = batch // SUB
    copy = pltpu.make_async_copy(received, levels, arrived)
    copy.start()
    lane = lax.broadcasted_iota(jnp.int32, (SUB, LANES), 1)
    radial = lax.broadcasted_iota(jnp.int32, (SUB, LANES), 0)
    at_once = cells.shape[1] // 2

    def enter(half, columns, jl):
        parts = dft4(columns, -1)
        for ql in range(FOUR):
            re, im = cmul_const(parts[ql], unit(ql * jl, ROWS))
            field[half, 0, ql * EIGHT + jl] = re
            field[half, 1, ql * EIGHT + jl] = im

    def joined(pieces):
        re_high, re_low = split(jnp.concatenate([p[0] for p in pieces], axis=0))
        im_high, im_low = split(jnp.concatenate([p[1] for p in pieces], axis=0))
        return jnp.concatenate([re_high, im_high, re_low, im_low, re_high, im_high], axis=1)

    def parted(product):
        return [
            (product[i * SUB : (i + 1) * SUB, :LANES], product[i * SUB : (i + 1) * SUB, LANES:]) for i in range(ROWS)
        ]

    rows = [ql + FOUR * qh for ql in range(FOUR) for qh in range(EIGHT)]

    def forward(half):
        pieces = []
        for ql in range(FOUR):
            column = [(field[half, 0, ql * EIGHT + jl], field[half, 1, ql * EIGHT + jl]) for jl in range(EIGHT)]
            for qh, (re, im) in enumerate(dft8(column, -1)):
                q = ql + FOUR * qh
                c, s = twiddle[0, q : q + 1, :], twiddle[1, q : q + 1, :]
                pieces.append((re * c - im * s, re * s + im * c))
        return jnp.dot(joined(pieces), w_forward[...], preferred_element_type=F32)

    def inverse(product):
        pieces = []
        for q, (re, im) in zip(rows, parted(product)):
            c, s = spread[0, q : q + 1, :], spread[1, q : q + 1, :]
            pieces.append((re * c - im * s, re * s + im * c))
        return jnp.dot(joined(pieces), w_inverse[...], preferred_element_type=F32)

    def leave(half, product):
        pieces = []
        for q, (re, im) in zip(rows, parted(product)):
            c, s = twiddle[0, q : q + 1, :], twiddle[1, q : q + 1, :]
            pieces.append((re * c + im * s, im * c - re * s))
        for ql in range(FOUR):
            column = dft8(pieces[ql * EIGHT : (ql + 1) * EIGHT], 1)
            for jl in range(EIGHT):
                back[half, 0, ql * EIGHT + jl] = column[jl][0]
                back[half, 1, ql * EIGHT + jl] = column[jl][1]

    def rotate(half, t, ground, jls):
        for jl in jls:
            column = []
            for ql in range(FOUR):
                c, s = unit(ql * jl, ROWS)
                column.append(
                    cmul_const((back[half, 0, ql * EIGHT + jl], back[half, 1, ql * EIGHT + jl]), (c, -s))
                )
            column = dft4(column, 1)
            moved = []
            for jh in range(FOUR):
                j = EIGHT * jh + jl
                phi = wide[j, pl.ds(half * SUB * steps + t, SUB, stride=steps), :] + tilt[j : j + 1, :]
                u = phi * phi
                sin_poly, cos_poly = sine[-1], cosine[-1]
                for a, b in zip(sine[-2::-1], cosine[-2::-1]):
                    sin_poly = sin_poly * u + a
                    cos_poly = cos_poly * u + b
                small = sin_poly * phi
                double = small * cos_poly
                turned_c = 1.0 - double * double
                turned_s = double * (math.sqrt(2.0) - small * small)
                re, im = column[jh]
                if (j + 1) * LANES > 3 * H // 4:
                    loss = absorb[j : j + 1, :]
                    re, im = re * loss, im * loss
                re, im = re * turned_c - im * turned_s, re * turned_s + im * turned_c
                if j < TERRAIN_ROWS:
                    open_air = lane + j * LANES >= ground
                    re, im = jnp.where(open_air, re, 0.0), jnp.where(open_air, im, 0.0)
                value = re * re + im * im
                high = value.astype(BF16).astype(F32)
                energy[half, j * SUB : (j + 1) * SUB, :LANES] = high
                energy[half, j * SUB : (j + 1) * SUB, LANES:] = value - high
                moved.append((re, im))
            enter(half, moved, jl)

    def binned(half, t):
        summed = jnp.dot(energy[half].astype(BF16), bins[...], preferred_element_type=F32)
        row = summed[:SUB]
        for j in range(1, ROWS):
            row = jnp.where(lane // (LANES // BIN) == j, summed[j * SUB : (j + 1) * SUB], row)
        power[pl.ds(pl.multiple_of(t * batch + half * SUB, SUB), SUB), :] = row

    def ground_of(half, t):
        row = cells[t // at_once, pl.ds(t % at_once, 1), :]
        my_lane = lane == section[0] * own + half * SUB + radial
        return jnp.sum(jnp.where(my_lane, row, 0), axis=1, keepdims=True)

    def turn_of(t, resting, moving):
        ground = ground_of(resting, t)
        product = forward(moving)
        rotate(resting, t, ground, range(EIGHT // 2))
        product = inverse(product)
        rotate(resting, t, ground, range(EIGHT // 2, EIGHT))
        leave(moving, product)
        binned(resting, t)

    def step(t, carry):
        for half in range(halves):
            turn_of(t, half, (half + 1) % halves)
        return carry

    for half in range(halves):
        for jl in range(EIGHT):
            columns = []
            for jh in range(FOUR):
                j = EIGHT * jh + jl
                columns.append(tuple(jnp.broadcast_to(start[k, j : j + 1, :], (SUB, LANES)) for k in range(2)))
            enter(half, columns, jl)
    power[...] = jnp.zeros_like(power)
    leave(0, inverse(forward(0)))
    copy.wait()
    per_source = heights // LANES

    def widen(source, carry):
        for b in range(batch):
            for c in range(per_source):
                raw = levels[source, b, :, c * LANES : (c + 1) * LANES]
                wide[source * per_source + c, b * steps : (b + 1) * steps, :] = raw.astype(F32)
        return carry

    lax.fori_loop(0, sections, widen, 0)
    lax.fori_loop(0, steps, step, 0)

    lane = lax.broadcasted_iota(jnp.int32, (1, LANES), 1)
    fit = LANES // batch
    tile_rows = []
    for t in range(steps):
        row = cells[t // at_once, at_once + t % at_once, :].reshape(1, LANES)
        row = pltpu.roll(row, lax.rem(batch * (t % fit) - section[0] * own + LANES, LANES), 1)
        row = jnp.where(lane % batch < own, row, -1)
        if t % fit == 0:
            tile_rows.append(jnp.where(lane < batch, row, -1))
        else:
            tile_rows[-1] = jnp.where(lane // batch == t % fit, row, tile_rows[-1])
    tile_row = jnp.concatenate(tile_rows, axis=1)
    tiles, cell_count = totals.shape[0], tile_row.shape[1]
    hot = (lax.broadcasted_iota(jnp.int32, (tiles, cell_count), 0) == tile_row).astype(F32).astype(BF16)
    value = power[...]
    high = value.astype(BF16)
    rest = value - high.astype(F32)
    middle = rest.astype(BF16)
    low = (rest - middle.astype(F32)).astype(BF16)
    gain = jnp.dot(hot, high, preferred_element_type=F32)
    gain += jnp.dot(hot, middle, preferred_element_type=F32)
    gain += jnp.dot(hot, low, preferred_element_type=F32)
    totals[...] = gain


def march(section, received, cells, start, consts, tiles, own):
    sections, batch, steps, heights = received.shape
    halves = batch // SUB
    vmem = pl.BlockSpec(memory_space=pltpu.VMEM)
    smem = pl.BlockSpec(memory_space=pltpu.SMEM)
    call = pl.pallas_call(
        functools.partial(march_kernel, own),
        out_shape=jax.ShapeDtypeStruct((tiles, BINS), F32),
        in_specs=[pl.BlockSpec(memory_space=pl.ANY)] + [vmem] * 9 + [smem],
        out_specs=vmem,
        scratch_shapes=[
            pltpu.VMEM(received.shape, BF16),
            pltpu.SemaphoreType.DMA,
            pltpu.VMEM((ROWS, batch * steps, LANES), F32),
            pltpu.VMEM((halves, 2, ROWS, SUB, LANES), F32),
            pltpu.VMEM((halves, 2, ROWS, SUB, LANES), F32),
            pltpu.VMEM((halves, ROWS * SUB, 2 * LANES), F32),
            pltpu.VMEM((-(-steps * batch // LANES) * LANES, BINS), F32),
        ],
        compiler_params=pltpu.CompilerParams(vmem_limit_bytes=44 * 1024 * 1024),
        cost_estimate=pl.CostEstimate(
            flops=steps * 1_600_000_000, bytes_accessed=4 * 1024 * 1024, transcendentals=0
        ),
        name="march",
    )
    return call(received, cells, start, *consts, section)


def gather_small(value):
    radial, sections = lax.axis_index("radial"), lax.axis_size("range")
    other = lax.ppermute(value, "radial", [(0, 1), (1, 0)])
    pair = jnp.stack([jnp.where(radial == 0, value, other), jnp.where(radial == 0, other, value)])
    section = lax.axis_index("range")
    held = jnp.zeros((sections, *pair.shape), pair.dtype)
    held = lax.dynamic_update_index_in_dim(held, pair, section, 0)
    width = 1
    while width < sections:
        base = section // width * width
        part = lax.dynamic_slice_in_dim(held, base, width, 0)
        part = lax.ppermute(part, "range", [(i, i ^ width) for i in range(sections)])
        held = lax.dynamic_update_slice_in_dim(held, part, base ^ width, 0)
        width *= 2
    return held


def local(refractivity, source, terrain, tile_map):
    sections = lax.axis_size("range")
    owners = sections * lax.axis_size("radial")
    radials, steps, heights = refractivity.shape
    own = radials // sections
    batch = -(-own // 16) * 16
    section = lax.axis_index("range").astype(jnp.int32).reshape(1)

    received = refractivity.reshape(sections, own, steps, heights)
    received = lax.all_to_all(received, "range", 0, 0, tiled=True)
    received = jnp.pad(received, ((0, 0), (0, batch - own), (0, 0), (0, 0)))
    everyone = gather_small(jnp.concatenate([terrain.T, tile_map.T]))
    cells = lax.dynamic_index_in_dim(everyone, lax.axis_index("radial"), 1, keepdims=False)
    start = source.reshape(2, ROWS, LANES)
    totals = march(
        section, received, cells, start, [jnp.asarray(v) for v in tables()], TILE_DEV * owners, own
    )

    everyone, totals = lax.optimization_barrier((everyone, totals))
    sent = lax.all_to_all(
        totals.reshape(owners, TILE_DEV, BINS), ("range", "radial"), 0, 0, tiled=True
    )
    ids = (lax.axis_index("range") * lax.axis_size("radial") + lax.axis_index("radial")) * TILE_DEV
    ids = ids + jnp.arange(TILE_DEV, dtype=jnp.int32)
    counts = jnp.sum((ids[:, None] == everyone[:, :, terrain.shape[1] :].reshape(1, -1)).astype(F32), axis=1)
    return jnp.sum(sent, axis=0) / counts[:, None]


def solution(mesh):
    in_specs = (
        P(("region", "radial"), None, "range"),
        P(None, "region"),
        P(("region", "radial"), "range"),
        P(("region", "radial"), "range"),
    )
    out_specs = P(("region", "range", "radial"), None)
    return jax.shard_map(local, mesh=mesh, in_specs=in_specs, out_specs=out_specs, check_vma=False)
```

```python
import functools
import math

import jax
import jax.numpy as jnp
import ml_dtypes
import numpy as np
from jax import lax
from jax.experimental import pallas as pl
from jax.experimental.pallas import tpu as pltpu
from jax.sharding import PartitionSpec as P

H = 4096
BIN = 32
LANES = 128
ROWS = H // LANES
FOUR = 4
EIGHT = 8
BINS = H // BIN
TILE_DEV = 16
TILT_SLOPE = 2.0
SPREAD_RATE = 0.5
ABSORB_RATE = 0.05
TERRAIN_ROWS = 4
SUB = 8

F32 = jnp.float32
BF16 = jnp.bfloat16


def split_np(table):
    high = table.astype(np.float32).astype(ml_dtypes.bfloat16)
    low = (table - high.astype(np.float64)).astype(ml_dtypes.bfloat16)
    return high, low


def tables():
    n = np.arange(LANES)
    angle = -2.0 * np.pi / LANES * (n[:, None] * n[None, :] % LANES)
    c, s = np.cos(angle), np.sin(angle)
    forward = np.block([[c, s], [-s, c]])
    inverse = np.block([[c, -s], [s, c]])
    weights = []
    for matrix in (forward, inverse):
        high, low = split_np(matrix)
        weights.append(np.stack([high, low]))
    q = np.arange(ROWS)
    angle = -2.0 * np.pi / H * (q[:, None] * n[None, :])
    twiddle = np.stack([np.cos(angle), np.sin(angle)]).astype(np.float32)
    frequency = q[:, None] + ROWS * n[None, :]
    signed = np.where(frequency >= H // 2, frequency - H, frequency)
    turning = -SPREAD_RATE * (2.0 * np.pi / H * signed) ** 2
    spread = (np.stack([np.cos(turning), np.sin(turning)]) / H).astype(np.float32)
    rel = np.arange(H).reshape(ROWS, LANES) / H
    tilt = (TILT_SLOPE * rel - 1.0).astype(np.float32)
    depth = np.maximum(rel - 0.75, 0.0) * 4.0
    absorb = np.exp(-ABSORB_RATE * depth * depth).astype(np.float32)
    bins = np.zeros((2 * LANES, BINS), np.float64)
    for lane in range(2 * LANES):
        bins[lane, (lane % LANES) // BIN :: LANES // BIN] = 1.0 / BIN
    return weights[0], weights[1], twiddle, spread, tilt, absorb, bins.astype(ml_dtypes.bfloat16)


def phase_polynomials():
    root = 2.0 ** 0.25
    sin_scale = root * math.sqrt(2.0)
    cos_scale = 2.0 * math.sqrt(2.0) / sin_scale
    limit = 7.001
    nodes = 0.5 * limit * limit * (1.0 + np.cos(np.pi * (np.arange(64) + 0.5) / 64))
    phi = np.sqrt(nodes)
    sine = np.polynomial.chebyshev.Chebyshev.fit(
        nodes, sin_scale * np.sin(phi / 4) / phi, 4, domain=[0, limit * limit]
    ).convert(kind=np.polynomial.Polynomial)
    cosine = np.polynomial.chebyshev.Chebyshev.fit(
        nodes, cos_scale * np.cos(phi / 4), 4, domain=[0, limit * limit]
    ).convert(kind=np.polynomial.Polynomial)
    return [float(v) for v in sine.coef], [float(v) for v in cosine.coef]


def unit(number, extent):
    angle = -2.0 * math.pi * (number % extent) / extent
    return math.cos(angle), math.sin(angle)


def cmul_const(value, factor):
    re, im = value
    c, s = factor
    if abs(s) < 1e-12 and c > 0:
        return value
    if abs(c) < 1e-12:
        return (im, -re) if s < 0 else (-im, re)
    return re * c - im * s, re * s + im * c


def add(a, b):
    return a[0] + b[0], a[1] + b[1]


def sub(a, b):
    return a[0] - b[0], a[1] - b[1]


def add_turned(a, b, sign):
    if sign < 0:
        return a[0] + b[1], a[1] - b[0]
    return a[0] - b[1], a[1] + b[0]


def dft4(x, sign):
    a, b = add(x[0], x[2]), sub(x[0], x[2])
    c, d = add(x[1], x[3]), sub(x[1], x[3])
    return [add(a, c), add_turned(b, d, sign), sub(a, c), add_turned(b, d, -sign)]


def eighth(a, sign):
    h = math.sqrt(0.5)
    re, im = a
    if sign < 0:
        return (re + im) * h, (im - re) * h
    return (re - im) * h, (re + im) * h


def dft8(x, sign):
    even = dft4(x[0::2], sign)
    odd = dft4(x[1::2], sign)
    odd[1], odd[3] = eighth(odd[1], sign), eighth(odd[3], sign)
    low = [add(even[0], odd[0]), add(even[1], odd[1]), add_turned(even[2], odd[2], sign), add_turned(even[3], odd[3], sign)]
    high = [sub(even[0], odd[0]), sub(even[1], odd[1]), add_turned(even[2], odd[2], -sign), add_turned(even[3], odd[3], -sign)]
    return low + high


def split(value):
    high = value.astype(BF16)
    low = (value - high.astype(F32)).astype(BF16)
    return high, low


def enter(field, columns, jl):
    parts = dft4(columns, -1)
    for ql in range(FOUR):
        re, im = cmul_const(parts[ql], unit(ql * jl, ROWS))
        field[0, ql * EIGHT + jl] = re
        field[1, ql * EIGHT + jl] = im


def joined(pieces):
    re_high, re_low = split(jnp.concatenate([p[0] for p in pieces], axis=0))
    im_high, im_low = split(jnp.concatenate([p[1] for p in pieces], axis=0))
    return jnp.concatenate([re_high, im_high, re_low, im_low, re_high, im_high], axis=1)


def weighted(left, weights):
    return jnp.dot(left, jnp.concatenate([weights[0], weights[0], weights[1]]), preferred_element_type=F32)


def spread_rows(table, wide):
    for index in np.ndindex(table.shape[:-2]):
        for row in range(table.shape[-2]):
            place = (*index, row)
            wide[place] = jnp.broadcast_to(table[(*index, pl.ds(row, 1))], (SUB, LANES))


def parted(product):
    return [(product[i * SUB : (i + 1) * SUB, :LANES], product[i * SUB : (i + 1) * SUB, LANES:]) for i in range(ROWS)]


Q_ROWS = [ql + FOUR * qh for ql in range(FOUR) for qh in range(EIGHT)]


def forward(field, w_forward, twiddle):
    pieces = []
    for ql in range(FOUR):
        column = [(field[0, ql * EIGHT + jl], field[1, ql * EIGHT + jl]) for jl in range(EIGHT)]
        for qh, (re, im) in enumerate(dft8(column, -1)):
            q = ql + FOUR * qh
            c, s = twiddle[0, q], twiddle[1, q]
            pieces.append((re * c - im * s, re * s + im * c))
    return weighted(joined(pieces), w_forward)


def inverse(product, w_inverse, spread):
    pieces = []
    for q, (re, im) in zip(Q_ROWS, parted(product)):
        c, s = spread[0, q], spread[1, q]
        pieces.append((re * c - im * s, re * s + im * c))
    return weighted(joined(pieces), w_inverse)


def leave(back, product, twiddle):
    pieces = []
    for q, (re, im) in zip(Q_ROWS, parted(product)):
        c, s = twiddle[0, q], twiddle[1, q]
        pieces.append((re * c + im * s, im * c - re * s))
    for ql in range(FOUR):
        column = dft8(pieces[ql * EIGHT : (ql + 1) * EIGHT], 1)
        for jl in range(EIGHT):
            back[0, ql * EIGHT + jl] = column[jl][0]
            back[1, ql * EIGHT + jl] = column[jl][1]


def launch_kernel(start, w_forward, w_inverse, twiddle_table, spread_table, back, field, twiddle, spread):
    spread_rows(twiddle_table, twiddle)
    spread_rows(spread_table, spread)
    for jl in range(EIGHT):
        columns = []
        for jh in range(FOUR):
            j = EIGHT * jh + jl
            columns.append(tuple(jnp.broadcast_to(start[k, j : j + 1, :], (SUB, LANES)) for k in range(2)))
        enter(field, columns, jl)
    product = inverse(forward(field, w_forward, twiddle), w_inverse, spread)
    leave(back, product, twiddle)


def launch(start, consts):
    vmem = pl.BlockSpec(memory_space=pltpu.VMEM)
    return pl.pallas_call(
        launch_kernel,
        out_shape=[jax.ShapeDtypeStruct((2, ROWS, SUB, LANES), F32)] * 2,
        in_specs=[vmem] * 5,
        out_specs=[vmem] * 2,
        scratch_shapes=[pltpu.VMEM((2, ROWS, SUB, LANES), F32)] * 2,
        compiler_params=pltpu.CompilerParams(vmem_limit_bytes=8 * 1024 * 1024),
        cost_estimate=pl.CostEstimate(flops=1_000_000_000, bytes_accessed=1024 * 1024, transcendentals=0),
        name="launch",
    )(start, *consts[:4])


def march_kernel(own, levels, cells, launched, entered, w_forward, w_inverse, *refs):
    tables, (bins, section, totals, wide, field, back, energy, power), wide_tables = refs[:4], refs[4:12], refs[12:]
    for table, place in zip(tables, wide_tables):
        spread_rows(table, place)
    twiddle, spread, tilt, absorb = wide_tables
    sine, cosine = phase_polynomials()
    sections, batch, steps, heights = levels.shape
    halves = batch // SUB
    lane = lax.broadcasted_iota(jnp.int32, (SUB, LANES), 1)
    radial = lax.broadcasted_iota(jnp.int32, (SUB, LANES), 0)
    at_once = cells.shape[1] // 2

    def rotate(half, t, ground, jls):
        for jl in jls:
            column = []
            for ql in range(FOUR):
                c, s = unit(ql * jl, ROWS)
                column.append(
                    cmul_const((back[half, 0, ql * EIGHT + jl], back[half, 1, ql * EIGHT + jl]), (c, -s))
                )
            column = dft4(column, 1)
            moved = []
            for jh in range(FOUR):
                j = EIGHT * jh + jl
                phi = wide[j, pl.ds(half * SUB * steps + t, SUB, stride=steps), :] + tilt[j]
                u = phi * phi
                sin_poly, cos_poly = sine[-1], cosine[-1]
                for a, b in zip(sine[-2::-1], cosine[-2::-1]):
                    sin_poly = sin_poly * u + a
                    cos_poly = cos_poly * u + b
                small = sin_poly * phi
                double = small * cos_poly
                turned_c = 1.0 - double * double
                turned_s = double * (math.sqrt(2.0) - small * small)
                re, im = column[jh]
                if (j + 1) * LANES > 3 * H // 4:
                    loss = absorb[j]
                    re, im = re * loss, im * loss
                re, im = re * turned_c - im * turned_s, re * turned_s + im * turned_c
                if j < TERRAIN_ROWS:
                    open_air = lane + j * LANES >= ground
                    re, im = jnp.where(open_air, re, 0.0), jnp.where(open_air, im, 0.0)
                value = re * re + im * im
                high = value.astype(BF16).astype(F32)
                energy[half, j * SUB : (j + 1) * SUB, :LANES] = high
                energy[half, j * SUB : (j + 1) * SUB, LANES:] = value - high
                moved.append((re, im))
            enter(field.at[half], moved, jl)

    def binned(half, t):
        summed = jnp.dot(energy[half].astype(BF16), bins[...], preferred_element_type=F32)
        row = summed[:SUB]
        for j in range(1, ROWS):
            row = jnp.where(lane // (LANES // BIN) == j, summed[j * SUB : (j + 1) * SUB], row)
        power[pl.ds(pl.multiple_of(t * batch + half * SUB, SUB), SUB), :] = row

    def ground_of(half, t):
        row = cells[t // at_once, pl.ds(t % at_once, 1), :]
        my_lane = lane == section[0] * own + half * SUB + radial
        return jnp.sum(jnp.where(my_lane, row, 0), axis=1, keepdims=True)

    def turn_of(t, resting, moving):
        ground = ground_of(resting, t)
        product = forward(field.at[moving], w_forward, twiddle)
        rotate(resting, t, ground, range(EIGHT // 2))
        product = inverse(product, w_inverse, spread)
        rotate(resting, t, ground, range(EIGHT // 2, EIGHT))
        leave(back.at[moving], product, twiddle)
        binned(resting, t)

    def step(t, carry):
        for half in range(halves):
            turn_of(t, half, (half + 1) % halves)
        return carry

    power[...] = jnp.zeros_like(power)
    for half in range(halves):
        back[half] = launched[...]
        field[half] = entered[...]
    per_source = heights // LANES

    def widen(source, carry):
        for b in range(batch):
            for c in range(per_source):
                raw = levels[source, b, :, c * LANES : (c + 1) * LANES]
                wide[source * per_source + c, b * steps : (b + 1) * steps, :] = raw.astype(F32)
        return carry

    lax.fori_loop(0, sections, widen, 0)
    lax.fori_loop(0, steps, step, 0)

    lane = lax.broadcasted_iota(jnp.int32, (1, LANES), 1)
    fit = LANES // batch
    tile_rows = []
    for t in range(steps):
        row = cells[t // at_once, at_once + t % at_once, :].reshape(1, LANES)
        row = pltpu.roll(row, lax.rem(batch * (t % fit) - section[0] * own + LANES, LANES), 1)
        row = jnp.where(lane % batch < own, row, -1)
        if t % fit == 0:
            tile_rows.append(jnp.where(lane < batch, row, -1))
        else:
            tile_rows[-1] = jnp.where(lane // batch == t % fit, row, tile_rows[-1])
    tile_row = jnp.concatenate(tile_rows, axis=1)
    tiles, cell_count = totals.shape[0], tile_row.shape[1]
    hot = (lax.broadcasted_iota(jnp.int32, (tiles, cell_count), 0) == tile_row).astype(F32).astype(BF16)
    value = power[...]
    high = value.astype(BF16)
    rest = value - high.astype(F32)
    middle = rest.astype(BF16)
    low = (rest - middle.astype(F32)).astype(BF16)
    gain = jnp.dot(hot, high, preferred_element_type=F32)
    gain += jnp.dot(hot, middle, preferred_element_type=F32)
    gain += jnp.dot(hot, low, preferred_element_type=F32)
    totals[...] = gain


def march(section, received, cells, launched, consts, tiles, own):
    sections, batch, steps, heights = received.shape
    halves = batch // SUB
    vmem = pl.BlockSpec(memory_space=pltpu.VMEM)
    smem = pl.BlockSpec(memory_space=pltpu.SMEM)
    call = pl.pallas_call(
        functools.partial(march_kernel, own),
        out_shape=jax.ShapeDtypeStruct((tiles, BINS), F32),
        in_specs=[vmem] * 11 + [smem],
        out_specs=vmem,
        scratch_shapes=[
            pltpu.VMEM((ROWS, batch * steps, LANES), F32),
            pltpu.VMEM((halves, 2, ROWS, SUB, LANES), F32),
            pltpu.VMEM((halves, 2, ROWS, SUB, LANES), F32),
            pltpu.VMEM((halves, ROWS * SUB, 2 * LANES), F32),
            pltpu.VMEM((-(-steps * batch // LANES) * LANES, BINS), F32),
        ] + [pltpu.VMEM((*table.shape[:-1], SUB, LANES), F32) for table in consts[2:6]],
        compiler_params=pltpu.CompilerParams(vmem_limit_bytes=10 * 1024 * 1024 + 4 * H * batch * steps),
        cost_estimate=pl.CostEstimate(
            flops=steps * 1_600_000_000, bytes_accessed=4 * 1024 * 1024, transcendentals=0
        ),
        name="march",
    )
    return call(received, cells, *launched, *consts, section)


def gather_small(value):
    radial, sections = lax.axis_index("radial"), lax.axis_size("range")
    other = lax.ppermute(value, "radial", [(0, 1), (1, 0)])
    pair = jnp.stack([jnp.where(radial == 0, value, other), jnp.where(radial == 0, other, value)])
    section = lax.axis_index("range")
    held = jnp.zeros((sections, *pair.shape), pair.dtype)
    for d in range(sections):
        part = lax.ppermute(pair, "range", [(i, i ^ d) for i in range(sections)]) if d else pair
        held = lax.dynamic_update_index_in_dim(held, part, section ^ d, 0)
    return held


def local(refractivity, source, terrain, tile_map):
    sections = lax.axis_size("range")
    owners = sections * lax.axis_size("radial")
    radials, steps, heights = refractivity.shape
    own = radials // sections
    batch = -(-own // 16) * 16
    section = lax.axis_index("range").astype(jnp.int32).reshape(1)

    received = refractivity.reshape(sections, own, steps, heights)
    received = lax.all_to_all(received, "range", 0, 0, tiled=True)
    received = jnp.pad(received, ((0, 0), (0, batch - own), (0, 0), (0, 0)))
    everyone = gather_small(jnp.concatenate([terrain.T, tile_map.T]))
    cells = lax.dynamic_index_in_dim(everyone, lax.axis_index("radial"), 1, keepdims=False)
    consts = [jnp.asarray(v) for v in tables()]
    launched = launch(source.reshape(2, ROWS, LANES), consts)
    totals = march(section, received, cells, launched, consts, TILE_DEV * owners, own)

    everyone, totals = lax.optimization_barrier((everyone, totals))
    sent = lax.all_to_all(
        totals.reshape(owners, TILE_DEV, BINS), ("range", "radial"), 0, 0, tiled=True
    )
    ids = (lax.axis_index("range") * lax.axis_size("radial") + lax.axis_index("radial")) * TILE_DEV
    ids = ids + jnp.arange(TILE_DEV, dtype=jnp.int32)
    counts = jnp.sum((ids[:, None] == everyone[:, :, terrain.shape[1] :].reshape(1, -1)).astype(F32), axis=1)
    return jnp.sum(sent, axis=0) / counts[:, None]


def solution(mesh):
    in_specs = (
        P(("region", "radial"), None, "range"),
        P(None, "region"),
        P(("region", "radial"), "range"),
        P(("region", "radial"), "range"),
    )
    out_specs = P(("region", "range", "radial"), None)
    return jax.shard_map(local, mesh=mesh, in_specs=in_specs, out_specs=out_specs, check_vma=False)
```

```python
import functools
import math

import jax
import jax.numpy as jnp
import ml_dtypes
import numpy as np
from jax import lax
from jax.experimental import pallas as pl
from jax.experimental.pallas import tpu as pltpu
from jax.sharding import PartitionSpec as P

H = 4096
BIN = 32
LANES = 128
ROWS = H // LANES
FOUR = 4
EIGHT = 8
BINS = H // BIN
TILE_DEV = 16
TILT_SLOPE = 2.0
SPREAD_RATE = 0.5
ABSORB_RATE = 0.05
TERRAIN_ROWS = 4
SUB = 8

F32 = jnp.float32
BF16 = jnp.bfloat16


def split_np(table):
    high = table.astype(np.float32).astype(ml_dtypes.bfloat16)
    low = (table - high.astype(np.float64)).astype(ml_dtypes.bfloat16)
    return high, low


def tables():
    n = np.arange(LANES)
    angle = -2.0 * np.pi / LANES * (n[:, None] * n[None, :] % LANES)
    c, s = np.cos(angle), np.sin(angle)
    forward = np.block([[c, s], [-s, c]])
    inverse = np.block([[c, -s], [s, c]])
    weights = []
    for matrix in (forward, inverse):
        high, low = split_np(matrix)
        weights.append(np.stack([high, low]))
    q = np.arange(ROWS)
    angle = -2.0 * np.pi / H * (q[:, None] * n[None, :])
    twiddle = np.stack([np.cos(angle), np.sin(angle)]).astype(np.float32)
    frequency = q[:, None] + ROWS * n[None, :]
    signed = np.where(frequency >= H // 2, frequency - H, frequency)
    turning = -SPREAD_RATE * (2.0 * np.pi / H * signed) ** 2
    spread = (np.stack([np.cos(turning), np.sin(turning)]) / H).astype(np.float32)
    rel = np.arange(H).reshape(ROWS, LANES) / H
    tilt = (TILT_SLOPE * rel - 1.0).astype(np.float32)
    depth = np.maximum(rel - 0.75, 0.0) * 4.0
    absorb = np.exp(-ABSORB_RATE * depth * depth).astype(np.float32)
    bins = np.zeros((2 * LANES, BINS), np.float64)
    for lane in range(2 * LANES):
        bins[lane, (lane % LANES) // BIN :: LANES // BIN] = 1.0 / BIN
    return weights[0], weights[1], twiddle, spread, tilt, absorb, bins.astype(ml_dtypes.bfloat16)


def phase_polynomials():
    root = 2.0 ** 0.25
    sin_scale = root * math.sqrt(2.0)
    cos_scale = 2.0 * math.sqrt(2.0) / sin_scale
    limit = 7.001
    nodes = 0.5 * limit * limit * (1.0 + np.cos(np.pi * (np.arange(64) + 0.5) / 64))
    phi = np.sqrt(nodes)
    sine = np.polynomial.chebyshev.Chebyshev.fit(
        nodes, sin_scale * np.sin(phi / 4) / phi, 4, domain=[0, limit * limit]
    ).convert(kind=np.polynomial.Polynomial)
    cosine = np.polynomial.chebyshev.Chebyshev.fit(
        nodes, cos_scale * np.cos(phi / 4), 4, domain=[0, limit * limit]
    ).convert(kind=np.polynomial.Polynomial)
    return [float(v) for v in sine.coef], [float(v) for v in cosine.coef]


def unit(number, extent):
    angle = -2.0 * math.pi * (number % extent) / extent
    return math.cos(angle), math.sin(angle)


def cmul_const(value, factor):
    re, im = value
    c, s = factor
    if abs(s) < 1e-12 and c > 0:
        return value
    if abs(c) < 1e-12:
        return (im, -re) if s < 0 else (-im, re)
    return re * c - im * s, re * s + im * c


def add(a, b):
    return a[0] + b[0], a[1] + b[1]


def sub(a, b):
    return a[0] - b[0], a[1] - b[1]


def add_turned(a, b, sign):
    if sign < 0:
        return a[0] + b[1], a[1] - b[0]
    return a[0] - b[1], a[1] + b[0]


def dft4(x, sign):
    a, b = add(x[0], x[2]), sub(x[0], x[2])
    c, d = add(x[1], x[3]), sub(x[1], x[3])
    return [add(a, c), add_turned(b, d, sign), sub(a, c), add_turned(b, d, -sign)]


def eighth(a, sign):
    h = math.sqrt(0.5)
    re, im = a
    if sign < 0:
        return (re + im) * h, (im - re) * h
    return (re - im) * h, (re + im) * h


def dft8(x, sign):
    even = dft4(x[0::2], sign)
    odd = dft4(x[1::2], sign)
    odd[1], odd[3] = eighth(odd[1], sign), eighth(odd[3], sign)
    low = [add(even[0], odd[0]), add(even[1], odd[1]), add_turned(even[2], odd[2], sign), add_turned(even[3], odd[3], sign)]
    high = [sub(even[0], odd[0]), sub(even[1], odd[1]), add_turned(even[2], odd[2], -sign), add_turned(even[3], odd[3], -sign)]
    return low + high


def split(value):
    high = value.astype(BF16)
    low = (value - high.astype(F32)).astype(BF16)
    return high, low


def enter(field, columns, jl):
    parts = dft4(columns, -1)
    for ql in range(FOUR):
        re, im = cmul_const(parts[ql], unit(ql * jl, ROWS))
        field[0, ql * EIGHT + jl] = re
        field[1, ql * EIGHT + jl] = im


def joined(pieces):
    re_high, re_low = split(jnp.concatenate([p[0] for p in pieces], axis=0))
    im_high, im_low = split(jnp.concatenate([p[1] for p in pieces], axis=0))
    return jnp.concatenate([re_high, im_high], axis=1), jnp.concatenate([re_low, im_low], axis=1)


def weighted(left, weights, between=()):
    high, low = left
    between = list(between) + [lambda: None] * 3
    total = None
    for part, weight in ((high, weights[0]), (low, weights[0]), (high, weights[1])):
        product = jnp.dot(part, weight, preferred_element_type=F32)
        between.pop(0)()
        total = product if total is None else total + product
    return total


def spread_rows(table, wide):
    for index in np.ndindex(table.shape[:-2]):
        for row in range(table.shape[-2]):
            place = (*index, row)
            wide[place] = jnp.broadcast_to(table[(*index, pl.ds(row, 1))], (SUB, LANES))


def parted(product):
    return [(product[i * SUB : (i + 1) * SUB, :LANES], product[i * SUB : (i + 1) * SUB, LANES:]) for i in range(ROWS)]


Q_ROWS = [ql + FOUR * qh for ql in range(FOUR) for qh in range(EIGHT)]


def forward(field, w_forward, twiddle, between=()):
    pieces = []
    for ql in range(FOUR):
        column = [(field[0, ql * EIGHT + jl], field[1, ql * EIGHT + jl]) for jl in range(EIGHT)]
        for qh, (re, im) in enumerate(dft8(column, -1)):
            q = ql + FOUR * qh
            c, s = twiddle[0, q], twiddle[1, q]
            pieces.append((re * c - im * s, re * s + im * c))
    return weighted(joined(pieces), w_forward, between)


def inverse(product, w_inverse, spread, between=()):
    pieces = []
    for q, (re, im) in zip(Q_ROWS, parted(product)):
        c, s = spread[0, q], spread[1, q]
        pieces.append((re * c - im * s, re * s + im * c))
    return weighted(joined(pieces), w_inverse, between)


def leave(back, product, twiddle):
    pieces = []
    for q, (re, im) in zip(Q_ROWS, parted(product)):
        c, s = twiddle[0, q], twiddle[1, q]
        pieces.append((re * c + im * s, im * c - re * s))
    for ql in range(FOUR):
        column = dft8(pieces[ql * EIGHT : (ql + 1) * EIGHT], 1)
        for jl in range(EIGHT):
            back[0, ql * EIGHT + jl] = column[jl][0]
            back[1, ql * EIGHT + jl] = column[jl][1]


def launch_kernel(start, w_forward, w_inverse, twiddle_table, spread_table, back, field, twiddle, spread):
    spread_rows(twiddle_table, twiddle)
    spread_rows(spread_table, spread)
    for jl in range(EIGHT):
        columns = []
        for jh in range(FOUR):
            j = EIGHT * jh + jl
            columns.append(tuple(jnp.broadcast_to(start[k, j : j + 1, :], (SUB, LANES)) for k in range(2)))
        enter(field, columns, jl)
    product = inverse(forward(field, w_forward, twiddle), w_inverse, spread)
    leave(back, product, twiddle)


def launch(start, consts):
    vmem = pl.BlockSpec(memory_space=pltpu.VMEM)
    return pl.pallas_call(
        launch_kernel,
        out_shape=[jax.ShapeDtypeStruct((2, ROWS, SUB, LANES), F32)] * 2,
        in_specs=[vmem] * 5,
        out_specs=[vmem] * 2,
        scratch_shapes=[pltpu.VMEM((2, ROWS, SUB, LANES), F32)] * 2,
        compiler_params=pltpu.CompilerParams(vmem_limit_bytes=8 * 1024 * 1024),
        cost_estimate=pl.CostEstimate(flops=1_000_000_000, bytes_accessed=1024 * 1024, transcendentals=0),
        name="launch",
    )(start, *consts[:4])


def march_kernel(own, levels, cells, launched, entered, w_forward, w_inverse, *refs):
    tables, (bins, section, totals, wide, field, back, energy, power), wide_tables = refs[:4], refs[4:12], refs[12:]
    for table, place in zip(tables, wide_tables):
        spread_rows(table, place)
    twiddle, spread, tilt, absorb = wide_tables
    sine, cosine = phase_polynomials()
    sections, batch, steps, heights = levels.shape
    halves = batch // SUB
    lane = lax.broadcasted_iota(jnp.int32, (SUB, LANES), 1)
    radial = lax.broadcasted_iota(jnp.int32, (SUB, LANES), 0)
    at_once = cells.shape[1] // 2

    def rotate(half, t, ground, jls):
        for jl in jls:
            column = []
            for ql in range(FOUR):
                c, s = unit(ql * jl, ROWS)
                column.append(
                    cmul_const((back[half, 0, ql * EIGHT + jl], back[half, 1, ql * EIGHT + jl]), (c, -s))
                )
            column = dft4(column, 1)
            moved = []
            for jh in range(FOUR):
                j = EIGHT * jh + jl
                phi = wide[j, pl.ds(half * SUB * steps + t, SUB, stride=steps), :] + tilt[j]
                u = phi * phi
                sin_poly, cos_poly = sine[-1], cosine[-1]
                for a, b in zip(sine[-2::-1], cosine[-2::-1]):
                    sin_poly = sin_poly * u + a
                    cos_poly = cos_poly * u + b
                small = sin_poly * phi
                double = small * cos_poly
                turned_c = 1.0 - double * double
                turned_s = double * (math.sqrt(2.0) - small * small)
                re, im = column[jh]
                if (j + 1) * LANES > 3 * H // 4:
                    loss = absorb[j]
                    re, im = re * loss, im * loss
                re, im = re * turned_c - im * turned_s, re * turned_s + im * turned_c
                if j < TERRAIN_ROWS:
                    open_air = lane + j * LANES >= ground
                    re, im = jnp.where(open_air, re, 0.0), jnp.where(open_air, im, 0.0)
                value = re * re + im * im
                high = value.astype(BF16).astype(F32)
                energy[half, j * SUB : (j + 1) * SUB, :LANES] = high
                energy[half, j * SUB : (j + 1) * SUB, LANES:] = value - high
                moved.append((re, im))
            enter(field.at[half], moved, jl)

    def binned(half, t):
        summed = jnp.dot(energy[half].astype(BF16), bins[...], preferred_element_type=F32)
        row = summed[:SUB]
        for j in range(1, ROWS):
            row = jnp.where(lane // (LANES // BIN) == j, summed[j * SUB : (j + 1) * SUB], row)
        power[pl.ds(pl.multiple_of(t * batch + half * SUB, SUB), SUB), :] = row

    def ground_of(half, t):
        row = cells[t // at_once, pl.ds(t % at_once, 1), :]
        my_lane = lane == section[0] * own + half * SUB + radial
        return jnp.sum(jnp.where(my_lane, row, 0), axis=1, keepdims=True)

    def turn_of(t, resting, moving):
        ground = ground_of(resting, t)
        pieces = [functools.partial(rotate, resting, t, ground, [jl]) for jl in range(EIGHT)]
        product = forward(field.at[moving], w_forward, twiddle, pieces[:3])
        binned(moving, jnp.maximum(t - 1, 0) if resting == 0 else t)
        product = inverse(product, w_inverse, spread, pieces[3:6])
        for piece in pieces[6:]:
            piece()
        leave(back.at[moving], product, twiddle)

    def step(t, carry):
        for half in range(halves):
            turn_of(t, half, (half + 1) % halves)
        return carry

    power[...] = jnp.zeros_like(power)
    for half in range(halves):
        back[half] = launched[...]
        field[half] = entered[...]
    per_source = heights // LANES

    def widen(source, carry):
        for b in range(batch):
            for c in range(per_source):
                raw = levels[source, b, :, c * LANES : (c + 1) * LANES]
                wide[source * per_source + c, b * steps : (b + 1) * steps, :] = raw.astype(F32)
        return carry

    lax.fori_loop(0, sections, widen, 0)
    energy[...] = jnp.zeros_like(energy)
    lax.fori_loop(0, steps, step, 0)
    binned(halves - 1, steps - 1)

    lane = lax.broadcasted_iota(jnp.int32, (1, LANES), 1)
    fit = LANES // batch
    tile_rows = []
    for t in range(steps):
        row = cells[t // at_once, at_once + t % at_once, :].reshape(1, LANES)
        row = pltpu.roll(row, lax.rem(batch * (t % fit) - section[0] * own + LANES, LANES), 1)
        row = jnp.where(lane % batch < own, row, -1)
        if t % fit == 0:
            tile_rows.append(jnp.where(lane < batch, row, -1))
        else:
            tile_rows[-1] = jnp.where(lane // batch == t % fit, row, tile_rows[-1])
    tile_row = jnp.concatenate(tile_rows, axis=1)
    tiles, cell_count = totals.shape[0], tile_row.shape[1]
    hot = (lax.broadcasted_iota(jnp.int32, (tiles, cell_count), 0) == tile_row).astype(F32).astype(BF16)
    value = power[...]
    high = value.astype(BF16)
    rest = value - high.astype(F32)
    middle = rest.astype(BF16)
    low = (rest - middle.astype(F32)).astype(BF16)
    gain = jnp.dot(hot, high, preferred_element_type=F32)
    gain += jnp.dot(hot, middle, preferred_element_type=F32)
    gain += jnp.dot(hot, low, preferred_element_type=F32)
    totals[...] = gain


def march(section, received, cells, launched, consts, tiles, own):
    sections, batch, steps, heights = received.shape
    halves = batch // SUB
    vmem = pl.BlockSpec(memory_space=pltpu.VMEM)
    smem = pl.BlockSpec(memory_space=pltpu.SMEM)
    call = pl.pallas_call(
        functools.partial(march_kernel, own),
        out_shape=jax.ShapeDtypeStruct((tiles, BINS), F32),
        in_specs=[vmem] * 11 + [smem],
        out_specs=vmem,
        scratch_shapes=[
            pltpu.VMEM((ROWS, batch * steps, LANES), F32),
            pltpu.VMEM((halves, 2, ROWS, SUB, LANES), F32),
            pltpu.VMEM((halves, 2, ROWS, SUB, LANES), F32),
            pltpu.VMEM((halves, ROWS * SUB, 2 * LANES), F32),
            pltpu.VMEM((-(-steps * batch // LANES) * LANES, BINS), F32),
        ] + [pltpu.VMEM((*table.shape[:-1], SUB, LANES), F32) for table in consts[2:6]],
        compiler_params=pltpu.CompilerParams(vmem_limit_bytes=10 * 1024 * 1024 + 4 * H * batch * steps),
        cost_estimate=pl.CostEstimate(
            flops=steps * 1_600_000_000, bytes_accessed=4 * 1024 * 1024, transcendentals=0
        ),
        name="march",
    )
    return call(received, cells, *launched, *consts, section)


def gather_small(value):
    radial, sections = lax.axis_index("radial"), lax.axis_size("range")
    other = lax.ppermute(value, "radial", [(0, 1), (1, 0)])
    pair = jnp.stack([jnp.where(radial == 0, value, other), jnp.where(radial == 0, other, value)])
    section = lax.axis_index("range")
    held = jnp.zeros((sections, *pair.shape), pair.dtype)
    for d in range(sections):
        part = lax.ppermute(pair, "range", [(i, i ^ d) for i in range(sections)]) if d else pair
        held = lax.dynamic_update_index_in_dim(held, part, section ^ d, 0)
    return held


def local(refractivity, source, terrain, tile_map):
    sections = lax.axis_size("range")
    owners = sections * lax.axis_size("radial")
    radials, steps, heights = refractivity.shape
    own = radials // sections
    batch = -(-own // 16) * 16
    section = lax.axis_index("range").astype(jnp.int32).reshape(1)

    received = refractivity.reshape(sections, own, steps, heights)
    received = lax.all_to_all(received, "range", 0, 0, tiled=True)
    received = jnp.pad(received, ((0, 0), (0, batch - own), (0, 0), (0, 0)))
    everyone = gather_small(jnp.concatenate([terrain.T, tile_map.T]))
    cells = lax.dynamic_index_in_dim(everyone, lax.axis_index("radial"), 1, keepdims=False)
    consts = [jnp.asarray(v) for v in tables()]
    launched = launch(source.reshape(2, ROWS, LANES), consts)
    totals = march(section, received, cells, launched, consts, TILE_DEV * owners, own)

    everyone, totals = lax.optimization_barrier((everyone, totals))
    sent = lax.all_to_all(
        totals.reshape(owners, TILE_DEV, BINS), ("range", "radial"), 0, 0, tiled=True
    )
    ids = (lax.axis_index("range") * lax.axis_size("radial") + lax.axis_index("radial")) * TILE_DEV
    ids = ids + jnp.arange(TILE_DEV, dtype=jnp.int32)
    counts = jnp.sum((ids[:, None] == everyone[:, :, terrain.shape[1] :].reshape(1, -1)).astype(F32), axis=1)
    return jnp.sum(sent, axis=0) / counts[:, None]


def solution(mesh):
    in_specs = (
        P(("region", "radial"), None, "range"),
        P(None, "region"),
        P(("region", "radial"), "range"),
        P(("region", "radial"), "range"),
    )
    out_specs = P(("region", "range", "radial"), None)
    return jax.shard_map(local, mesh=mesh, in_specs=in_specs, out_specs=out_specs, check_vma=False)
```

```python
import functools
import math

import jax
import jax.numpy as jnp
import ml_dtypes
import numpy as np
from jax import lax
from jax.experimental import pallas as pl
from jax.experimental.pallas import tpu as pltpu
from jax.sharding import PartitionSpec as P

H = 4096
BIN = 32
LANES = 128
ROWS = H // LANES
FOUR = 4
EIGHT = 8
BINS = H // BIN
TILE_DEV = 16
TILT_SLOPE = 2.0
SPREAD_RATE = 0.5
ABSORB_RATE = 0.05
TERRAIN_ROWS = 4
SUB = 8

F32 = jnp.float32
BF16 = jnp.bfloat16


def split_np(table):
    high = table.astype(np.float32).astype(ml_dtypes.bfloat16)
    low = (table - high.astype(np.float64)).astype(ml_dtypes.bfloat16)
    return high, low


def tables():
    n = np.arange(LANES)
    angle = -2.0 * np.pi / LANES * (n[:, None] * n[None, :] % LANES)
    c, s = np.cos(angle), np.sin(angle)
    forward = np.block([[c, s], [-s, c]])
    inverse = np.block([[c, -s], [s, c]])
    weights = []
    for matrix in (forward, inverse):
        high, low = split_np(matrix)
        weights.append(np.concatenate([high, low], axis=1))
    q = np.arange(ROWS)
    angle = -2.0 * np.pi / H * (q[:, None] * n[None, :])
    twiddle = np.stack([np.cos(angle), np.sin(angle)]).astype(np.float32)
    frequency = q[:, None] + ROWS * n[None, :]
    signed = np.where(frequency >= H // 2, frequency - H, frequency)
    turning = -SPREAD_RATE * (2.0 * np.pi / H * signed) ** 2
    spread = (np.stack([np.cos(turning), np.sin(turning)]) / H).astype(np.float32)
    rel = np.arange(H).reshape(ROWS, LANES) / H
    tilt = (TILT_SLOPE * rel - 1.0).astype(np.float32)
    depth = np.maximum(rel - 0.75, 0.0) * 4.0
    absorb = np.exp(-ABSORB_RATE * depth * depth).astype(np.float32)
    bins = np.zeros((2 * LANES, BINS), np.float64)
    for lane in range(2 * LANES):
        bins[lane, (lane % LANES) // BIN :: LANES // BIN] = 1.0 / BIN
    return weights[0], weights[1], twiddle, spread, tilt, absorb, bins.astype(ml_dtypes.bfloat16)


def phase_polynomials():
    root = 2.0 ** 0.25
    sin_scale = root * math.sqrt(2.0)
    cos_scale = 2.0 * math.sqrt(2.0) / sin_scale
    limit = 7.001
    nodes = 0.5 * limit * limit * (1.0 + np.cos(np.pi * (np.arange(64) + 0.5) / 64))
    phi = np.sqrt(nodes)
    sine = np.polynomial.chebyshev.Chebyshev.fit(
        nodes, sin_scale * np.sin(phi / 4) / phi, 4, domain=[0, limit * limit]
    ).convert(kind=np.polynomial.Polynomial)
    cosine = np.polynomial.chebyshev.Chebyshev.fit(
        nodes, cos_scale * np.cos(phi / 4), 4, domain=[0, limit * limit]
    ).convert(kind=np.polynomial.Polynomial)
    return [float(v) for v in sine.coef], [float(v) for v in cosine.coef]


def unit(number, extent):
    angle = -2.0 * math.pi * (number % extent) / extent
    return math.cos(angle), math.sin(angle)


def cmul_const(value, factor):
    re, im = value
    c, s = factor
    if abs(s) < 1e-12 and c > 0:
        return value
    if abs(c) < 1e-12:
        return (im, -re) if s < 0 else (-im, re)
    return re * c - im * s, re * s + im * c


def add(a, b):
    return a[0] + b[0], a[1] + b[1]


def sub(a, b):
    return a[0] - b[0], a[1] - b[1]


def add_turned(a, b, sign):
    if sign < 0:
        return a[0] + b[1], a[1] - b[0]
    return a[0] - b[1], a[1] + b[0]


def dft4(x, sign):
    a, b = add(x[0], x[2]), sub(x[0], x[2])
    c, d = add(x[1], x[3]), sub(x[1], x[3])
    return [add(a, c), add_turned(b, d, sign), sub(a, c), add_turned(b, d, -sign)]


def eighth(a, sign):
    h = math.sqrt(0.5)
    re, im = a
    if sign < 0:
        return (re + im) * h, (im - re) * h
    return (re - im) * h, (re + im) * h


def dft8(x, sign):
    even = dft4(x[0::2], sign)
    odd = dft4(x[1::2], sign)
    odd[1], odd[3] = eighth(odd[1], sign), eighth(odd[3], sign)
    low = [add(even[0], odd[0]), add(even[1], odd[1]), add_turned(even[2], odd[2], sign), add_turned(even[3], odd[3], sign)]
    high = [sub(even[0], odd[0]), sub(even[1], odd[1]), add_turned(even[2], odd[2], -sign), add_turned(even[3], odd[3], -sign)]
    return low + high


def split(value):
    high = value.astype(BF16)
    low = (value - high.astype(F32)).astype(BF16)
    return high, low


def enter(field, columns, jl):
    parts = dft4(columns, -1)
    for ql in range(FOUR):
        re, im = cmul_const(parts[ql], unit(ql * jl, ROWS))
        field[0, ql * EIGHT + jl] = re
        field[1, ql * EIGHT + jl] = im


def joined(pieces):
    re_high, re_low = split(jnp.concatenate([p[0] for p in pieces], axis=0))
    im_high, im_low = split(jnp.concatenate([p[1] for p in pieces], axis=0))
    return jnp.concatenate(
        [jnp.concatenate([re_high, im_high], axis=1), jnp.concatenate([re_low, im_low], axis=1)], axis=0
    )


def weighted(left, weights):
    product = jnp.dot(left, weights[...], preferred_element_type=F32)
    rows, width = left.shape[0] // 2, weights.shape[1] // 2
    high, low = product[:rows], product[rows:]
    return high[:, :width] + (high[:, width:] + low[:, :width]) + low[:, width:]


def spread_rows(table, wide):
    for index in np.ndindex(table.shape[:-2]):
        for row in range(table.shape[-2]):
            place = (*index, row)
            wide[place] = jnp.broadcast_to(table[(*index, pl.ds(row, 1))], (SUB, LANES))


def parted(product):
    return [(product[i * SUB : (i + 1) * SUB, :LANES], product[i * SUB : (i + 1) * SUB, LANES:]) for i in range(ROWS)]


Q_ROWS = [ql + FOUR * qh for ql in range(FOUR) for qh in range(EIGHT)]


def forward(field, w_forward, twiddle):
    pieces = []
    for ql in range(FOUR):
        column = [(field[0, ql * EIGHT + jl], field[1, ql * EIGHT + jl]) for jl in range(EIGHT)]
        for qh, (re, im) in enumerate(dft8(column, -1)):
            q = ql + FOUR * qh
            c, s = twiddle[0, q], twiddle[1, q]
            pieces.append((re * c - im * s, re * s + im * c))
    return weighted(joined(pieces), w_forward)


def inverse(product, w_inverse, spread):
    pieces = []
    for q, (re, im) in zip(Q_ROWS, parted(product)):
        c, s = spread[0, q], spread[1, q]
        pieces.append((re * c - im * s, re * s + im * c))
    return weighted(joined(pieces), w_inverse)


def leave(back, product, twiddle):
    pieces = []
    for q, (re, im) in zip(Q_ROWS, parted(product)):
        c, s = twiddle[0, q], twiddle[1, q]
        pieces.append((re * c + im * s, im * c - re * s))
    for ql in range(FOUR):
        column = dft8(pieces[ql * EIGHT : (ql + 1) * EIGHT], 1)
        for jl in range(EIGHT):
            back[0, ql * EIGHT + jl] = column[jl][0]
            back[1, ql * EIGHT + jl] = column[jl][1]


def launch_kernel(start, w_forward, w_inverse, twiddle_table, spread_table, back, field, twiddle, spread):
    spread_rows(twiddle_table, twiddle)
    spread_rows(spread_table, spread)
    for jl in range(EIGHT):
        columns = []
        for jh in range(FOUR):
            j = EIGHT * jh + jl
            columns.append(tuple(jnp.broadcast_to(start[k, j : j + 1, :], (SUB, LANES)) for k in range(2)))
        enter(field, columns, jl)
    product = inverse(forward(field, w_forward, twiddle), w_inverse, spread)
    leave(back, product, twiddle)


def launch(start, consts):
    vmem = pl.BlockSpec(memory_space=pltpu.VMEM)
    return pl.pallas_call(
        launch_kernel,
        out_shape=[jax.ShapeDtypeStruct((2, ROWS, SUB, LANES), F32)] * 2,
        in_specs=[vmem] * 5,
        out_specs=[vmem] * 2,
        scratch_shapes=[pltpu.VMEM((2, ROWS, SUB, LANES), F32)] * 2,
        compiler_params=pltpu.CompilerParams(vmem_limit_bytes=8 * 1024 * 1024),
        cost_estimate=pl.CostEstimate(flops=1_000_000_000, bytes_accessed=1024 * 1024, transcendentals=0),
        name="launch",
    )(start, *consts[:4])


def march_kernel(own, levels, cells, launched, entered, w_forward, w_inverse, *refs):
    tables, (bins, section, totals, wide, field, back, energy, power), wide_tables = refs[:4], refs[4:12], refs[12:]
    for table, place in zip(tables, wide_tables):
        spread_rows(table, place)
    twiddle, spread, tilt, absorb = wide_tables
    sine, cosine = phase_polynomials()
    sections, batch, steps, heights = levels.shape
    halves = batch // SUB
    lane = lax.broadcasted_iota(jnp.int32, (SUB, LANES), 1)
    radial = lax.broadcasted_iota(jnp.int32, (SUB, LANES), 0)
    at_once = cells.shape[1] // 2

    def rotate(half, t, ground, jls):
        for jl in jls:
            column = []
            for ql in range(FOUR):
                c, s = unit(ql * jl, ROWS)
                column.append(
                    cmul_const((back[half, 0, ql * EIGHT + jl], back[half, 1, ql * EIGHT + jl]), (c, -s))
                )
            column = dft4(column, 1)
            moved = []
            for jh in range(FOUR):
                j = EIGHT * jh + jl
                phi = wide[j, pl.ds(half * SUB * steps + t, SUB, stride=steps), :] + tilt[j]
                u = phi * phi
                sin_poly, cos_poly = sine[-1], cosine[-1]
                for a, b in zip(sine[-2::-1], cosine[-2::-1]):
                    sin_poly = sin_poly * u + a
                    cos_poly = cos_poly * u + b
                small = sin_poly * phi
                double = small * cos_poly
                turned_c = 1.0 - double * double
                turned_s = double * (math.sqrt(2.0) - small * small)
                re, im = column[jh]
                if (j + 1) * LANES > 3 * H // 4:
                    loss = absorb[j]
                    re, im = re * loss, im * loss
                re, im = re * turned_c - im * turned_s, re * turned_s + im * turned_c
                if j < TERRAIN_ROWS:
                    open_air = lane + j * LANES >= ground
                    re, im = jnp.where(open_air, re, 0.0), jnp.where(open_air, im, 0.0)
                value = re * re + im * im
                high = value.astype(BF16).astype(F32)
                energy[half, j * SUB : (j + 1) * SUB, :LANES] = high
                energy[half, j * SUB : (j + 1) * SUB, LANES:] = value - high
                moved.append((re, im))
            enter(field.at[half], moved, jl)

    def binned(half, t):
        summed = jnp.dot(energy[half].astype(BF16), bins[...], preferred_element_type=F32)
        row = summed[:SUB]
        for j in range(1, ROWS):
            row = jnp.where(lane // (LANES // BIN) == j, summed[j * SUB : (j + 1) * SUB], row)
        power[pl.ds(pl.multiple_of(t * batch + half * SUB, SUB), SUB), :] = row

    def ground_of(half, t):
        row = cells[t // at_once, pl.ds(t % at_once, 1), :]
        my_lane = lane == section[0] * own + half * SUB + radial
        return jnp.sum(jnp.where(my_lane, row, 0), axis=1, keepdims=True)

    def turn_of(t, resting, moving):
        ground = ground_of(resting, t)
        pieces = [functools.partial(rotate, resting, t, ground, [jl]) for jl in range(EIGHT)]
        product = forward(field.at[moving], w_forward, twiddle)
        for piece in pieces[: EIGHT // 2]:
            piece()
        binned(moving, jnp.maximum(t - 1, 0) if resting == 0 else t)
        product = inverse(product, w_inverse, spread)
        for piece in pieces[EIGHT // 2 :]:
            piece()
        leave(back.at[moving], product, twiddle)

    def step(t, carry):
        for half in range(halves):
            turn_of(t, half, (half + 1) % halves)
        return carry

    power[...] = jnp.zeros_like(power)
    for half in range(halves):
        back[half] = launched[...]
        field[half] = entered[...]
    per_source = heights // LANES

    def widen(source, carry):
        for b in range(batch):
            for c in range(per_source):
                raw = levels[source, b, :, c * LANES : (c + 1) * LANES]
                wide[source * per_source + c, b * steps : (b + 1) * steps, :] = raw.astype(F32)
        return carry

    lax.fori_loop(0, sections, widen, 0)
    energy[...] = jnp.zeros_like(energy)
    lax.fori_loop(0, steps, step, 0)
    binned(halves - 1, steps - 1)

    lane = lax.broadcasted_iota(jnp.int32, (1, LANES), 1)
    fit = LANES // batch
    tile_rows = []
    for t in range(steps):
        row = cells[t // at_once, at_once + t % at_once, :].reshape(1, LANES)
        row = pltpu.roll(row, lax.rem(batch * (t % fit) - section[0] * own + LANES, LANES), 1)
        row = jnp.where(lane % batch < own, row, -1)
        if t % fit == 0:
            tile_rows.append(jnp.where(lane < batch, row, -1))
        else:
            tile_rows[-1] = jnp.where(lane // batch == t % fit, row, tile_rows[-1])
    tile_row = jnp.concatenate(tile_rows, axis=1)
    tiles, cell_count = totals.shape[0], tile_row.shape[1]
    hot = (lax.broadcasted_iota(jnp.int32, (tiles, cell_count), 0) == tile_row).astype(F32).astype(BF16)
    value = power[...]
    high = value.astype(BF16)
    rest = value - high.astype(F32)
    middle = rest.astype(BF16)
    low = (rest - middle.astype(F32)).astype(BF16)
    gain = jnp.dot(hot, high, preferred_element_type=F32)
    gain += jnp.dot(hot, middle, preferred_element_type=F32)
    gain += jnp.dot(hot, low, preferred_element_type=F32)
    totals[...] = gain


def march(section, received, cells, launched, consts, tiles, own):
    sections, batch, steps, heights = received.shape
    halves = batch // SUB
    vmem = pl.BlockSpec(memory_space=pltpu.VMEM)
    smem = pl.BlockSpec(memory_space=pltpu.SMEM)
    call = pl.pallas_call(
        functools.partial(march_kernel, own),
        out_shape=jax.ShapeDtypeStruct((tiles, BINS), F32),
        in_specs=[vmem] * 11 + [smem],
        out_specs=vmem,
        scratch_shapes=[
            pltpu.VMEM((ROWS, batch * steps, LANES), F32),
            pltpu.VMEM((halves, 2, ROWS, SUB, LANES), F32),
            pltpu.VMEM((halves, 2, ROWS, SUB, LANES), F32),
            pltpu.VMEM((halves, ROWS * SUB, 2 * LANES), F32),
            pltpu.VMEM((-(-steps * batch // LANES) * LANES, BINS), F32),
        ] + [pltpu.VMEM((*table.shape[:-1], SUB, LANES), F32) for table in consts[2:6]],
        compiler_params=pltpu.CompilerParams(vmem_limit_bytes=10 * 1024 * 1024 + 4 * H * batch * steps),
        cost_estimate=pl.CostEstimate(
            flops=steps * 1_600_000_000, bytes_accessed=4 * 1024 * 1024, transcendentals=0
        ),
        name="march",
    )
    return call(received, cells, *launched, *consts, section)


def gather_small(value):
    radial, sections = lax.axis_index("radial"), lax.axis_size("range")
    other = lax.ppermute(value, "radial", [(0, 1), (1, 0)])
    pair = jnp.stack([jnp.where(radial == 0, value, other), jnp.where(radial == 0, other, value)])
    section = lax.axis_index("range")
    held = jnp.zeros((sections, *pair.shape), pair.dtype)
    for d in range(sections):
        part = lax.ppermute(pair, "range", [(i, i ^ d) for i in range(sections)]) if d else pair
        held = lax.dynamic_update_index_in_dim(held, part, section ^ d, 0)
    return held


def local(refractivity, source, terrain, tile_map):
    sections = lax.axis_size("range")
    owners = sections * lax.axis_size("radial")
    radials, steps, heights = refractivity.shape
    own = radials // sections
    batch = -(-own // 16) * 16
    section = lax.axis_index("range").astype(jnp.int32).reshape(1)

    received = refractivity.reshape(sections, own, steps, heights)
    received = lax.all_to_all(received, "range", 0, 0, tiled=True)
    received = jnp.pad(received, ((0, 0), (0, batch - own), (0, 0), (0, 0)))
    everyone = gather_small(jnp.concatenate([terrain.T, tile_map.T]))
    cells = lax.dynamic_index_in_dim(everyone, lax.axis_index("radial"), 1, keepdims=False)
    consts = [jnp.asarray(v) for v in tables()]
    launched = launch(source.reshape(2, ROWS, LANES), consts)
    totals = march(section, received, cells, launched, consts, TILE_DEV * owners, own)

    everyone, totals = lax.optimization_barrier((everyone, totals))
    sent = lax.all_to_all(
        totals.reshape(owners, TILE_DEV, BINS), ("range", "radial"), 0, 0, tiled=True
    )
    ids = (lax.axis_index("range") * lax.axis_size("radial") + lax.axis_index("radial")) * TILE_DEV
    ids = ids + jnp.arange(TILE_DEV, dtype=jnp.int32)
    counts = jnp.sum((ids[:, None] == everyone[:, :, terrain.shape[1] :].reshape(1, -1)).astype(F32), axis=1)
    return jnp.sum(sent, axis=0) / counts[:, None]


def solution(mesh):
    in_specs = (
        P(("region", "radial"), None, "range"),
        P(None, "region"),
        P(("region", "radial"), "range"),
        P(("region", "radial"), "range"),
    )
    out_specs = P(("region", "range", "radial"), None)
    return jax.shard_map(local, mesh=mesh, in_specs=in_specs, out_specs=out_specs, check_vma=False)
```

```python
import functools
import math

import jax
import jax.numpy as jnp
import ml_dtypes
import numpy as np
from jax import lax
from jax.experimental import pallas as pl
from jax.experimental.pallas import tpu as pltpu
from jax.sharding import PartitionSpec as P

H = 4096
BIN = 32
LANES = 128
ROWS = H // LANES
FOUR = 4
EIGHT = 8
BINS = H // BIN
TILE_DEV = 16
TILT_SLOPE = 2.0
SPREAD_RATE = 0.5
ABSORB_RATE = 0.05
TERRAIN_ROWS = 4
SUB = 8

F32 = jnp.float32
BF16 = jnp.bfloat16


def split_np(table):
    high = table.astype(np.float32).astype(ml_dtypes.bfloat16)
    low = (table - high.astype(np.float64)).astype(ml_dtypes.bfloat16)
    return high, low


def tables():
    n = np.arange(LANES)
    angle = -2.0 * np.pi / LANES * (n[:, None] * n[None, :] % LANES)
    c, s = np.cos(angle), np.sin(angle)
    forward = np.block([[c, s], [-s, c]])
    inverse = np.block([[c, -s], [s, c]])
    weights = []
    for matrix in (forward, inverse):
        high, low = split_np(matrix)
        weights.append(np.stack([high, low]))
    q = np.arange(ROWS)
    angle = -2.0 * np.pi / H * (q[:, None] * n[None, :])
    twiddle = np.stack([np.cos(angle), np.sin(angle)]).astype(np.float32)
    frequency = q[:, None] + ROWS * n[None, :]
    signed = np.where(frequency >= H // 2, frequency - H, frequency)
    turning = -SPREAD_RATE * (2.0 * np.pi / H * signed) ** 2
    spread = (np.stack([np.cos(turning), np.sin(turning)]) / H).astype(np.float32)
    rel = np.arange(H).reshape(ROWS, LANES) / H
    tilt = (TILT_SLOPE * rel - 1.0).astype(np.float32)
    depth = np.maximum(rel - 0.75, 0.0) * 4.0
    absorb = np.exp(-ABSORB_RATE * depth * depth).astype(np.float32)
    bins = np.arange(BINS)
    order = np.zeros((BINS, BINS))
    order[bins % (LANES // BIN) * BIN + bins // (LANES // BIN), bins] = 1.0 / BIN
    return weights[0], weights[1], twiddle, spread, tilt, absorb, order.astype(ml_dtypes.bfloat16)


def phase_polynomials():
    root = 2.0 ** 0.25
    sin_scale = root * math.sqrt(2.0)
    cos_scale = 2.0 * math.sqrt(2.0) / sin_scale
    limit = 7.001
    nodes = 0.5 * limit * limit * (1.0 + np.cos(np.pi * (np.arange(64) + 0.5) / 64))
    phi = np.sqrt(nodes)
    sine = np.polynomial.chebyshev.Chebyshev.fit(
        nodes, sin_scale * np.sin(phi / 4) / phi, 4, domain=[0, limit * limit]
    ).convert(kind=np.polynomial.Polynomial)
    cosine = np.polynomial.chebyshev.Chebyshev.fit(
        nodes, cos_scale * np.cos(phi / 4), 4, domain=[0, limit * limit]
    ).convert(kind=np.polynomial.Polynomial)
    return [float(v) for v in sine.coef], [float(v) for v in cosine.coef]


def unit(number, extent):
    angle = -2.0 * math.pi * (number % extent) / extent
    return math.cos(angle), math.sin(angle)


def cmul_const(value, factor):
    re, im = value
    c, s = factor
    if abs(s) < 1e-12 and c > 0:
        return value
    if abs(c) < 1e-12:
        return (im, -re) if s < 0 else (-im, re)
    return re * c - im * s, re * s + im * c


def add(a, b):
    return a[0] + b[0], a[1] + b[1]


def sub(a, b):
    return a[0] - b[0], a[1] - b[1]


def add_turned(a, b, sign):
    if sign < 0:
        return a[0] + b[1], a[1] - b[0]
    return a[0] - b[1], a[1] + b[0]


def dft4(x, sign):
    a, b = add(x[0], x[2]), sub(x[0], x[2])
    c, d = add(x[1], x[3]), sub(x[1], x[3])
    return [add(a, c), add_turned(b, d, sign), sub(a, c), add_turned(b, d, -sign)]


def eighth(a, sign):
    h = math.sqrt(0.5)
    re, im = a
    if sign < 0:
        return (re + im) * h, (im - re) * h
    return (re - im) * h, (re + im) * h


def dft8(x, sign):
    even = dft4(x[0::2], sign)
    odd = dft4(x[1::2], sign)
    odd[1], odd[3] = eighth(odd[1], sign), eighth(odd[3], sign)
    low = [add(even[0], odd[0]), add(even[1], odd[1]), add_turned(even[2], odd[2], sign), add_turned(even[3], odd[3], sign)]
    high = [sub(even[0], odd[0]), sub(even[1], odd[1]), add_turned(even[2], odd[2], -sign), add_turned(even[3], odd[3], -sign)]
    return low + high


def split(value):
    high = value.astype(BF16)
    low = (value - high.astype(F32)).astype(BF16)
    return high, low


def enter(field, columns, jl):
    parts = dft4(columns, -1)
    for ql in range(FOUR):
        re, im = cmul_const(parts[ql], unit(ql * jl, ROWS))
        field[0, ql * EIGHT + jl] = re
        field[1, ql * EIGHT + jl] = im


def joined(pieces):
    re_high, re_low = split(jnp.concatenate([p[0] for p in pieces], axis=0))
    im_high, im_low = split(jnp.concatenate([p[1] for p in pieces], axis=0))
    return jnp.concatenate([re_high, im_high, re_low, im_low, re_high, im_high], axis=1)


def weighted(left, weights):
    return jnp.dot(left, jnp.concatenate([weights[0], weights[0], weights[1]]), preferred_element_type=F32)


def spread_rows(table, wide):
    for index in np.ndindex(table.shape[:-2]):
        for row in range(table.shape[-2]):
            place = (*index, row)
            wide[place] = jnp.broadcast_to(table[(*index, pl.ds(row, 1))], wide.shape[-2:])


def chain(ql, batch, field, back, w_forward, w_inverse, twiddle, spread):
    column = [(field[0, ql * EIGHT + jl], field[1, ql * EIGHT + jl]) for jl in range(EIGHT)]
    pieces = []
    for qh, (re, im) in enumerate(dft8(column, -1)):
        c, s = twiddle[0, ql + FOUR * qh], twiddle[1, ql + FOUR * qh]
        pieces.append((re * c - im * s, re * s + im * c))
    product = weighted(joined(pieces), w_forward)
    pieces = []
    for qh in range(EIGHT):
        re, im = (product[qh * batch : (qh + 1) * batch, k * LANES : (k + 1) * LANES] for k in range(2))
        c, s = spread[0, ql + FOUR * qh], spread[1, ql + FOUR * qh]
        pieces.append((re * c - im * s, re * s + im * c))
    product = weighted(joined(pieces), w_inverse)
    pieces = []
    for qh in range(EIGHT):
        re, im = (product[qh * batch : (qh + 1) * batch, k * LANES : (k + 1) * LANES] for k in range(2))
        c, s = twiddle[0, ql + FOUR * qh], twiddle[1, ql + FOUR * qh]
        pieces.append((re * c + im * s, im * c - re * s))
    for jl, (re, im) in enumerate(dft8(pieces, 1)):
        back[0, ql * EIGHT + jl] = re
        back[1, ql * EIGHT + jl] = im


def merged(a, b, distance, lane):
    a = a + pltpu.roll(a, LANES - distance, 1)
    b = b + pltpu.roll(b, distance, 1)
    return jnp.where(lane & distance == 0, a, b)


def launch_kernel(start, w_forward, w_inverse, twiddle_table, spread_table, back, field, twiddle, spread):
    spread_rows(twiddle_table, twiddle)
    spread_rows(spread_table, spread)
    for jl in range(EIGHT):
        columns = []
        for jh in range(FOUR):
            j = EIGHT * jh + jl
            columns.append(tuple(jnp.broadcast_to(start[k, j : j + 1, :], (SUB, LANES)) for k in range(2)))
        enter(field, columns, jl)
    for ql in range(FOUR):
        chain(ql, SUB, field, back, w_forward, w_inverse, twiddle, spread)


def launch(start, consts):
    vmem = pl.BlockSpec(memory_space=pltpu.VMEM)
    return pl.pallas_call(
        launch_kernel,
        out_shape=jax.ShapeDtypeStruct((2, ROWS, SUB, LANES), F32),
        in_specs=[vmem] * 5,
        out_specs=vmem,
        scratch_shapes=[pltpu.VMEM((2, ROWS, SUB, LANES), F32)] * 3,
        compiler_params=pltpu.CompilerParams(vmem_limit_bytes=8 * 1024 * 1024),
        cost_estimate=pl.CostEstimate(flops=1_000_000_000, bytes_accessed=1024 * 1024, transcendentals=0),
        name="launch",
    )(start, *consts[:4])


def march_kernel(own, levels, cells, launched, w_forward, w_inverse, *refs):
    tables, (order, section, totals, wide, field, back, power), wide_tables = refs[:4], refs[4:11], refs[11:]
    for table, place in zip(tables, wide_tables):
        spread_rows(table, place)
    twiddle, spread, tilt, absorb = wide_tables
    sine, cosine = phase_polynomials()
    sections, batch, steps, heights = levels.shape
    lane = lax.broadcasted_iota(jnp.int32, (batch, LANES), 1)
    radial = lax.broadcasted_iota(jnp.int32, (batch, LANES), 0)
    my_lane = lane == section[0] * own + radial
    at_once = cells.shape[1] // 2

    def rotate(t, ground, jl):
        column = []
        for ql in range(FOUR):
            c, s = unit(ql * jl, ROWS)
            column.append(cmul_const((back[0, ql * EIGHT + jl], back[1, ql * EIGHT + jl]), (c, -s)))
        column = dft4(column, 1)
        moved, energy = [], []
        for jh in range(FOUR):
            j = EIGHT * jh + jl
            phi = wide[j, pl.ds(t, batch, stride=steps), :] + tilt[j]
            u = phi * phi
            sin_poly, cos_poly = sine[-1], cosine[-1]
            for a, b in zip(sine[-2::-1], cosine[-2::-1]):
                sin_poly = sin_poly * u + a
                cos_poly = cos_poly * u + b
            small = sin_poly * phi
            double = small * cos_poly
            turned_c = 1.0 - double * double
            turned_s = double * (math.sqrt(2.0) - small * small)
            re, im = column[jh]
            if (j + 1) * LANES > 3 * H // 4:
                loss = absorb[j]
                re, im = re * loss, im * loss
            re, im = re * turned_c - im * turned_s, re * turned_s + im * turned_c
            if j < TERRAIN_ROWS:
                open_air = lane + j * LANES >= ground
                re, im = jnp.where(open_air, re, 0.0), jnp.where(open_air, im, 0.0)
            energy.append(re * re + im * im)
            moved.append((re, im))
        enter(field, moved, jl)
        return merged(
            merged(energy[0], energy[2], 16, lane), merged(energy[1], energy[3], 16, lane), 8, lane
        )

    def step(t, carry):
        row = cells[t // at_once, pl.ds(t % at_once, 1), :]
        ground = jnp.sum(jnp.where(my_lane, row, 0), axis=1, keepdims=True)
        sums = [rotate(t, ground, jl) for jl in range(EIGHT)]
        for distance in (4, 2, 1):
            sums = [merged(a, b, distance, lane) for a, b in zip(sums[: len(sums) // 2], sums[len(sums) // 2 :])]
        power[pl.ds(pl.multiple_of(t * batch, batch), batch), :] = sums[0]

        @pl.when(t + 1 < steps)
        def _():
            for ql in range(FOUR):
                chain(ql, batch, field, back, w_forward, w_inverse, twiddle, spread)

        return carry

    power[...] = jnp.zeros_like(power)
    for place in np.ndindex(back.shape[:2]):
        back[place] = jnp.concatenate([launched[place]] * (batch // SUB))
    per_source = heights // LANES

    def widen(source, carry):
        for b in range(batch):
            for c in range(per_source):
                raw = levels[source, b, :, c * LANES : (c + 1) * LANES]
                wide[source * per_source + c, b * steps : (b + 1) * steps, :] = raw.astype(F32)
        return carry

    lax.fori_loop(0, sections, widen, 0)
    lax.fori_loop(0, steps, step, 0)

    lane = lax.broadcasted_iota(jnp.int32, (1, LANES), 1)
    fit = LANES // batch
    tile_rows = []
    for t in range(steps):
        row = cells[t // at_once, at_once + t % at_once, :].reshape(1, LANES)
        row = pltpu.roll(row, lax.rem(batch * (t % fit) - section[0] * own + LANES, LANES), 1)
        row = jnp.where(lane % batch < own, row, -1)
        if t % fit == 0:
            tile_rows.append(jnp.where(lane < batch, row, -1))
        else:
            tile_rows[-1] = jnp.where(lane // batch == t % fit, row, tile_rows[-1])
    tile_row = jnp.concatenate(tile_rows, axis=1)
    tiles, cell_count = totals.shape[0], tile_row.shape[1]
    hot = (lax.broadcasted_iota(jnp.int32, (tiles, cell_count), 0) == tile_row).astype(F32).astype(BF16)
    value = power[...]
    gain = jnp.zeros((tiles, BINS), F32)
    for _ in range(3):
        part = value.astype(BF16)
        value = value - part.astype(F32)
        part = jnp.dot(part, order[...], preferred_element_type=F32).astype(BF16)
        gain += jnp.dot(hot, part, preferred_element_type=F32)
    totals[...] = gain


def march(section, received, cells, launched, consts, tiles, own):
    sections, batch, steps, heights = received.shape
    vmem = pl.BlockSpec(memory_space=pltpu.VMEM)
    smem = pl.BlockSpec(memory_space=pltpu.SMEM)
    call = pl.pallas_call(
        functools.partial(march_kernel, own),
        out_shape=jax.ShapeDtypeStruct((tiles, BINS), F32),
        in_specs=[vmem] * 10 + [smem],
        out_specs=vmem,
        scratch_shapes=[
            pltpu.VMEM((ROWS, batch * steps, LANES), F32),
            pltpu.VMEM((2, ROWS, batch, LANES), F32),
            pltpu.VMEM((2, ROWS, batch, LANES), F32),
            pltpu.VMEM((-(-steps * batch // LANES) * LANES, BINS), F32),
        ] + [pltpu.VMEM((*table.shape[:-1], batch, LANES), F32) for table in consts[2:6]],
        compiler_params=pltpu.CompilerParams(vmem_limit_bytes=10 * 1024 * 1024 + 4 * H * batch * steps),
        cost_estimate=pl.CostEstimate(
            flops=steps * 1_600_000_000, bytes_accessed=4 * 1024 * 1024, transcendentals=0
        ),
        name="march",
    )
    return call(received, cells, launched, *consts, section)


def gather_small(value):
    radial, sections = lax.axis_index("radial"), lax.axis_size("range")
    other = lax.ppermute(value, "radial", [(0, 1), (1, 0)])
    pair = jnp.stack([jnp.where(radial == 0, value, other), jnp.where(radial == 0, other, value)])
    section = lax.axis_index("range")
    held = jnp.zeros((sections, *pair.shape), pair.dtype)
    for d in range(sections):
        part = lax.ppermute(pair, "range", [(i, i ^ d) for i in range(sections)]) if d else pair
        held = lax.dynamic_update_index_in_dim(held, part, section ^ d, 0)
    return held


def local(refractivity, source, terrain, tile_map):
    sections = lax.axis_size("range")
    owners = sections * lax.axis_size("radial")
    radials, steps, heights = refractivity.shape
    own = radials // sections
    batch = -(-own // 16) * 16
    section = lax.axis_index("range").astype(jnp.int32).reshape(1)

    received = refractivity.reshape(sections, own, steps, heights)
    received = lax.all_to_all(received, "range", 0, 0, tiled=True)
    received = jnp.pad(received, ((0, 0), (0, batch - own), (0, 0), (0, 0)))
    everyone = gather_small(jnp.concatenate([terrain.T, tile_map.T]))
    cells = lax.dynamic_index_in_dim(everyone, lax.axis_index("radial"), 1, keepdims=False)
    consts = [jnp.asarray(v) for v in tables()]
    launched = launch(source.reshape(2, ROWS, LANES), consts)
    totals = march(section, received, cells, launched, consts, TILE_DEV * owners, own)

    everyone, totals = lax.optimization_barrier((everyone, totals))
    sent = lax.all_to_all(
        totals.reshape(owners, TILE_DEV, BINS), ("range", "radial"), 0, 0, tiled=True
    )
    ids = (lax.axis_index("range") * lax.axis_size("radial") + lax.axis_index("radial")) * TILE_DEV
    ids = ids + jnp.arange(TILE_DEV, dtype=jnp.int32)
    counts = jnp.sum((ids[:, None] == everyone[:, :, terrain.shape[1] :].reshape(1, -1)).astype(F32), axis=1)
    return jnp.sum(sent, axis=0) / counts[:, None]


def solution(mesh):
    in_specs = (
        P(("region", "radial"), None, "range"),
        P(None, "region"),
        P(("region", "radial"), "range"),
        P(("region", "radial"), "range"),
    )
    out_specs = P(("region", "range", "radial"), None)
    return jax.shard_map(local, mesh=mesh, in_specs=in_specs, out_specs=out_specs, check_vma=False)
```

```python
import functools
import math

import jax
import jax.numpy as jnp
import ml_dtypes
import numpy as np
from jax import lax
from jax.experimental import pallas as pl
from jax.experimental.pallas import tpu as pltpu
from jax.sharding import PartitionSpec as P

H = 4096
BIN = 32
LANES = 128
ROWS = H // LANES
FOUR = 4
EIGHT = 8
BINS = H // BIN
TILE_DEV = 16
TILT_SLOPE = 2.0
SPREAD_RATE = 0.5
ABSORB_RATE = 0.05
TERRAIN_ROWS = 4
SUB = 8

F32 = jnp.float32
BF16 = jnp.bfloat16


def split_np(table):
    high = table.astype(np.float32).astype(ml_dtypes.bfloat16)
    low = (table - high.astype(np.float64)).astype(ml_dtypes.bfloat16)
    return high, low


def tables():
    n = np.arange(LANES)
    angle = -2.0 * np.pi / LANES * (n[:, None] * n[None, :] % LANES)
    c, s = np.cos(angle), np.sin(angle)
    forward = np.block([[c, s], [-s, c]])
    inverse = np.block([[c, -s], [s, c]])
    weights = []
    for matrix in (forward, inverse):
        high, low = split_np(matrix)
        weights.append(np.stack([high, low]))
    q = np.arange(ROWS)
    angle = -2.0 * np.pi / H * (q[:, None] * n[None, :])
    twiddle = np.stack([np.cos(angle), np.sin(angle)]).astype(np.float32)
    frequency = q[:, None] + ROWS * n[None, :]
    signed = np.where(frequency >= H // 2, frequency - H, frequency)
    turning = -SPREAD_RATE * (2.0 * np.pi / H * signed) ** 2
    spread = (np.stack([np.cos(turning), np.sin(turning)]) / H).astype(np.float32)
    rel = np.arange(H).reshape(ROWS, LANES) / H
    tilt = (TILT_SLOPE * rel - 1.0).astype(np.float32)
    depth = np.maximum(rel - 0.75, 0.0) * 4.0
    absorb = np.exp(-ABSORB_RATE * depth * depth).astype(np.float32)
    bins = np.arange(BINS)
    order = np.zeros((BINS, BINS))
    order[bins % (LANES // BIN) * BIN + bins // (LANES // BIN), bins] = 1.0 / BIN
    return weights[0], weights[1], twiddle, spread, tilt, absorb, order.astype(ml_dtypes.bfloat16)


def phase_polynomials():
    root = 2.0 ** 0.25
    sin_scale = root * math.sqrt(2.0)
    cos_scale = 2.0 * math.sqrt(2.0) / sin_scale
    limit = 7.001
    nodes = 0.5 * limit * limit * (1.0 + np.cos(np.pi * (np.arange(64) + 0.5) / 64))
    phi = np.sqrt(nodes)
    sine = np.polynomial.chebyshev.Chebyshev.fit(
        nodes, sin_scale * np.sin(phi / 4) / phi, 4, domain=[0, limit * limit]
    ).convert(kind=np.polynomial.Polynomial)
    cosine = np.polynomial.chebyshev.Chebyshev.fit(
        nodes, cos_scale * np.cos(phi / 4), 4, domain=[0, limit * limit]
    ).convert(kind=np.polynomial.Polynomial)
    return [float(v) for v in sine.coef], [float(v) for v in cosine.coef]


def unit(number, extent):
    angle = -2.0 * math.pi * (number % extent) / extent
    return math.cos(angle), math.sin(angle)


def cmul_const(value, factor):
    re, im = value
    c, s = factor
    if abs(s) < 1e-12 and c > 0:
        return value
    if abs(c) < 1e-12:
        return (im, -re) if s < 0 else (-im, re)
    return re * c - im * s, re * s + im * c


def add(a, b):
    return a[0] + b[0], a[1] + b[1]


def sub(a, b):
    return a[0] - b[0], a[1] - b[1]


def add_turned(a, b, sign):
    if sign < 0:
        return a[0] + b[1], a[1] - b[0]
    return a[0] - b[1], a[1] + b[0]


def dft4(x, sign):
    a, b = add(x[0], x[2]), sub(x[0], x[2])
    c, d = add(x[1], x[3]), sub(x[1], x[3])
    return [add(a, c), add_turned(b, d, sign), sub(a, c), add_turned(b, d, -sign)]


def eighth(a, sign):
    h = math.sqrt(0.5)
    re, im = a
    if sign < 0:
        return (re + im) * h, (im - re) * h
    return (re - im) * h, (re + im) * h


def dft8(x, sign):
    even = dft4(x[0::2], sign)
    odd = dft4(x[1::2], sign)
    odd[1], odd[3] = eighth(odd[1], sign), eighth(odd[3], sign)
    low = [add(even[0], odd[0]), add(even[1], odd[1]), add_turned(even[2], odd[2], sign), add_turned(even[3], odd[3], sign)]
    high = [sub(even[0], odd[0]), sub(even[1], odd[1]), add_turned(even[2], odd[2], -sign), add_turned(even[3], odd[3], -sign)]
    return low + high


def split(value):
    high = value.astype(BF16)
    low = (value - high.astype(F32)).astype(BF16)
    return high, low


def enter(field, columns, jl):
    parts = dft4(columns, -1)
    for ql in range(FOUR):
        re, im = cmul_const(parts[ql], unit(ql * jl, ROWS))
        field[0, ql * EIGHT + jl] = re
        field[1, ql * EIGHT + jl] = im


def joined(pieces):
    re_high, re_low = split(jnp.concatenate([p[0] for p in pieces], axis=0))
    im_high, im_low = split(jnp.concatenate([p[1] for p in pieces], axis=0))
    return jnp.concatenate([re_high, im_high], axis=1), jnp.concatenate([re_low, im_low], axis=1)


def weighted(left, weights, between=()):
    high, low = left
    between = list(between) + [lambda: None] * 3
    total = None
    for part, weight in ((high, weights[0]), (low, weights[0]), (high, weights[1])):
        product = jnp.dot(part, weight, preferred_element_type=F32)
        between.pop(0)()
        total = product if total is None else total + product
    return total


def spread_rows(table, wide):
    for index in np.ndindex(table.shape[:-2]):
        for row in range(table.shape[-2]):
            place = (*index, row)
            wide[place] = jnp.broadcast_to(table[(*index, pl.ds(row, 1))], (SUB, LANES))


def parted(product):
    return [(product[i * SUB : (i + 1) * SUB, :LANES], product[i * SUB : (i + 1) * SUB, LANES:]) for i in range(ROWS)]


Q_ROWS = [ql + FOUR * qh for ql in range(FOUR) for qh in range(EIGHT)]


def forward(field, w_forward, twiddle, between=()):
    pieces = []
    for ql in range(FOUR):
        column = [(field[0, ql * EIGHT + jl], field[1, ql * EIGHT + jl]) for jl in range(EIGHT)]
        for qh, (re, im) in enumerate(dft8(column, -1)):
            q = ql + FOUR * qh
            c, s = twiddle[0, q], twiddle[1, q]
            pieces.append((re * c - im * s, re * s + im * c))
    return weighted(joined(pieces), w_forward, between)


def inverse(product, w_inverse, spread, between=()):
    pieces = []
    for q, (re, im) in zip(Q_ROWS, parted(product)):
        c, s = spread[0, q], spread[1, q]
        pieces.append((re * c - im * s, re * s + im * c))
    return weighted(joined(pieces), w_inverse, between)


def leave(back, product, twiddle):
    pieces = []
    for q, (re, im) in zip(Q_ROWS, parted(product)):
        c, s = twiddle[0, q], twiddle[1, q]
        pieces.append((re * c + im * s, im * c - re * s))
    for ql in range(FOUR):
        column = dft8(pieces[ql * EIGHT : (ql + 1) * EIGHT], 1)
        for jl in range(EIGHT):
            back[0, ql * EIGHT + jl] = column[jl][0]
            back[1, ql * EIGHT + jl] = column[jl][1]


def merged(a, b, distance, lane):
    a = a + pltpu.roll(a, LANES - distance, 1)
    b = b + pltpu.roll(b, distance, 1)
    return jnp.where(lane & distance == 0, a, b)


def launch_kernel(start, w_forward, w_inverse, twiddle_table, spread_table, back, field, twiddle, spread):
    spread_rows(twiddle_table, twiddle)
    spread_rows(spread_table, spread)
    for jl in range(EIGHT):
        columns = []
        for jh in range(FOUR):
            j = EIGHT * jh + jl
            columns.append(tuple(jnp.broadcast_to(start[k, j : j + 1, :], (SUB, LANES)) for k in range(2)))
        enter(field, columns, jl)
    product = inverse(forward(field, w_forward, twiddle), w_inverse, spread)
    leave(back, product, twiddle)


def launch(start, consts):
    vmem = pl.BlockSpec(memory_space=pltpu.VMEM)
    return pl.pallas_call(
        launch_kernel,
        out_shape=[jax.ShapeDtypeStruct((2, ROWS, SUB, LANES), F32)] * 2,
        in_specs=[vmem] * 5,
        out_specs=[vmem] * 2,
        scratch_shapes=[pltpu.VMEM((2, ROWS, SUB, LANES), F32)] * 2,
        compiler_params=pltpu.CompilerParams(vmem_limit_bytes=8 * 1024 * 1024),
        cost_estimate=pl.CostEstimate(flops=1_000_000_000, bytes_accessed=1024 * 1024, transcendentals=0),
        name="launch",
    )(start, *consts[:4])


def march_kernel(own, levels, cells, launched, entered, w_forward, w_inverse, *refs):
    tables, (order, section, totals, wide, field, back, power), wide_tables = refs[:4], refs[4:11], refs[11:]
    for table, place in zip(tables, wide_tables):
        spread_rows(table, place)
    twiddle, spread, tilt, absorb = wide_tables
    sine, cosine = phase_polynomials()
    sections, batch, steps, heights = levels.shape
    halves = batch // SUB
    lane = lax.broadcasted_iota(jnp.int32, (SUB, LANES), 1)
    radial = lax.broadcasted_iota(jnp.int32, (SUB, LANES), 0)
    at_once = cells.shape[1] // 2

    def rotate(half, t, ground, jl, sums):
        column = []
        for ql in range(FOUR):
            c, s = unit(ql * jl, ROWS)
            column.append(
                cmul_const((back[half, 0, ql * EIGHT + jl], back[half, 1, ql * EIGHT + jl]), (c, -s))
            )
        column = dft4(column, 1)
        moved, energy = [], []
        for jh in range(FOUR):
            j = EIGHT * jh + jl
            phi = wide[j, pl.ds(half * SUB * steps + t, SUB, stride=steps), :] + tilt[j]
            u = phi * phi
            sin_poly, cos_poly = sine[-1], cosine[-1]
            for a, b in zip(sine[-2::-1], cosine[-2::-1]):
                sin_poly = sin_poly * u + a
                cos_poly = cos_poly * u + b
            small = sin_poly * phi
            double = small * cos_poly
            turned_c = 1.0 - double * double
            turned_s = double * (math.sqrt(2.0) - small * small)
            re, im = column[jh]
            if (j + 1) * LANES > 3 * H // 4:
                loss = absorb[j]
                re, im = re * loss, im * loss
            re, im = re * turned_c - im * turned_s, re * turned_s + im * turned_c
            if j < TERRAIN_ROWS:
                open_air = lane + j * LANES >= ground
                re, im = jnp.where(open_air, re, 0.0), jnp.where(open_air, im, 0.0)
            energy.append(re * re + im * im)
            moved.append((re, im))
        enter(field.at[half], moved, jl)
        sums.append(merged(
            merged(energy[0], energy[2], 16, lane), merged(energy[1], energy[3], 16, lane), 8, lane
        ))

    def ground_of(half, t):
        row = cells[t // at_once, pl.ds(t % at_once, 1), :]
        my_lane = lane == section[0] * own + half * SUB + radial
        return jnp.sum(jnp.where(my_lane, row, 0), axis=1, keepdims=True)

    def turn_of(t, resting, moving):
        ground = ground_of(resting, t)
        sums = []
        pieces = [functools.partial(rotate, resting, t, ground, jl, sums) for jl in range(EIGHT)]
        product = forward(field.at[moving], w_forward, twiddle, pieces[:3])
        product = inverse(product, w_inverse, spread, pieces[3:6])
        for piece in pieces[6:]:
            piece()
        for distance in (4, 2, 1):
            sums = [merged(a, b, distance, lane) for a, b in zip(sums[: len(sums) // 2], sums[len(sums) // 2 :])]
        power[pl.ds(pl.multiple_of(t * batch + resting * SUB, SUB), SUB), :] = sums[0]
        leave(back.at[moving], product, twiddle)

    def step(t, carry):
        for half in range(halves):
            turn_of(t, half, (half + 1) % halves)
        return carry

    power[...] = jnp.zeros_like(power)
    for half in range(halves):
        back[half] = launched[...]
        field[half] = entered[...]
    per_source = heights // LANES

    def widen(source, carry):
        for b in range(batch):
            for c in range(per_source):
                raw = levels[source, b, :, c * LANES : (c + 1) * LANES]
                wide[source * per_source + c, b * steps : (b + 1) * steps, :] = raw.astype(F32)
        return carry

    lax.fori_loop(0, sections, widen, 0)
    lax.fori_loop(0, steps, step, 0)

    lane = lax.broadcasted_iota(jnp.int32, (1, LANES), 1)
    fit = LANES // batch
    tile_rows = []
    for t in range(steps):
        row = cells[t // at_once, at_once + t % at_once, :].reshape(1, LANES)
        row = pltpu.roll(row, lax.rem(batch * (t % fit) - section[0] * own + LANES, LANES), 1)
        row = jnp.where(lane % batch < own, row, -1)
        if t % fit == 0:
            tile_rows.append(jnp.where(lane < batch, row, -1))
        else:
            tile_rows[-1] = jnp.where(lane // batch == t % fit, row, tile_rows[-1])
    tile_row = jnp.concatenate(tile_rows, axis=1)
    tiles, cell_count = totals.shape[0], tile_row.shape[1]
    hot = (lax.broadcasted_iota(jnp.int32, (tiles, cell_count), 0) == tile_row).astype(F32).astype(BF16)
    value = power[...]
    gain = jnp.zeros((tiles, BINS), F32)
    for _ in range(3):
        part = value.astype(BF16)
        value = value - part.astype(F32)
        part = jnp.dot(part, order[...], preferred_element_type=F32).astype(BF16)
        gain += jnp.dot(hot, part, preferred_element_type=F32)
    totals[...] = gain


def march(section, received, cells, launched, consts, tiles, own):
    sections, batch, steps, heights = received.shape
    halves = batch // SUB
    vmem = pl.BlockSpec(memory_space=pltpu.VMEM)
    smem = pl.BlockSpec(memory_space=pltpu.SMEM)
    call = pl.pallas_call(
        functools.partial(march_kernel, own),
        out_shape=jax.ShapeDtypeStruct((tiles, BINS), F32),
        in_specs=[vmem] * 11 + [smem],
        out_specs=vmem,
        scratch_shapes=[
            pltpu.VMEM((ROWS, batch * steps, LANES), F32),
            pltpu.VMEM((halves, 2, ROWS, SUB, LANES), F32),
            pltpu.VMEM((halves, 2, ROWS, SUB, LANES), F32),
            pltpu.VMEM((-(-steps * batch // LANES) * LANES, BINS), F32),
        ] + [pltpu.VMEM((*table.shape[:-1], SUB, LANES), F32) for table in consts[2:6]],
        compiler_params=pltpu.CompilerParams(vmem_limit_bytes=10 * 1024 * 1024 + 4 * H * batch * steps),
        cost_estimate=pl.CostEstimate(
            flops=steps * 1_600_000_000, bytes_accessed=4 * 1024 * 1024, transcendentals=0
        ),
        name="march",
    )
    return call(received, cells, *launched, *consts, section)


def gather_small(value):
    radial, sections = lax.axis_index("radial"), lax.axis_size("range")
    other = lax.ppermute(value, "radial", [(0, 1), (1, 0)])
    pair = jnp.stack([jnp.where(radial == 0, value, other), jnp.where(radial == 0, other, value)])
    section = lax.axis_index("range")
    next_pair = lax.ppermute(pair, "range", [(i, i ^ 1) for i in range(sections)])
    even = section % 2 == 0
    both = jnp.stack([jnp.where(even, pair, next_pair), jnp.where(even, next_pair, pair)])
    held = jnp.zeros((sections, *pair.shape), pair.dtype)
    for d in range(0, sections, 2):
        part = lax.ppermute(both, "range", [(i, i ^ d) for i in range(sections)]) if d else both
        held = lax.dynamic_update_slice_in_dim(held, part, (section ^ d) // 2 * 2, 0)
    return held


def local(refractivity, source, terrain, tile_map):
    sections = lax.axis_size("range")
    owners = sections * lax.axis_size("radial")
    radials, steps, heights = refractivity.shape
    own = radials // sections
    batch = -(-own // 16) * 16
    section = lax.axis_index("range").astype(jnp.int32).reshape(1)

    received = refractivity.reshape(sections, own, steps, heights)
    received = lax.all_to_all(received, "range", 0, 0, tiled=True)
    received = jnp.pad(received, ((0, 0), (0, batch - own), (0, 0), (0, 0)))
    everyone = gather_small(jnp.concatenate([terrain.T, tile_map.T]))
    cells = lax.dynamic_index_in_dim(everyone, lax.axis_index("radial"), 1, keepdims=False)
    consts = [jnp.asarray(v) for v in tables()]
    launched = launch(source.reshape(2, ROWS, LANES), consts)
    totals = march(section, received, cells, launched, consts, TILE_DEV * owners, own)

    everyone, totals = lax.optimization_barrier((everyone, totals))
    sent = lax.all_to_all(
        totals.reshape(owners, TILE_DEV, BINS), ("range", "radial"), 0, 0, tiled=True
    )
    ids = (lax.axis_index("range") * lax.axis_size("radial") + lax.axis_index("radial")) * TILE_DEV
    ids = ids + jnp.arange(TILE_DEV, dtype=jnp.int32)
    counts = jnp.sum((ids[:, None] == everyone[:, :, terrain.shape[1] :].reshape(1, -1)).astype(F32), axis=1)
    return jnp.sum(sent, axis=0) / counts[:, None]


def solution(mesh):
    in_specs = (
        P(("region", "radial"), None, "range"),
        P(None, "region"),
        P(("region", "radial"), "range"),
        P(("region", "radial"), "range"),
    )
    out_specs = P(("region", "range", "radial"), None)
    return jax.shard_map(local, mesh=mesh, in_specs=in_specs, out_specs=out_specs, check_vma=False)
```

```python
import functools
import math

import jax
import jax.numpy as jnp
import ml_dtypes
import numpy as np
from jax import lax
from jax.experimental import pallas as pl
from jax.experimental.pallas import tpu as pltpu
from jax.sharding import PartitionSpec as P

H = 4096
BIN = 32
LANES = 128
ROWS = H // LANES
FOUR = 4
EIGHT = 8
BINS = H // BIN
TILE_DEV = 16
TILT_SLOPE = 2.0
SPREAD_RATE = 0.5
ABSORB_RATE = 0.05
TERRAIN_ROWS = 4
SUB = 8
EARLY_SHARE = 0.6875

F32 = jnp.float32
BF16 = jnp.bfloat16


def split_np(table):
    high = table.astype(np.float32).astype(ml_dtypes.bfloat16)
    low = (table - high.astype(np.float64)).astype(ml_dtypes.bfloat16)
    return high, low


def tables():
    n = np.arange(LANES)
    angle = -2.0 * np.pi / LANES * (n[:, None] * n[None, :] % LANES)
    c, s = np.cos(angle), np.sin(angle)
    forward = np.block([[c, s], [-s, c]])
    inverse = np.block([[c, -s], [s, c]])
    weights = []
    for matrix in (forward, inverse):
        high, low = split_np(matrix)
        weights.append(np.stack([high, low]))
    q = np.arange(ROWS)
    angle = -2.0 * np.pi / H * (q[:, None] * n[None, :])
    twiddle = np.stack([np.cos(angle), np.sin(angle)]).astype(np.float32)
    frequency = q[:, None] + ROWS * n[None, :]
    signed = np.where(frequency >= H // 2, frequency - H, frequency)
    turning = -SPREAD_RATE * (2.0 * np.pi / H * signed) ** 2
    spread = (np.stack([np.cos(turning), np.sin(turning)]) / H).astype(np.float32)
    rel = np.arange(H).reshape(ROWS, LANES) / H
    tilt = (TILT_SLOPE * rel - 1.0).astype(np.float32)
    depth = np.maximum(rel - 0.75, 0.0) * 4.0
    absorb = np.exp(-ABSORB_RATE * depth * depth).astype(np.float32)
    bins = np.zeros((2 * LANES, BINS), np.float64)
    for lane in range(2 * LANES):
        bins[lane, (lane % LANES) // BIN :: LANES // BIN] = 1.0 / BIN
    return weights[0], weights[1], twiddle, spread, tilt, absorb, bins.astype(ml_dtypes.bfloat16)


def phase_polynomials():
    root = 2.0 ** 0.25
    sin_scale = root * math.sqrt(2.0)
    cos_scale = 2.0 * math.sqrt(2.0) / sin_scale
    limit = 7.001
    nodes = 0.5 * limit * limit * (1.0 + np.cos(np.pi * (np.arange(64) + 0.5) / 64))
    phi = np.sqrt(nodes)
    sine = np.polynomial.chebyshev.Chebyshev.fit(
        nodes, sin_scale * np.sin(phi / 4) / phi, 4, domain=[0, limit * limit]
    ).convert(kind=np.polynomial.Polynomial)
    cosine = np.polynomial.chebyshev.Chebyshev.fit(
        nodes, cos_scale * np.cos(phi / 4), 4, domain=[0, limit * limit]
    ).convert(kind=np.polynomial.Polynomial)
    return [float(v) for v in sine.coef], [float(v) for v in cosine.coef]


def unit(number, extent):
    angle = -2.0 * math.pi * (number % extent) / extent
    return math.cos(angle), math.sin(angle)


def cmul_const(value, factor):
    re, im = value
    c, s = factor
    if abs(s) < 1e-12 and c > 0:
        return value
    if abs(c) < 1e-12:
        return (im, -re) if s < 0 else (-im, re)
    return re * c - im * s, re * s + im * c


def add(a, b):
    return a[0] + b[0], a[1] + b[1]


def sub(a, b):
    return a[0] - b[0], a[1] - b[1]


def add_turned(a, b, sign):
    if sign < 0:
        return a[0] + b[1], a[1] - b[0]
    return a[0] - b[1], a[1] + b[0]


def dft4(x, sign):
    a, b = add(x[0], x[2]), sub(x[0], x[2])
    c, d = add(x[1], x[3]), sub(x[1], x[3])
    return [add(a, c), add_turned(b, d, sign), sub(a, c), add_turned(b, d, -sign)]


def eighth(a, sign):
    h = math.sqrt(0.5)
    re, im = a
    if sign < 0:
        return (re + im) * h, (im - re) * h
    return (re - im) * h, (re + im) * h


def dft8(x, sign):
    even = dft4(x[0::2], sign)
    odd = dft4(x[1::2], sign)
    odd[1], odd[3] = eighth(odd[1], sign), eighth(odd[3], sign)
    low = [add(even[0], odd[0]), add(even[1], odd[1]), add_turned(even[2], odd[2], sign), add_turned(even[3], odd[3], sign)]
    high = [sub(even[0], odd[0]), sub(even[1], odd[1]), add_turned(even[2], odd[2], -sign), add_turned(even[3], odd[3], -sign)]
    return low + high


def split(value):
    high = value.astype(BF16)
    low = (value - high.astype(F32)).astype(BF16)
    return high, low


def enter(field, columns, jl):
    parts = dft4(columns, -1)
    for ql in range(FOUR):
        re, im = cmul_const(parts[ql], unit(ql * jl, ROWS))
        field[0, ql * EIGHT + jl] = re
        field[1, ql * EIGHT + jl] = im


def joined(pieces):
    re_high, re_low = split(jnp.concatenate([p[0] for p in pieces], axis=0))
    im_high, im_low = split(jnp.concatenate([p[1] for p in pieces], axis=0))
    return jnp.concatenate([re_high, im_high], axis=1), jnp.concatenate([re_low, im_low], axis=1)


def weighted(left, weights, between=()):
    high, low = left
    between = list(between) + [lambda: None] * 3
    total = None
    for part, weight in ((high, weights[0]), (low, weights[0]), (high, weights[1])):
        product = jnp.dot(part, weight, preferred_element_type=F32)
        between.pop(0)()
        total = product if total is None else total + product
    return total


def spread_rows(table, wide):
    for index in np.ndindex(table.shape[:-2]):
        for row in range(table.shape[-2]):
            place = (*index, row)
            wide[place] = jnp.broadcast_to(table[(*index, pl.ds(row, 1))], (SUB, LANES))


def parted(product):
    return [(product[i * SUB : (i + 1) * SUB, :LANES], product[i * SUB : (i + 1) * SUB, LANES:]) for i in range(ROWS)]


Q_ROWS = [ql + FOUR * qh for ql in range(FOUR) for qh in range(EIGHT)]


def forward(field, w_forward, twiddle, between=()):
    pieces = []
    for ql in range(FOUR):
        column = [(field[0, ql * EIGHT + jl], field[1, ql * EIGHT + jl]) for jl in range(EIGHT)]
        for qh, (re, im) in enumerate(dft8(column, -1)):
            q = ql + FOUR * qh
            c, s = twiddle[0, q], twiddle[1, q]
            pieces.append((re * c - im * s, re * s + im * c))
    return weighted(joined(pieces), w_forward, between)


def inverse(product, w_inverse, spread, between=()):
    pieces = []
    for q, (re, im) in zip(Q_ROWS, parted(product)):
        c, s = spread[0, q], spread[1, q]
        pieces.append((re * c - im * s, re * s + im * c))
    return weighted(joined(pieces), w_inverse, between)


def leave(back, product, twiddle):
    pieces = []
    for q, (re, im) in zip(Q_ROWS, parted(product)):
        c, s = twiddle[0, q], twiddle[1, q]
        pieces.append((re * c + im * s, im * c - re * s))
    for ql in range(FOUR):
        column = dft8(pieces[ql * EIGHT : (ql + 1) * EIGHT], 1)
        for jl in range(EIGHT):
            back[0, ql * EIGHT + jl] = column[jl][0]
            back[1, ql * EIGHT + jl] = column[jl][1]


def launch_kernel(start, w_forward, w_inverse, twiddle_table, spread_table, back, field, twiddle, spread):
    spread_rows(twiddle_table, twiddle)
    spread_rows(spread_table, spread)
    for jl in range(EIGHT):
        columns = []
        for jh in range(FOUR):
            j = EIGHT * jh + jl
            columns.append(tuple(jnp.broadcast_to(start[k, j : j + 1, :], (SUB, LANES)) for k in range(2)))
        enter(field, columns, jl)
    product = inverse(forward(field, w_forward, twiddle), w_inverse, spread)
    leave(back, product, twiddle)


def launch(start, consts):
    vmem = pl.BlockSpec(memory_space=pltpu.VMEM)
    return pl.pallas_call(
        launch_kernel,
        out_shape=[jax.ShapeDtypeStruct((2, ROWS, SUB, LANES), F32)] * 2,
        in_specs=[vmem] * 5,
        out_specs=[vmem] * 2,
        scratch_shapes=[pltpu.VMEM((2, ROWS, SUB, LANES), F32)] * 2,
        compiler_params=pltpu.CompilerParams(vmem_limit_bytes=8 * 1024 * 1024),
        cost_estimate=pl.CostEstimate(flops=1_000_000_000, bytes_accessed=1024 * 1024, transcendentals=0),
        name="launch",
    )(start, *consts[:4])


def march_kernel(begin, steps, own, last, levels, cells, launched, entered, totals_in, w_forward, w_inverse, *refs):
    tables, (bins, section, totals), refs = refs[:4], refs[4:7], refs[7:]
    if not last:
        (left_back, left_field), refs = refs[:2], refs[2:]
    (field, back, energy, power), wide_tables = refs[:4], refs[4:]
    for table, place in zip(tables, wide_tables):
        spread_rows(table, place)
    twiddle, spread, tilt, absorb = wide_tables
    sine, cosine = phase_polynomials()
    heights = levels.shape[2]
    batch = levels.shape[1] // steps
    halves = batch // SUB
    lane = lax.broadcasted_iota(jnp.int32, (SUB, LANES), 1)
    radial = lax.broadcasted_iota(jnp.int32, (SUB, LANES), 0)
    at_once = cells.shape[1] // 2

    def rotate(half, t, ground, jls):
        for jl in jls:
            column = []
            for ql in range(FOUR):
                c, s = unit(ql * jl, ROWS)
                column.append(
                    cmul_const((back[half, 0, ql * EIGHT + jl], back[half, 1, ql * EIGHT + jl]), (c, -s))
                )
            column = dft4(column, 1)
            moved = []
            for jh in range(FOUR):
                j = EIGHT * jh + jl
                place = j * LANES
                raw = levels[
                    place // heights, pl.ds(pl.multiple_of(t * batch, batch), batch),
                    place % heights : place % heights + LANES,
                ]
                phi = raw.astype(F32)[half * SUB : (half + 1) * SUB] + tilt[j]
                u = phi * phi
                sin_poly, cos_poly = sine[-1], cosine[-1]
                for a, b in zip(sine[-2::-1], cosine[-2::-1]):
                    sin_poly = sin_poly * u + a
                    cos_poly = cos_poly * u + b
                small = sin_poly * phi
                double = small * cos_poly
                turned_c = 1.0 - double * double
                turned_s = double * (math.sqrt(2.0) - small * small)
                re, im = column[jh]
                if (j + 1) * LANES > 3 * H // 4:
                    loss = absorb[j]
                    re, im = re * loss, im * loss
                re, im = re * turned_c - im * turned_s, re * turned_s + im * turned_c
                if j < TERRAIN_ROWS:
                    open_air = lane + j * LANES >= ground
                    re, im = jnp.where(open_air, re, 0.0), jnp.where(open_air, im, 0.0)
                value = re * re + im * im
                high = value.astype(BF16).astype(F32)
                energy[half, j * SUB : (j + 1) * SUB, :LANES] = high
                energy[half, j * SUB : (j + 1) * SUB, LANES:] = value - high
                moved.append((re, im))
            enter(field.at[half], moved, jl)

    def binned(half, t):
        summed = jnp.dot(energy[half].astype(BF16), bins[...], preferred_element_type=F32)
        row = summed[:SUB]
        for j in range(1, ROWS):
            row = jnp.where(lane // (LANES // BIN) == j, summed[j * SUB : (j + 1) * SUB], row)
        power[pl.ds(pl.multiple_of(t * batch + half * SUB, SUB), SUB), :] = row

    def ground_of(half, t):
        row = cells[(begin + t) // at_once, pl.ds((begin + t) % at_once, 1), :]
        my_lane = lane == section[0] * own + half * SUB + radial
        return jnp.sum(jnp.where(my_lane, row, 0), axis=1, keepdims=True)

    def turn_of(t, resting, moving):
        ground = ground_of(resting, t)
        pieces = [functools.partial(rotate, resting, t, ground, [jl]) for jl in range(EIGHT)]
        product = forward(field.at[moving], w_forward, twiddle, pieces[:3])
        binned(moving, jnp.maximum(t - 1, 0) if resting == 0 else t)
        product = inverse(product, w_inverse, spread, pieces[3:6])
        for piece in pieces[6:]:
            piece()
        leave(back.at[moving], product, twiddle)

    def step(t, carry):
        for half in range(halves):
            turn_of(t, half, (half + 1) % halves)
        return carry

    power[...] = jnp.zeros_like(power)
    back[0] = launched[...]
    for half in range(1, halves):
        field[half] = entered[half - 1]
    energy[...] = jnp.zeros_like(energy)
    lax.fori_loop(0, steps, step, 0)
    binned(halves - 1, steps - 1)
    if not last:
        left_back[...] = back[0]
        for half in range(1, halves):
            left_field[half - 1] = field[half]

    lane = lax.broadcasted_iota(jnp.int32, (1, LANES), 1)
    fit = LANES // batch
    tile_rows = []
    for t in range(steps):
        row = cells[(begin + t) // at_once, at_once + (begin + t) % at_once, :].reshape(1, LANES)
        row = pltpu.roll(row, lax.rem(batch * (t % fit) - section[0] * own + LANES, LANES), 1)
        row = jnp.where(lane % batch < own, row, -1)
        if t % fit == 0:
            tile_rows.append(jnp.where(lane < batch, row, -1))
        else:
            tile_rows[-1] = jnp.where(lane // batch == t % fit, row, tile_rows[-1])
    tile_row = jnp.concatenate(tile_rows, axis=1)
    tiles, cell_count = totals.shape[0], tile_row.shape[1]
    hot = (lax.broadcasted_iota(jnp.int32, (tiles, cell_count), 0) == tile_row).astype(F32).astype(BF16)
    value = power[...]
    high = value.astype(BF16)
    rest = value - high.astype(F32)
    middle = rest.astype(BF16)
    low = (rest - middle.astype(F32)).astype(BF16)
    gain = jnp.dot(hot, high, preferred_element_type=F32)
    gain += jnp.dot(hot, middle, preferred_element_type=F32)
    gain += jnp.dot(hot, low, preferred_element_type=F32)
    totals[...] = totals_in[...] + gain


def march(section, begin, steps, received, cells, state, totals, consts, own, last):
    batch = received.shape[1] // steps
    halves = batch // SUB
    vmem = pl.BlockSpec(memory_space=pltpu.VMEM)
    smem = pl.BlockSpec(memory_space=pltpu.SMEM)
    outputs = [jax.ShapeDtypeStruct(totals.shape, F32)]
    if not last:
        outputs += [jax.ShapeDtypeStruct(part.shape, F32) for part in state]
    call = pl.pallas_call(
        functools.partial(march_kernel, begin, steps, own, last),
        out_shape=outputs,
        in_specs=[vmem] * 12 + [smem],
        out_specs=[vmem] * len(outputs),
        scratch_shapes=[
            pltpu.VMEM((halves, 2, ROWS, SUB, LANES), F32),
            pltpu.VMEM((halves, 2, ROWS, SUB, LANES), F32),
            pltpu.VMEM((halves, ROWS * SUB, 2 * LANES), F32),
            pltpu.VMEM((-(-steps * batch // LANES) * LANES, BINS), F32),
        ] + [pltpu.VMEM((*table.shape[:-1], SUB, LANES), F32) for table in consts[2:6]],
        compiler_params=pltpu.CompilerParams(vmem_limit_bytes=12 * 1024 * 1024),
        cost_estimate=pl.CostEstimate(
            flops=steps * 1_600_000_000, bytes_accessed=4 * 1024 * 1024, transcendentals=0
        ),
        input_output_aliases={4: 0} if last else {2: 1, 3: 2, 4: 0},
        name="march",
    )
    return call(received, cells, *state, totals, *consts, section)


def turn_steps(block, rows, begin, end, out):
    own, steps, heights = block.shape
    batch = out.shape[0] // (end - begin)
    for c in range(heights // LANES):
        column = slice(c * LANES, (c + 1) * LANES)
        for b in range(own):
            rows[c, b * steps : (b + 1) * steps, :] = block[b, :, column].astype(F32)
        for t in range(begin, end):
            taken = rows[c, pl.ds(t, own, stride=steps), :].astype(BF16)
            if own < batch:
                taken = jnp.pad(taken, ((0, batch - own), (0, 0)))
            out[(t - begin) * batch : (t - begin + 1) * batch, column] = taken


def fill_slabs(begin, end, own, batch, owners, levels, slabs, blocks, turned, rows, sems):
    arrive = [
        pltpu.make_async_copy(levels.at[pl.ds(owner * own, own)], blocks.at[i], sems.at[0, i])
        for i, owner in enumerate(owners)
    ]
    leave = [pltpu.make_async_copy(turned.at[i], slab, sems.at[1, i]) for i, slab in enumerate(slabs)]
    for copy in arrive:
        copy.start()
    for i in range(len(slabs)):
        arrive[i].wait()
        turn_steps(blocks.at[i], rows, begin, end, turned.at[i])
        leave[i].start()
    for copy in leave:
        copy.wait()


def slab_scratch(number, own, steps, heights, count):
    return [
        pltpu.VMEM((number, own, steps, heights), BF16),
        pltpu.VMEM((number, count, heights), BF16),
        pltpu.VMEM((heights // LANES, own * steps, LANES), F32),
        pltpu.SemaphoreType.DMA((2, number)),
    ]


def deal(levels, begin, end, sections, own, batch):
    steps, heights = levels.shape[1:]
    count = (end - begin) * batch
    anywhere = pl.BlockSpec(memory_space=pl.ANY)

    def kernel(levels, out, *scratch):
        places = [out.at[i] for i in range(sections)]
        fill_slabs(begin, end, own, batch, range(sections), levels, places, *scratch)

    return pl.pallas_call(
        kernel,
        out_shape=jax.ShapeDtypeStruct((sections, count, heights), BF16),
        in_specs=[anywhere],
        out_specs=anywhere,
        scratch_shapes=slab_scratch(sections, own, steps, heights, count),
        compiler_params=pltpu.CompilerParams(vmem_limit_bytes=58 * 1024 * 1024),
        cost_estimate=pl.CostEstimate(flops=1_000_000_000, bytes_accessed=4 * 1024 * 1024, transcendentals=0),
        name="deal",
    )(levels)


def gather_small(value):
    radial, sections = lax.axis_index("radial"), lax.axis_size("range")
    other = lax.ppermute(value, "radial", [(0, 1), (1, 0)])
    pair = jnp.stack([jnp.where(radial == 0, value, other), jnp.where(radial == 0, other, value)])
    section = lax.axis_index("range")
    next_pair = lax.ppermute(pair, "range", [(i, i ^ 1) for i in range(sections)])
    even = section % 2 == 0
    both = jnp.stack([jnp.where(even, pair, next_pair), jnp.where(even, next_pair, pair)])
    held = jnp.zeros((sections, *pair.shape), pair.dtype)
    for d in range(0, sections, 2):
        part = lax.ppermute(both, "range", [(i, i ^ d) for i in range(sections)]) if d else both
        held = lax.dynamic_update_slice_in_dim(held, part, (section ^ d) // 2 * 2, 0)
    return held


def local(refractivity, source, terrain, tile_map):
    sections = lax.axis_size("range")
    owners = sections * lax.axis_size("radial")
    radials, steps, heights = refractivity.shape
    own = radials // sections
    batch = -(-own // 16) * 16
    section = lax.axis_index("range").astype(jnp.int32).reshape(1)

    middle = round(EARLY_SHARE * steps)
    dealt = deal(refractivity, 0, middle, sections, own, batch)
    refractivity, dealt = lax.optimization_barrier((refractivity, dealt))
    early = lax.all_to_all(dealt, "range", 0, 0, tiled=True)
    late = lax.all_to_all(deal(refractivity, middle, steps, sections, own, batch), "range", 0, 0, tiled=True)
    everyone = gather_small(jnp.concatenate([terrain.T, tile_map.T]))
    cells = lax.dynamic_index_in_dim(everyone, lax.axis_index("radial"), 1, keepdims=False)
    consts = [jnp.asarray(v) for v in tables()]
    launched, entered = launch(source.reshape(2, ROWS, LANES), consts)
    state = (launched, jnp.stack([entered] * (batch // SUB - 1)))
    totals = jnp.zeros((TILE_DEV * owners, BINS), F32)
    totals, *state = march(section, 0, middle, early, cells, state, totals, consts, own, False)
    (totals,) = march(section, middle, steps - middle, late, cells, state, totals, consts, own, True)

    everyone, totals = lax.optimization_barrier((everyone, totals))
    sent = lax.all_to_all(
        totals.reshape(owners, TILE_DEV, BINS), ("range", "radial"), 0, 0, tiled=True
    )
    ids = (lax.axis_index("range") * lax.axis_size("radial") + lax.axis_index("radial")) * TILE_DEV
    ids = ids + jnp.arange(TILE_DEV, dtype=jnp.int32)
    counts = jnp.sum((ids[:, None] == everyone[:, :, terrain.shape[1] :].reshape(1, -1)).astype(F32), axis=1)
    return jnp.sum(sent, axis=0) / counts[:, None]


def solution(mesh):
    in_specs = (
        P(("region", "radial"), None, "range"),
        P(None, "region"),
        P(("region", "radial"), "range"),
        P(("region", "radial"), "range"),
    )
    out_specs = P(("region", "range", "radial"), None)
    return jax.shard_map(local, mesh=mesh, in_specs=in_specs, out_specs=out_specs, check_vma=False)
```

```python
import functools
import math

import jax
import jax.numpy as jnp
import ml_dtypes
import numpy as np
from jax import lax
from jax.experimental import pallas as pl
from jax.experimental.pallas import tpu as pltpu
from jax.sharding import PartitionSpec as P

H = 4096
BIN = 32
LANES = 128
ROWS = H // LANES
FOUR = 4
EIGHT = 8
BINS = H // BIN
TILE_DEV = 16
TILT_SLOPE = 2.0
SPREAD_RATE = 0.5
ABSORB_RATE = 0.05
TERRAIN_ROWS = 4
SUB = 8
EARLY_SHARE = 0.6875

F32 = jnp.float32
BF16 = jnp.bfloat16


def split_np(table):
    high = table.astype(np.float32).astype(ml_dtypes.bfloat16)
    low = (table - high.astype(np.float64)).astype(ml_dtypes.bfloat16)
    return high, low


def tables():
    n = np.arange(LANES)
    angle = -2.0 * np.pi / LANES * (n[:, None] * n[None, :] % LANES)
    c, s = np.cos(angle), np.sin(angle)
    forward = np.block([[c, s], [-s, c]])
    inverse = np.block([[c, -s], [s, c]])
    weights = []
    for matrix in (forward, inverse):
        high, low = split_np(matrix)
        weights.append(np.stack([high, low]))
    q = np.arange(ROWS)
    angle = -2.0 * np.pi / H * (q[:, None] * n[None, :])
    twiddle = np.stack([np.cos(angle), np.sin(angle)]).astype(np.float32)
    frequency = q[:, None] + ROWS * n[None, :]
    signed = np.where(frequency >= H // 2, frequency - H, frequency)
    turning = -SPREAD_RATE * (2.0 * np.pi / H * signed) ** 2
    spread = (np.stack([np.cos(turning), np.sin(turning)]) / H).astype(np.float32)
    rel = np.arange(H).reshape(ROWS, LANES) / H
    tilt = (TILT_SLOPE * rel - 1.0).astype(np.float32)
    depth = np.maximum(rel - 0.75, 0.0) * 4.0
    absorb = np.exp(-ABSORB_RATE * depth * depth).astype(np.float32)
    bins = np.zeros((2 * LANES, BINS), np.float64)
    for lane in range(2 * LANES):
        bins[lane, (lane % LANES) // BIN :: LANES // BIN] = 1.0 / BIN
    return weights[0], weights[1], twiddle, spread, tilt, absorb, bins.astype(ml_dtypes.bfloat16)


def phase_polynomials():
    root = 2.0 ** 0.25
    sin_scale = root * math.sqrt(2.0)
    cos_scale = 2.0 * math.sqrt(2.0) / sin_scale
    limit = 7.001
    nodes = 0.5 * limit * limit * (1.0 + np.cos(np.pi * (np.arange(64) + 0.5) / 64))
    phi = np.sqrt(nodes)
    sine = np.polynomial.chebyshev.Chebyshev.fit(
        nodes, sin_scale * np.sin(phi / 4) / phi, 4, domain=[0, limit * limit]
    ).convert(kind=np.polynomial.Polynomial)
    cosine = np.polynomial.chebyshev.Chebyshev.fit(
        nodes, cos_scale * np.cos(phi / 4), 4, domain=[0, limit * limit]
    ).convert(kind=np.polynomial.Polynomial)
    return [float(v) for v in sine.coef], [float(v) for v in cosine.coef]


def unit(number, extent):
    angle = -2.0 * math.pi * (number % extent) / extent
    return math.cos(angle), math.sin(angle)


def cmul_const(value, factor):
    re, im = value
    c, s = factor
    if abs(s) < 1e-12 and c > 0:
        return value
    if abs(c) < 1e-12:
        return (im, -re) if s < 0 else (-im, re)
    return re * c - im * s, re * s + im * c


def add(a, b):
    return a[0] + b[0], a[1] + b[1]


def sub(a, b):
    return a[0] - b[0], a[1] - b[1]


def add_turned(a, b, sign):
    if sign < 0:
        return a[0] + b[1], a[1] - b[0]
    return a[0] - b[1], a[1] + b[0]


def dft4(x, sign):
    a, b = add(x[0], x[2]), sub(x[0], x[2])
    c, d = add(x[1], x[3]), sub(x[1], x[3])
    return [add(a, c), add_turned(b, d, sign), sub(a, c), add_turned(b, d, -sign)]


def eighth(a, sign):
    h = math.sqrt(0.5)
    re, im = a
    if sign < 0:
        return (re + im) * h, (im - re) * h
    return (re - im) * h, (re + im) * h


def dft8(x, sign):
    even = dft4(x[0::2], sign)
    odd = dft4(x[1::2], sign)
    odd[1], odd[3] = eighth(odd[1], sign), eighth(odd[3], sign)
    low = [add(even[0], odd[0]), add(even[1], odd[1]), add_turned(even[2], odd[2], sign), add_turned(even[3], odd[3], sign)]
    high = [sub(even[0], odd[0]), sub(even[1], odd[1]), add_turned(even[2], odd[2], -sign), add_turned(even[3], odd[3], -sign)]
    return low + high


def split(value):
    high = value.astype(BF16)
    low = (value - high.astype(F32)).astype(BF16)
    return high, low


def enter(field, columns, jl):
    parts = dft4(columns, -1)
    for ql in range(FOUR):
        re, im = cmul_const(parts[ql], unit(ql * jl, ROWS))
        field[0, ql * EIGHT + jl] = re
        field[1, ql * EIGHT + jl] = im


def joined(pieces):
    re_high, re_low = split(jnp.concatenate([p[0] for p in pieces], axis=0))
    im_high, im_low = split(jnp.concatenate([p[1] for p in pieces], axis=0))
    return jnp.concatenate([re_high, im_high], axis=1), jnp.concatenate([re_low, im_low], axis=1)


def weighted(left, weights, between=()):
    high, low = left
    between = list(between) + [lambda: None] * 3
    total = None
    for part, weight in ((high, weights[0]), (low, weights[0]), (high, weights[1])):
        product = jnp.dot(part, weight, preferred_element_type=F32)
        between.pop(0)()
        total = product if total is None else total + product
    return total


def spread_rows(table, wide):
    for index in np.ndindex(table.shape[:-2]):
        for row in range(table.shape[-2]):
            place = (*index, row)
            wide[place] = jnp.broadcast_to(table[(*index, pl.ds(row, 1))], (SUB, LANES))


def parted(product):
    return [(product[i * SUB : (i + 1) * SUB, :LANES], product[i * SUB : (i + 1) * SUB, LANES:]) for i in range(ROWS)]


Q_ROWS = [ql + FOUR * qh for ql in range(FOUR) for qh in range(EIGHT)]


def forward(field, w_forward, twiddle, between=()):
    pieces = []
    for ql in range(FOUR):
        column = [(field[0, ql * EIGHT + jl], field[1, ql * EIGHT + jl]) for jl in range(EIGHT)]
        for qh, (re, im) in enumerate(dft8(column, -1)):
            q = ql + FOUR * qh
            c, s = twiddle[0, q], twiddle[1, q]
            pieces.append((re * c - im * s, re * s + im * c))
    return weighted(joined(pieces), w_forward, between)


def inverse(product, w_inverse, spread, between=()):
    pieces = []
    for q, (re, im) in zip(Q_ROWS, parted(product)):
        c, s = spread[0, q], spread[1, q]
        pieces.append((re * c - im * s, re * s + im * c))
    return weighted(joined(pieces), w_inverse, between)


def leave(back, product, twiddle):
    pieces = []
    for q, (re, im) in zip(Q_ROWS, parted(product)):
        c, s = twiddle[0, q], twiddle[1, q]
        pieces.append((re * c + im * s, im * c - re * s))
    for ql in range(FOUR):
        column = dft8(pieces[ql * EIGHT : (ql + 1) * EIGHT], 1)
        for jl in range(EIGHT):
            back[0, ql * EIGHT + jl] = column[jl][0]
            back[1, ql * EIGHT + jl] = column[jl][1]


def launch_kernel(start, w_forward, w_inverse, twiddle_table, spread_table, back, field, twiddle, spread):
    spread_rows(twiddle_table, twiddle)
    spread_rows(spread_table, spread)
    for jl in range(EIGHT):
        columns = []
        for jh in range(FOUR):
            j = EIGHT * jh + jl
            columns.append(tuple(jnp.broadcast_to(start[k, j : j + 1, :], (SUB, LANES)) for k in range(2)))
        enter(field, columns, jl)
    product = inverse(forward(field, w_forward, twiddle), w_inverse, spread)
    leave(back, product, twiddle)


def launch(start, consts):
    vmem = pl.BlockSpec(memory_space=pltpu.VMEM)
    return pl.pallas_call(
        launch_kernel,
        out_shape=[jax.ShapeDtypeStruct((2, ROWS, SUB, LANES), F32)] * 2,
        in_specs=[vmem] * 5,
        out_specs=[vmem] * 2,
        scratch_shapes=[pltpu.VMEM((2, ROWS, SUB, LANES), F32)] * 2,
        compiler_params=pltpu.CompilerParams(vmem_limit_bytes=8 * 1024 * 1024),
        cost_estimate=pl.CostEstimate(flops=1_000_000_000, bytes_accessed=1024 * 1024, transcendentals=0),
        name="launch",
    )(start, *consts[:4])


def march_kernel(begin, steps, own, last, levels, cells, launched, entered, *refs):
    if begin > 0:
        totals_in, refs = refs[0], refs[1:]
    (w_forward, w_inverse), refs = refs[:2], refs[2:]
    tables, (bins, section, totals), refs = refs[:4], refs[4:7], refs[7:]
    if not last:
        (left_back, left_field), refs = refs[:2], refs[2:]
    (field, back, energy, power), wide_tables = refs[:4], refs[4:]
    for table, place in zip(tables, wide_tables):
        spread_rows(table, place)
    twiddle, spread, tilt, absorb = wide_tables
    sine, cosine = phase_polynomials()
    heights = levels.shape[2]
    batch = levels.shape[1] // steps
    halves = batch // SUB
    lane = lax.broadcasted_iota(jnp.int32, (SUB, LANES), 1)
    radial = lax.broadcasted_iota(jnp.int32, (SUB, LANES), 0)
    at_once = cells.shape[1] // 2

    def rotate(half, t, ground, jls):
        for jl in jls:
            column = []
            for ql in range(FOUR):
                c, s = unit(ql * jl, ROWS)
                column.append(
                    cmul_const((back[half, 0, ql * EIGHT + jl], back[half, 1, ql * EIGHT + jl]), (c, -s))
                )
            column = dft4(column, 1)
            moved, value = [], []
            for jh in range(FOUR):
                j = EIGHT * jh + jl
                place = j * LANES
                raw = levels[
                    place // heights, pl.ds(pl.multiple_of(t * batch, batch), batch),
                    place % heights : place % heights + LANES,
                ]
                phi = raw.astype(F32)[half * SUB : (half + 1) * SUB] + tilt[j]
                u = phi * phi
                sin_poly, cos_poly = sine[-1], cosine[-1]
                for a, b in zip(sine[-2::-1], cosine[-2::-1]):
                    sin_poly = sin_poly * u + a
                    cos_poly = cos_poly * u + b
                small = sin_poly * phi
                double = small * cos_poly
                turned_c = 1.0 - double * double
                turned_s = double * (math.sqrt(2.0) - small * small)
                re, im = column[jh]
                if (j + 1) * LANES > 3 * H // 4:
                    loss = absorb[j]
                    re, im = re * loss, im * loss
                re, im = re * turned_c - im * turned_s, re * turned_s + im * turned_c
                if j < TERRAIN_ROWS:
                    open_air = lane + j * LANES >= ground
                    re, im = jnp.where(open_air, re, 0.0), jnp.where(open_air, im, 0.0)
                value.append(re * re + im * im)
                moved.append((re, im))
            enter(field.at[half], moved, jl)
            place = FOUR * jl * SUB
            energy[half, place : place + FOUR * SUB, :] = jnp.concatenate(split(jnp.concatenate(value)), axis=1)

    def binned(half, t):
        summed = jnp.dot(energy[half], bins[...], preferred_element_type=F32)
        row = summed[:SUB]
        for i in range(1, ROWS):
            j = i // FOUR + EIGHT * (i % FOUR)
            row = jnp.where(lane // (LANES // BIN) == j, summed[i * SUB : (i + 1) * SUB], row)
        power[pl.ds(pl.multiple_of(t * batch + half * SUB, SUB), SUB), :] = row

    def ground_of(half, t):
        row = cells[(begin + t) // at_once, pl.ds((begin + t) % at_once, 1), :]
        my_lane = lane == section[0] * own + half * SUB + radial
        return jnp.sum(jnp.where(my_lane, row, 0), axis=1, keepdims=True)

    def turn_of(t, resting, moving):
        ground = ground_of(resting, t)
        pieces = [functools.partial(rotate, resting, t, ground, [jl]) for jl in range(EIGHT)]
        product = forward(field.at[moving], w_forward, twiddle, pieces[:3])
        binned(moving, jnp.maximum(t - 1, 0) if resting == 0 else t)
        product = inverse(product, w_inverse, spread, pieces[3:6])
        for piece in pieces[6:]:
            piece()
        leave(back.at[moving], product, twiddle)

    def last_turn(t, resting, before):
        rotate(resting, t, ground_of(resting, t), range(EIGHT))
        binned(before, t)

    def step(t, carry):
        for half in range(halves):
            turn_of(t, half, (half + 1) % halves)
        return carry

    power[...] = jnp.zeros_like(power)
    back[0] = launched[...]
    for half in range(1, halves):
        field[half] = entered[half - 1]
    energy[...] = jnp.zeros_like(energy)
    whole_steps = steps - 1 if last else steps
    lax.fori_loop(0, whole_steps, step, 0)
    if last:
        for half in range(halves - 1):
            turn_of(whole_steps, half, half + 1)
        last_turn(whole_steps, halves - 1, halves - 2)
    binned(halves - 1, steps - 1)
    if not last:
        left_back[...] = back[0]
        for half in range(1, halves):
            left_field[half - 1] = field[half]

    lane = lax.broadcasted_iota(jnp.int32, (1, LANES), 1)
    fit = LANES // batch
    tile_rows = []
    for t in range(steps):
        row = cells[(begin + t) // at_once, at_once + (begin + t) % at_once, :].reshape(1, LANES)
        row = pltpu.roll(row, lax.rem(batch * (t % fit) - section[0] * own + LANES, LANES), 1)
        row = jnp.where(lane % batch < own, row, -1)
        if t % fit == 0:
            tile_rows.append(jnp.where(lane < batch, row, -1))
        else:
            tile_rows[-1] = jnp.where(lane // batch == t % fit, row, tile_rows[-1])
    tile_row = jnp.concatenate(tile_rows, axis=1)
    tiles, cell_count = totals.shape[0], tile_row.shape[1]
    hot = (lax.broadcasted_iota(jnp.int32, (tiles, cell_count), 0) == tile_row).astype(F32).astype(BF16)
    value = power[...]
    high = value.astype(BF16)
    rest = value - high.astype(F32)
    middle = rest.astype(BF16)
    low = (rest - middle.astype(F32)).astype(BF16)
    gain = jnp.dot(hot, high, preferred_element_type=F32)
    gain += jnp.dot(hot, middle, preferred_element_type=F32)
    gain += jnp.dot(hot, low, preferred_element_type=F32)
    totals[...] = gain if begin == 0 else totals_in[...] + gain


def march(section, begin, steps, received, cells, state, totals, consts, tiles, own, last):
    batch = received.shape[1] // steps
    halves = batch // SUB
    vmem = pl.BlockSpec(memory_space=pltpu.VMEM)
    smem = pl.BlockSpec(memory_space=pltpu.SMEM)
    outputs = [jax.ShapeDtypeStruct((tiles, BINS), F32)]
    if not last:
        outputs += [jax.ShapeDtypeStruct(part.shape, F32) for part in state]
    call = pl.pallas_call(
        functools.partial(march_kernel, begin, steps, own, last),
        out_shape=outputs,
        in_specs=[vmem] * (11 + len(totals)) + [smem],
        out_specs=[vmem] * len(outputs),
        scratch_shapes=[
            pltpu.VMEM((halves, 2, ROWS, SUB, LANES), F32),
            pltpu.VMEM((halves, 2, ROWS, SUB, LANES), F32),
            pltpu.VMEM((halves, ROWS * SUB, 2 * LANES), BF16),
            pltpu.VMEM((-(-steps * batch // LANES) * LANES, BINS), F32),
        ] + [pltpu.VMEM((*table.shape[:-1], SUB, LANES), F32) for table in consts[2:6]],
        compiler_params=pltpu.CompilerParams(vmem_limit_bytes=12 * 1024 * 1024),
        cost_estimate=pl.CostEstimate(
            flops=steps * 1_600_000_000, bytes_accessed=4 * 1024 * 1024, transcendentals=0
        ),
        input_output_aliases={4: 0} if last else {2: 1, 3: 2},
        name="march",
    )
    return call(received, cells, *state, *totals, *consts, section)


def turn_steps(block, rows, begin, end, out):
    own, steps, heights = block.shape
    batch = out.shape[0] // (end - begin)
    for c in range(heights // LANES):
        column = slice(c * LANES, (c + 1) * LANES)
        for b in range(own):
            rows[c, b * steps : (b + 1) * steps, :] = block[b, :, column].astype(F32)
        for t in range(begin, end):
            taken = rows[c, pl.ds(t, own, stride=steps), :].astype(BF16)
            if own < batch:
                taken = jnp.pad(taken, ((0, batch - own), (0, 0)))
            out[(t - begin) * batch : (t - begin + 1) * batch, column] = taken


def fill_slabs(begin, end, own, batch, owners, levels, slabs, blocks, turned, rows, sems):
    arrive = [
        pltpu.make_async_copy(levels.at[pl.ds(owner * own, own)], blocks.at[i], sems.at[0, i])
        for i, owner in enumerate(owners)
    ]
    leave = [pltpu.make_async_copy(turned.at[i], slab, sems.at[1, i]) for i, slab in enumerate(slabs)]
    for copy in arrive:
        copy.start()
    for i in range(len(slabs)):
        arrive[i].wait()
        turn_steps(blocks.at[i], rows, begin, end, turned.at[i])
        leave[i].start()
    for copy in leave:
        copy.wait()


def slab_scratch(number, own, steps, heights, count):
    return [
        pltpu.VMEM((number, own, steps, heights), BF16),
        pltpu.VMEM((number, count, heights), BF16),
        pltpu.VMEM((heights // LANES, own * steps, LANES), F32),
        pltpu.SemaphoreType.DMA((2, number)),
    ]


def deal(levels, begin, end, sections, own, batch):
    steps, heights = levels.shape[1:]
    count = (end - begin) * batch
    anywhere = pl.BlockSpec(memory_space=pl.ANY)

    def kernel(levels, out, *scratch):
        places = [out.at[i] for i in range(sections)]
        fill_slabs(begin, end, own, batch, range(sections), levels, places, *scratch)

    return pl.pallas_call(
        kernel,
        out_shape=jax.ShapeDtypeStruct((sections, count, heights), BF16),
        in_specs=[anywhere],
        out_specs=anywhere,
        scratch_shapes=slab_scratch(sections, own, steps, heights, count),
        compiler_params=pltpu.CompilerParams(vmem_limit_bytes=58 * 1024 * 1024),
        cost_estimate=pl.CostEstimate(flops=1_000_000_000, bytes_accessed=4 * 1024 * 1024, transcendentals=0),
        name="deal",
    )(levels)


def gather_small(value):
    radial, sections = lax.axis_index("radial"), lax.axis_size("range")
    other = lax.ppermute(value, "radial", [(0, 1), (1, 0)])
    pair = jnp.stack([jnp.where(radial == 0, value, other), jnp.where(radial == 0, other, value)])
    section = lax.axis_index("range")
    next_pair = lax.ppermute(pair, "range", [(i, i ^ 1) for i in range(sections)])
    even = section % 2 == 0
    both = jnp.stack([jnp.where(even, pair, next_pair), jnp.where(even, next_pair, pair)])
    held = jnp.zeros((sections, *pair.shape), pair.dtype)
    for d in range(0, sections, 2):
        part = lax.ppermute(both, "range", [(i, i ^ d) for i in range(sections)]) if d else both
        held = lax.dynamic_update_slice_in_dim(held, part, (section ^ d) // 2 * 2, 0)
    return held


def local(refractivity, source, terrain, tile_map):
    sections = lax.axis_size("range")
    owners = sections * lax.axis_size("radial")
    radials, steps, heights = refractivity.shape
    own = radials // sections
    batch = -(-own // 16) * 16
    section = lax.axis_index("range").astype(jnp.int32).reshape(1)

    middle = round(EARLY_SHARE * steps)
    dealt = deal(refractivity, 0, middle, sections, own, batch)
    refractivity, dealt = lax.optimization_barrier((refractivity, dealt))
    early = lax.all_to_all(dealt, "range", 0, 0, tiled=True)
    late = lax.all_to_all(deal(refractivity, middle, steps, sections, own, batch), "range", 0, 0, tiled=True)
    everyone = gather_small(jnp.concatenate([terrain.T, tile_map.T]))
    cells = lax.dynamic_index_in_dim(everyone, lax.axis_index("radial"), 1, keepdims=False)
    consts = [jnp.asarray(v) for v in tables()]
    launched, entered = launch(source.reshape(2, ROWS, LANES), consts)
    state = (launched, jnp.stack([entered] * (batch // SUB - 1)))
    tiles = TILE_DEV * owners
    totals, *state = march(section, 0, middle, early, cells, state, [], consts, tiles, own, False)
    (totals,) = march(section, middle, steps - middle, late, cells, state, [totals], consts, tiles, own, True)

    everyone, totals = lax.optimization_barrier((everyone, totals))
    sent = lax.all_to_all(
        totals.reshape(owners, TILE_DEV, BINS), ("range", "radial"), 0, 0, tiled=True
    )
    ids = (lax.axis_index("range") * lax.axis_size("radial") + lax.axis_index("radial")) * TILE_DEV
    ids = ids + jnp.arange(TILE_DEV, dtype=jnp.int32)
    counts = jnp.sum((ids[:, None] == everyone[:, :, terrain.shape[1] :].reshape(1, -1)).astype(F32), axis=1)
    return jnp.sum(sent, axis=0) / counts[:, None]


def solution(mesh):
    in_specs = (
        P(("region", "radial"), None, "range"),
        P(None, "region"),
        P(("region", "radial"), "range"),
        P(("region", "radial"), "range"),
    )
    out_specs = P(("region", "range", "radial"), None)
    return jax.shard_map(local, mesh=mesh, in_specs=in_specs, out_specs=out_specs, check_vma=False)
```

```python
import functools
import math

import jax
import jax.numpy as jnp
import ml_dtypes
import numpy as np
from jax import lax
from jax.experimental import pallas as pl
from jax.experimental.pallas import tpu as pltpu
from jax.sharding import PartitionSpec as P

H = 4096
BIN = 32
LANES = 128
ROWS = H // LANES
FOUR = 4
EIGHT = 8
BINS = H // BIN
TILE_DEV = 16
TILT_SLOPE = 2.0
SPREAD_RATE = 0.5
ABSORB_RATE = 0.05
TERRAIN_ROWS = 4
SUB = 8
EARLY_SHARE = 0.6875

F32 = jnp.float32
BF16 = jnp.bfloat16


def split_np(table):
    high = table.astype(np.float32).astype(ml_dtypes.bfloat16)
    low = (table - high.astype(np.float64)).astype(ml_dtypes.bfloat16)
    return high, low


def tables():
    n = np.arange(LANES)
    angle = -2.0 * np.pi / LANES * (n[:, None] * n[None, :] % LANES)
    c, s = np.cos(angle), np.sin(angle)
    forward = np.block([[c, s], [-s, c]])
    inverse = np.block([[c, -s], [s, c]])
    weights = []
    for matrix in (forward, inverse):
        high, low = split_np(matrix)
        weights.append(np.stack([high, low]))
    q = np.arange(ROWS)
    angle = -2.0 * np.pi / H * (q[:, None] * n[None, :])
    twiddle = np.stack([np.cos(angle), np.sin(angle)]).astype(np.float32)
    frequency = q[:, None] + ROWS * n[None, :]
    signed = np.where(frequency >= H // 2, frequency - H, frequency)
    turning = -SPREAD_RATE * (2.0 * np.pi / H * signed) ** 2
    spread = (np.stack([np.cos(turning), np.sin(turning)]) / H).astype(np.float32)
    rel = np.arange(H).reshape(ROWS, LANES) / H
    tilt = (TILT_SLOPE * rel - 1.0).astype(np.float32)
    depth = np.maximum(rel - 0.75, 0.0) * 4.0
    absorb = np.exp(-ABSORB_RATE * depth * depth).astype(np.float32)
    bins = np.zeros((2 * LANES, BINS), np.float64)
    for lane in range(2 * LANES):
        bins[lane, (lane % LANES) // BIN :: LANES // BIN] = 1.0 / BIN
    return weights[0], weights[1], twiddle, spread, tilt, absorb, bins.astype(ml_dtypes.bfloat16)


def phase_polynomials():
    root = 2.0 ** 0.25
    sin_scale = root * math.sqrt(2.0)
    cos_scale = 2.0 * math.sqrt(2.0) / sin_scale
    limit = 7.001
    nodes = 0.5 * limit * limit * (1.0 + np.cos(np.pi * (np.arange(64) + 0.5) / 64))
    phi = np.sqrt(nodes)
    sine = np.polynomial.chebyshev.Chebyshev.fit(
        nodes, sin_scale * np.sin(phi / 4) / phi, 4, domain=[0, limit * limit]
    ).convert(kind=np.polynomial.Polynomial)
    cosine = np.polynomial.chebyshev.Chebyshev.fit(
        nodes, cos_scale * np.cos(phi / 4), 4, domain=[0, limit * limit]
    ).convert(kind=np.polynomial.Polynomial)
    return [float(v) for v in sine.coef], [float(v) for v in cosine.coef]


def unit(number, extent):
    angle = -2.0 * math.pi * (number % extent) / extent
    return math.cos(angle), math.sin(angle)


def cmul_const(value, factor):
    re, im = value
    c, s = factor
    if abs(s) < 1e-12 and c > 0:
        return value
    if abs(c) < 1e-12:
        return (im, -re) if s < 0 else (-im, re)
    return re * c - im * s, re * s + im * c


def add(a, b):
    return a[0] + b[0], a[1] + b[1]


def sub(a, b):
    return a[0] - b[0], a[1] - b[1]


def add_turned(a, b, sign):
    if sign < 0:
        return a[0] + b[1], a[1] - b[0]
    return a[0] - b[1], a[1] + b[0]


def dft4(x, sign):
    a, b = add(x[0], x[2]), sub(x[0], x[2])
    c, d = add(x[1], x[3]), sub(x[1], x[3])
    return [add(a, c), add_turned(b, d, sign), sub(a, c), add_turned(b, d, -sign)]


def eighth(a, sign):
    h = math.sqrt(0.5)
    re, im = a
    if sign < 0:
        return (re + im) * h, (im - re) * h
    return (re - im) * h, (re + im) * h


def dft8(x, sign):
    even = dft4(x[0::2], sign)
    odd = dft4(x[1::2], sign)
    odd[1], odd[3] = eighth(odd[1], sign), eighth(odd[3], sign)
    low = [add(even[0], odd[0]), add(even[1], odd[1]), add_turned(even[2], odd[2], sign), add_turned(even[3], odd[3], sign)]
    high = [sub(even[0], odd[0]), sub(even[1], odd[1]), add_turned(even[2], odd[2], -sign), add_turned(even[3], odd[3], -sign)]
    return low + high


def split(value):
    high = value.astype(BF16)
    low = (value - high.astype(F32)).astype(BF16)
    return high, low


def enter(field, columns, jl):
    parts = dft4(columns, -1)
    for ql in range(FOUR):
        re, im = cmul_const(parts[ql], unit(ql * jl, ROWS))
        field[0, ql * EIGHT + jl] = re
        field[1, ql * EIGHT + jl] = im


def joined(pieces):
    re_high, re_low = split(jnp.concatenate([p[0] for p in pieces], axis=0))
    im_high, im_low = split(jnp.concatenate([p[1] for p in pieces], axis=0))
    return jnp.concatenate([re_high, im_high, re_low, im_low, re_high, im_high], axis=1)


def weighted(left, weights, between=()):
    product = jnp.dot(
        left, jnp.concatenate([weights[0], weights[0], weights[1]]), preferred_element_type=F32
    )
    for work in between:
        work()
    return product


def spread_rows(table, wide):
    for index in np.ndindex(table.shape[:-2]):
        for row in range(table.shape[-2]):
            place = (*index, row)
            wide[place] = jnp.broadcast_to(table[(*index, pl.ds(row, 1))], (SUB, LANES))


def parted(product):
    return [(product[i * SUB : (i + 1) * SUB, :LANES], product[i * SUB : (i + 1) * SUB, LANES:]) for i in range(ROWS)]


Q_ROWS = [ql + FOUR * qh for ql in range(FOUR) for qh in range(EIGHT)]


def forward(field, w_forward, twiddle, between=()):
    pieces = []
    for ql in range(FOUR):
        column = [(field[0, ql * EIGHT + jl], field[1, ql * EIGHT + jl]) for jl in range(EIGHT)]
        for qh, (re, im) in enumerate(dft8(column, -1)):
            q = ql + FOUR * qh
            c, s = twiddle[0, q], twiddle[1, q]
            pieces.append((re * c - im * s, re * s + im * c))
    return weighted(joined(pieces), w_forward, between)


def inverse(product, w_inverse, spread, between=()):
    pieces = []
    for q, (re, im) in zip(Q_ROWS, parted(product)):
        c, s = spread[0, q], spread[1, q]
        pieces.append((re * c - im * s, re * s + im * c))
    return weighted(joined(pieces), w_inverse, between)


def leave(back, product, twiddle):
    pieces = []
    for q, (re, im) in zip(Q_ROWS, parted(product)):
        c, s = twiddle[0, q], twiddle[1, q]
        pieces.append((re * c + im * s, im * c - re * s))
    for ql in range(FOUR):
        column = dft8(pieces[ql * EIGHT : (ql + 1) * EIGHT], 1)
        for jl in range(EIGHT):
            back[0, ql * EIGHT + jl] = column[jl][0]
            back[1, ql * EIGHT + jl] = column[jl][1]


def launch_kernel(start, w_forward, w_inverse, twiddle_table, spread_table, back, field, twiddle, spread):
    spread_rows(twiddle_table, twiddle)
    spread_rows(spread_table, spread)
    for jl in range(EIGHT):
        columns = []
        for jh in range(FOUR):
            j = EIGHT * jh + jl
            columns.append(tuple(jnp.broadcast_to(start[k, j : j + 1, :], (SUB, LANES)) for k in range(2)))
        enter(field, columns, jl)
    product = inverse(forward(field, w_forward, twiddle), w_inverse, spread)
    leave(back, product, twiddle)


def launch(start, consts):
    vmem = pl.BlockSpec(memory_space=pltpu.VMEM)
    return pl.pallas_call(
        launch_kernel,
        out_shape=[jax.ShapeDtypeStruct((2, ROWS, SUB, LANES), F32)] * 2,
        in_specs=[vmem] * 5,
        out_specs=[vmem] * 2,
        scratch_shapes=[pltpu.VMEM((2, ROWS, SUB, LANES), F32)] * 2,
        compiler_params=pltpu.CompilerParams(vmem_limit_bytes=8 * 1024 * 1024),
        cost_estimate=pl.CostEstimate(flops=1_000_000_000, bytes_accessed=1024 * 1024, transcendentals=0),
        name="launch",
    )(start, *consts[:4])


def march_kernel(begin, steps, own, last, levels, cells, launched, entered, *refs):
    if begin > 0:
        totals_in, refs = refs[0], refs[1:]
    (w_forward, w_inverse), refs = refs[:2], refs[2:]
    tables, (bins, section, totals), refs = refs[:4], refs[4:7], refs[7:]
    if not last:
        (left_back, left_field), refs = refs[:2], refs[2:]
    (field, back, energy, power), wide_tables = refs[:4], refs[4:]
    for table, place in zip(tables, wide_tables):
        spread_rows(table, place)
    twiddle, spread, tilt, absorb = wide_tables
    sine, cosine = phase_polynomials()
    heights = levels.shape[2]
    batch = levels.shape[1] // steps
    halves = batch // SUB
    lane = lax.broadcasted_iota(jnp.int32, (SUB, LANES), 1)
    radial = lax.broadcasted_iota(jnp.int32, (SUB, LANES), 0)
    at_once = cells.shape[1] // 2

    def rotate(half, t, ground, jls):
        for jl in jls:
            column = []
            for ql in range(FOUR):
                c, s = unit(ql * jl, ROWS)
                column.append(
                    cmul_const((back[half, 0, ql * EIGHT + jl], back[half, 1, ql * EIGHT + jl]), (c, -s))
                )
            column = dft4(column, 1)
            moved, value = [], []
            for jh in range(FOUR):
                j = EIGHT * jh + jl
                place = j * LANES
                raw = levels[
                    place // heights, pl.ds(pl.multiple_of(t * batch, batch), batch),
                    place % heights : place % heights + LANES,
                ]
                phi = raw.astype(F32)[half * SUB : (half + 1) * SUB] + tilt[j]
                u = phi * phi
                sin_poly, cos_poly = sine[-1], cosine[-1]
                for a, b in zip(sine[-2::-1], cosine[-2::-1]):
                    sin_poly = sin_poly * u + a
                    cos_poly = cos_poly * u + b
                small = sin_poly * phi
                double = small * cos_poly
                turned_c = 1.0 - double * double
                turned_s = double * (math.sqrt(2.0) - small * small)
                re, im = column[jh]
                if (j + 1) * LANES > 3 * H // 4:
                    loss = absorb[j]
                    re, im = re * loss, im * loss
                re, im = re * turned_c - im * turned_s, re * turned_s + im * turned_c
                if j < TERRAIN_ROWS:
                    open_air = lane + j * LANES >= ground
                    re, im = jnp.where(open_air, re, 0.0), jnp.where(open_air, im, 0.0)
                value.append(re * re + im * im)
                moved.append((re, im))
            enter(field.at[half], moved, jl)
            place = FOUR * jl * SUB
            energy[half, place : place + FOUR * SUB, :] = jnp.concatenate(split(jnp.concatenate(value)), axis=1)

    def binned(half, t):
        summed = jnp.dot(energy[half], bins[...], preferred_element_type=F32)
        row = summed[:SUB]
        for i in range(1, ROWS):
            j = i // FOUR + EIGHT * (i % FOUR)
            row = jnp.where(lane // (LANES // BIN) == j, summed[i * SUB : (i + 1) * SUB], row)
        power[pl.ds(pl.multiple_of(t * batch + half * SUB, SUB), SUB), :] = row

    def ground_of(half, t):
        row = cells[(begin + t) // at_once, pl.ds((begin + t) % at_once, 1), :]
        my_lane = lane == section[0] * own + half * SUB + radial
        return jnp.sum(jnp.where(my_lane, row, 0), axis=1, keepdims=True)

    def turn_of(t, resting, moving):
        ground = ground_of(resting, t)
        pieces = [functools.partial(rotate, resting, t, ground, [jl]) for jl in range(EIGHT)]
        product = forward(field.at[moving], w_forward, twiddle, pieces[:3])
        binned(moving, jnp.maximum(t - 1, 0) if resting == 0 else t)
        product = inverse(product, w_inverse, spread, pieces[3:6])
        for piece in pieces[6:]:
            piece()
        leave(back.at[moving], product, twiddle)

    def last_turn(t, resting, before):
        rotate(resting, t, ground_of(resting, t), range(EIGHT))
        binned(before, t)

    def step(t, carry):
        for half in range(halves):
            turn_of(t, half, (half + 1) % halves)
        return carry

    power[...] = jnp.zeros_like(power)
    back[0] = launched[...]
    for half in range(1, halves):
        field[half] = entered[half - 1]
    energy[...] = jnp.zeros_like(energy)
    whole_steps = steps - 1 if last else steps
    lax.fori_loop(0, whole_steps, step, 0)
    if last:
        for half in range(halves - 1):
            turn_of(whole_steps, half, half + 1)
        last_turn(whole_steps, halves - 1, halves - 2)
    binned(halves - 1, steps - 1)
    if not last:
        left_back[...] = back[0]
        for half in range(1, halves):
            left_field[half - 1] = field[half]

    lane = lax.broadcasted_iota(jnp.int32, (1, LANES), 1)
    fit = LANES // batch
    tile_rows = []
    for t in range(steps):
        row = cells[(begin + t) // at_once, at_once + (begin + t) % at_once, :].reshape(1, LANES)
        row = pltpu.roll(row, lax.rem(batch * (t % fit) - section[0] * own + LANES, LANES), 1)
        row = jnp.where(lane % batch < own, row, -1)
        if t % fit == 0:
            tile_rows.append(jnp.where(lane < batch, row, -1))
        else:
            tile_rows[-1] = jnp.where(lane // batch == t % fit, row, tile_rows[-1])
    tile_row = jnp.concatenate(tile_rows, axis=1)
    tiles, cell_count = totals.shape[0], tile_row.shape[1]
    hot = (lax.broadcasted_iota(jnp.int32, (tiles, cell_count), 0) == tile_row).astype(F32).astype(BF16)
    value = power[...]
    high = value.astype(BF16)
    rest = value - high.astype(F32)
    middle = rest.astype(BF16)
    low = (rest - middle.astype(F32)).astype(BF16)
    gain = jnp.dot(hot, high, preferred_element_type=F32)
    gain += jnp.dot(hot, middle, preferred_element_type=F32)
    gain += jnp.dot(hot, low, preferred_element_type=F32)
    totals[...] = gain if begin == 0 else totals_in[...] + gain


def march(section, begin, steps, received, cells, state, totals, consts, tiles, own, last):
    batch = received.shape[1] // steps
    halves = batch // SUB
    vmem = pl.BlockSpec(memory_space=pltpu.VMEM)
    smem = pl.BlockSpec(memory_space=pltpu.SMEM)
    outputs = [jax.ShapeDtypeStruct((tiles, BINS), F32)]
    if not last:
        outputs += [jax.ShapeDtypeStruct(part.shape, F32) for part in state]
    call = pl.pallas_call(
        functools.partial(march_kernel, begin, steps, own, last),
        out_shape=outputs,
        in_specs=[vmem] * (11 + len(totals)) + [smem],
        out_specs=[vmem] * len(outputs),
        scratch_shapes=[
            pltpu.VMEM((halves, 2, ROWS, SUB, LANES), F32),
            pltpu.VMEM((halves, 2, ROWS, SUB, LANES), F32),
            pltpu.VMEM((halves, ROWS * SUB, 2 * LANES), BF16),
            pltpu.VMEM((-(-steps * batch // LANES) * LANES, BINS), F32),
        ] + [pltpu.VMEM((*table.shape[:-1], SUB, LANES), F32) for table in consts[2:6]],
        compiler_params=pltpu.CompilerParams(vmem_limit_bytes=12 * 1024 * 1024),
        cost_estimate=pl.CostEstimate(
            flops=steps * 1_600_000_000, bytes_accessed=4 * 1024 * 1024, transcendentals=0
        ),
        input_output_aliases={4: 0} if last else {2: 1, 3: 2},
        name="march",
    )
    return call(received, cells, *state, *totals, *consts, section)


def turn_steps(block, rows, begin, end, out):
    own, steps, heights = block.shape
    batch = out.shape[0] // (end - begin)
    for c in range(heights // LANES):
        column = slice(c * LANES, (c + 1) * LANES)
        for b in range(own):
            rows[c, b * steps : (b + 1) * steps, :] = block[b, :, column].astype(F32)
        for t in range(begin, end):
            taken = rows[c, pl.ds(t, own, stride=steps), :].astype(BF16)
            if own < batch:
                taken = jnp.pad(taken, ((0, batch - own), (0, 0)))
            out[(t - begin) * batch : (t - begin + 1) * batch, column] = taken


def fill_slabs(begin, end, own, batch, owners, levels, slabs, blocks, turned, rows, sems):
    arrive = [
        pltpu.make_async_copy(levels.at[pl.ds(owner * own, own)], blocks.at[i], sems.at[0, i])
        for i, owner in enumerate(owners)
    ]
    leave = [pltpu.make_async_copy(turned.at[i], slab, sems.at[1, i]) for i, slab in enumerate(slabs)]
    for copy in arrive:
        copy.start()
    for i in range(len(slabs)):
        arrive[i].wait()
        turn_steps(blocks.at[i], rows, begin, end, turned.at[i])
        leave[i].start()
    for copy in leave:
        copy.wait()


def slab_scratch(number, own, steps, heights, count):
    return [
        pltpu.VMEM((number, own, steps, heights), BF16),
        pltpu.VMEM((number, count, heights), BF16),
        pltpu.VMEM((heights // LANES, own * steps, LANES), F32),
        pltpu.SemaphoreType.DMA((2, number)),
    ]


def deal(levels, begin, end, sections, own, batch):
    steps, heights = levels.shape[1:]
    count = (end - begin) * batch
    anywhere = pl.BlockSpec(memory_space=pl.ANY)

    def kernel(levels, out, *scratch):
        places = [out.at[i] for i in range(sections)]
        fill_slabs(begin, end, own, batch, range(sections), levels, places, *scratch)

    return pl.pallas_call(
        kernel,
        out_shape=jax.ShapeDtypeStruct((sections, count, heights), BF16),
        in_specs=[anywhere],
        out_specs=anywhere,
        scratch_shapes=slab_scratch(sections, own, steps, heights, count),
        compiler_params=pltpu.CompilerParams(vmem_limit_bytes=58 * 1024 * 1024),
        cost_estimate=pl.CostEstimate(flops=1_000_000_000, bytes_accessed=4 * 1024 * 1024, transcendentals=0),
        name="deal",
    )(levels)


def gather_small(value):
    radial, sections = lax.axis_index("radial"), lax.axis_size("range")
    other = lax.ppermute(value, "radial", [(0, 1), (1, 0)])
    pair = jnp.stack([jnp.where(radial == 0, value, other), jnp.where(radial == 0, other, value)])
    section = lax.axis_index("range")
    next_pair = lax.ppermute(pair, "range", [(i, i ^ 1) for i in range(sections)])
    even = section % 2 == 0
    both = jnp.stack([jnp.where(even, pair, next_pair), jnp.where(even, next_pair, pair)])
    held = jnp.zeros((sections, *pair.shape), pair.dtype)
    for d in range(0, sections, 2):
        part = lax.ppermute(both, "range", [(i, i ^ d) for i in range(sections)]) if d else both
        held = lax.dynamic_update_slice_in_dim(held, part, (section ^ d) // 2 * 2, 0)
    return held


def local(refractivity, source, terrain, tile_map):
    sections = lax.axis_size("range")
    owners = sections * lax.axis_size("radial")
    radials, steps, heights = refractivity.shape
    own = radials // sections
    batch = -(-own // 16) * 16
    section = lax.axis_index("range").astype(jnp.int32).reshape(1)

    middle = round(EARLY_SHARE * steps)
    dealt = deal(refractivity, 0, middle, sections, own, batch)
    refractivity, dealt = lax.optimization_barrier((refractivity, dealt))
    early = lax.all_to_all(dealt, "range", 0, 0, tiled=True)
    late = lax.all_to_all(deal(refractivity, middle, steps, sections, own, batch), "range", 0, 0, tiled=True)
    everyone = gather_small(jnp.concatenate([terrain.T, tile_map.T]))
    cells = lax.dynamic_index_in_dim(everyone, lax.axis_index("radial"), 1, keepdims=False)
    consts = [jnp.asarray(v) for v in tables()]
    launched, entered = launch(source.reshape(2, ROWS, LANES), consts)
    state = (launched, jnp.stack([entered] * (batch // SUB - 1)))
    tiles = TILE_DEV * owners
    totals, *state = march(section, 0, middle, early, cells, state, [], consts, tiles, own, False)
    (totals,) = march(section, middle, steps - middle, late, cells, state, [totals], consts, tiles, own, True)

    everyone, totals = lax.optimization_barrier((everyone, totals))
    sent = lax.all_to_all(
        totals.reshape(owners, TILE_DEV, BINS), ("range", "radial"), 0, 0, tiled=True
    )
    ids = (lax.axis_index("range") * lax.axis_size("radial") + lax.axis_index("radial")) * TILE_DEV
    ids = ids + jnp.arange(TILE_DEV, dtype=jnp.int32)
    counts = jnp.sum((ids[:, None] == everyone[:, :, terrain.shape[1] :].reshape(1, -1)).astype(F32), axis=1)
    return jnp.sum(sent, axis=0) / counts[:, None]


def solution(mesh):
    in_specs = (
        P(("region", "radial"), None, "range"),
        P(None, "region"),
        P(("region", "radial"), "range"),
        P(("region", "radial"), "range"),
    )
    out_specs = P(("region", "range", "radial"), None)
    return jax.shard_map(local, mesh=mesh, in_specs=in_specs, out_specs=out_specs, check_vma=False)
```

```python
import functools
import math

import jax
import jax.numpy as jnp
import ml_dtypes
import numpy as np
from jax import lax
from jax.experimental import pallas as pl
from jax.experimental.pallas import tpu as pltpu
from jax.sharding import PartitionSpec as P

H = 4096
BIN = 32
LANES = 128
ROWS = H // LANES
FOUR = 4
EIGHT = 8
BINS = H // BIN
TILE_DEV = 16
TILT_SLOPE = 2.0
SPREAD_RATE = 0.5
ABSORB_RATE = 0.05
TERRAIN_ROWS = 4
SUB = 8
EARLY_SHARE = 0.6875

F32 = jnp.float32
BF16 = jnp.bfloat16


def split_np(table):
    high = table.astype(np.float32).astype(ml_dtypes.bfloat16)
    low = (table - high.astype(np.float64)).astype(ml_dtypes.bfloat16)
    return high, low


def tables():
    n = np.arange(LANES)
    angle = -2.0 * np.pi / LANES * (n[:, None] * n[None, :] % LANES)
    c, s = np.cos(angle), np.sin(angle)
    forward = np.block([[c, s], [-s, c]])
    inverse = np.block([[c, -s], [s, c]])
    weights = []
    for matrix in (forward, inverse):
        high, low = split_np(matrix)
        weights.append(np.stack([high, low]))
    q = np.arange(ROWS)
    angle = -2.0 * np.pi / H * (q[:, None] * n[None, :])
    twiddle = np.stack([np.cos(angle), np.sin(angle)]).astype(np.float32)
    frequency = q[:, None] + ROWS * n[None, :]
    signed = np.where(frequency >= H // 2, frequency - H, frequency)
    turning = -SPREAD_RATE * (2.0 * np.pi / H * signed) ** 2
    spread = (np.stack([np.cos(turning), np.sin(turning)]) / H).astype(np.float32)
    rel = np.arange(H).reshape(ROWS, LANES) / H
    tilt = (TILT_SLOPE * rel - 1.0).astype(np.float32)
    depth = np.maximum(rel - 0.75, 0.0) * 4.0
    absorb = np.exp(-ABSORB_RATE * depth * depth).astype(np.float32)
    bins = np.zeros((2 * LANES, BINS), np.float64)
    for lane in range(2 * LANES):
        bins[lane, (lane % LANES) // BIN :: LANES // BIN] = 1.0 / BIN
    return weights[0], weights[1], twiddle, spread, tilt, absorb, bins.astype(ml_dtypes.bfloat16)


def phase_polynomials():
    root = 2.0 ** 0.25
    sin_scale = root * math.sqrt(2.0)
    cos_scale = 2.0 * math.sqrt(2.0) / sin_scale
    limit = 7.001
    nodes = 0.5 * limit * limit * (1.0 + np.cos(np.pi * (np.arange(64) + 0.5) / 64))
    phi = np.sqrt(nodes)
    sine = np.polynomial.chebyshev.Chebyshev.fit(
        nodes, sin_scale * np.sin(phi / 4) / phi, 4, domain=[0, limit * limit]
    ).convert(kind=np.polynomial.Polynomial)
    cosine = np.polynomial.chebyshev.Chebyshev.fit(
        nodes, cos_scale * np.cos(phi / 4), 4, domain=[0, limit * limit]
    ).convert(kind=np.polynomial.Polynomial)
    return [float(v) for v in sine.coef], [float(v) for v in cosine.coef]


def unit(number, extent):
    angle = -2.0 * math.pi * (number % extent) / extent
    return math.cos(angle), math.sin(angle)


def cmul_const(value, factor):
    re, im = value
    c, s = factor
    if abs(s) < 1e-12 and c > 0:
        return value
    if abs(c) < 1e-12:
        return (im, -re) if s < 0 else (-im, re)
    return re * c - im * s, re * s + im * c


def add(a, b):
    return a[0] + b[0], a[1] + b[1]


def sub(a, b):
    return a[0] - b[0], a[1] - b[1]


def add_turned(a, b, sign):
    if sign < 0:
        return a[0] + b[1], a[1] - b[0]
    return a[0] - b[1], a[1] + b[0]


def dft4(x, sign):
    a, b = add(x[0], x[2]), sub(x[0], x[2])
    c, d = add(x[1], x[3]), sub(x[1], x[3])
    return [add(a, c), add_turned(b, d, sign), sub(a, c), add_turned(b, d, -sign)]


def eighth(a, sign):
    h = math.sqrt(0.5)
    re, im = a
    if sign < 0:
        return (re + im) * h, (im - re) * h
    return (re - im) * h, (re + im) * h


def dft8(x, sign):
    even = dft4(x[0::2], sign)
    odd = dft4(x[1::2], sign)
    odd[1], odd[3] = eighth(odd[1], sign), eighth(odd[3], sign)
    low = [add(even[0], odd[0]), add(even[1], odd[1]), add_turned(even[2], odd[2], sign), add_turned(even[3], odd[3], sign)]
    high = [sub(even[0], odd[0]), sub(even[1], odd[1]), add_turned(even[2], odd[2], -sign), add_turned(even[3], odd[3], -sign)]
    return low + high


def split(value):
    high = value.astype(BF16)
    low = (value - high.astype(F32)).astype(BF16)
    return high, low


def enter(field, columns, jl):
    parts = dft4(columns, -1)
    for ql in range(FOUR):
        re, im = cmul_const(parts[ql], unit(ql * jl, ROWS))
        field[0, ql * EIGHT + jl] = re
        field[1, ql * EIGHT + jl] = im


def joined(pieces):
    re_high, re_low = split(jnp.concatenate([p[0] for p in pieces], axis=0))
    im_high, im_low = split(jnp.concatenate([p[1] for p in pieces], axis=0))
    return jnp.concatenate([re_high, im_high, re_low, im_low, re_high, im_high], axis=1)


def weighted(left, weights, between=()):
    product = jnp.dot(
        left, jnp.concatenate([weights[0], weights[0], weights[1]]), preferred_element_type=F32
    )
    for work in between:
        work()
    return product


def spread_rows(table, wide):
    for index in np.ndindex(table.shape[:-2]):
        for row in range(table.shape[-2]):
            place = (*index, row)
            wide[place] = jnp.broadcast_to(table[(*index, pl.ds(row, 1))], (SUB, LANES))


def parted(product):
    return [(product[i * SUB : (i + 1) * SUB, :LANES], product[i * SUB : (i + 1) * SUB, LANES:]) for i in range(ROWS)]


Q_ROWS = [ql + FOUR * qh for ql in range(FOUR) for qh in range(EIGHT)]


def forward(field, w_forward, twiddle, between=()):
    pieces = []
    for ql in range(FOUR):
        column = [(field[0, ql * EIGHT + jl], field[1, ql * EIGHT + jl]) for jl in range(EIGHT)]
        for qh, (re, im) in enumerate(dft8(column, -1)):
            q = ql + FOUR * qh
            c, s = twiddle[0, q], twiddle[1, q]
            pieces.append((re * c - im * s, re * s + im * c))
    return weighted(joined(pieces), w_forward, between)


def inverse(product, w_inverse, spread, between=()):
    pieces = []
    for q, (re, im) in zip(Q_ROWS, parted(product)):
        c, s = spread[0, q], spread[1, q]
        pieces.append((re * c - im * s, re * s + im * c))
    return weighted(joined(pieces), w_inverse, between)


def leave(back, product, twiddle):
    pieces = []
    for q, (re, im) in zip(Q_ROWS, parted(product)):
        c, s = twiddle[0, q], twiddle[1, q]
        pieces.append((re * c + im * s, im * c - re * s))
    for ql in range(FOUR):
        column = dft8(pieces[ql * EIGHT : (ql + 1) * EIGHT], 1)
        for jl in range(EIGHT):
            back[0, ql * EIGHT + jl] = column[jl][0]
            back[1, ql * EIGHT + jl] = column[jl][1]


def launch_kernel(start, w_forward, w_inverse, twiddle_table, spread_table, back, field, twiddle, spread):
    spread_rows(twiddle_table, twiddle)
    spread_rows(spread_table, spread)
    for jl in range(EIGHT):
        columns = []
        for jh in range(FOUR):
            j = EIGHT * jh + jl
            columns.append(tuple(jnp.broadcast_to(start[k, j : j + 1, :], (SUB, LANES)) for k in range(2)))
        enter(field, columns, jl)
    product = inverse(forward(field, w_forward, twiddle), w_inverse, spread)
    leave(back, product, twiddle)


def launch(start, consts):
    vmem = pl.BlockSpec(memory_space=pltpu.VMEM)
    return pl.pallas_call(
        launch_kernel,
        out_shape=[jax.ShapeDtypeStruct((2, ROWS, SUB, LANES), F32)] * 2,
        in_specs=[vmem] * 5,
        out_specs=[vmem] * 2,
        scratch_shapes=[pltpu.VMEM((2, ROWS, SUB, LANES), F32)] * 2,
        compiler_params=pltpu.CompilerParams(vmem_limit_bytes=8 * 1024 * 1024),
        cost_estimate=pl.CostEstimate(flops=1_000_000_000, bytes_accessed=1024 * 1024, transcendentals=0),
        name="launch",
    )(start, *consts[:4])


def march_kernel(begin, steps, own, last, levels, cells, launched, entered, *refs):
    if begin > 0:
        totals_in, refs = refs[0], refs[1:]
    (w_forward, w_inverse), refs = refs[:2], refs[2:]
    tables, (bins, section, totals), refs = refs[:4], refs[4:7], refs[7:]
    if not last:
        (left_back, left_field), refs = refs[:2], refs[2:]
    (field, back, energy, power), wide_tables = refs[:4], refs[4:]
    for table, place in zip(tables, wide_tables):
        spread_rows(table, place)
    twiddle, spread, tilt, absorb = wide_tables
    sine, cosine = phase_polynomials()
    heights = levels.shape[2]
    batch = levels.shape[1] // steps
    halves = batch // SUB
    lane = lax.broadcasted_iota(jnp.int32, (SUB, LANES), 1)
    radial = lax.broadcasted_iota(jnp.int32, (SUB, LANES), 0)
    at_once = cells.shape[1] // 2

    def rotate(half, t, ground, jls):
        for jl in jls:
            column = []
            for ql in range(FOUR):
                c, s = unit(ql * jl, ROWS)
                column.append(
                    cmul_const((back[half, 0, ql * EIGHT + jl], back[half, 1, ql * EIGHT + jl]), (c, -s))
                )
            column = dft4(column, 1)
            moved, value = [], []
            for jh in range(FOUR):
                j = EIGHT * jh + jl
                place = j * LANES
                raw = levels[
                    place // heights, pl.ds(pl.multiple_of(t * batch, batch), batch),
                    place % heights : place % heights + LANES,
                ]
                phi = raw.astype(F32)[half * SUB : (half + 1) * SUB] + tilt[j]
                u = phi * phi
                sin_poly, cos_poly = sine[-1], cosine[-1]
                for a, b in zip(sine[-2::-1], cosine[-2::-1]):
                    sin_poly = sin_poly * u + a
                    cos_poly = cos_poly * u + b
                small = sin_poly * phi
                double = small * cos_poly
                turned_c = 1.0 - double * double
                turned_s = double * (math.sqrt(2.0) - small * small)
                re, im = column[jh]
                if (j + 1) * LANES > 3 * H // 4:
                    loss = absorb[j]
                    re, im = re * loss, im * loss
                re, im = re * turned_c - im * turned_s, re * turned_s + im * turned_c
                if j < TERRAIN_ROWS:
                    open_air = lane + j * LANES >= ground
                    re, im = jnp.where(open_air, re, 0.0), jnp.where(open_air, im, 0.0)
                value.append(re * re + im * im)
                moved.append((re, im))
            enter(field.at[half], moved, jl)
            place = FOUR * jl * SUB
            energy[half, place : place + FOUR * SUB, :] = jnp.concatenate(split(jnp.concatenate(value)), axis=1)

    def binned(half, t):
        summed = jnp.dot(energy[half], bins[...], preferred_element_type=F32)
        row = summed[:SUB]
        for i in range(1, ROWS):
            j = i // FOUR + EIGHT * (i % FOUR)
            row = jnp.where(lane // (LANES // BIN) == j, summed[i * SUB : (i + 1) * SUB], row)
        power[pl.ds(pl.multiple_of(t * batch + half * SUB, SUB), SUB), :] = row

    def ground_of(half, t):
        row = cells[(begin + t) // at_once, pl.ds((begin + t) % at_once, 1), :]
        my_lane = lane == section[0] * own + half * SUB + radial
        return jnp.sum(jnp.where(my_lane, row, 0), axis=1, keepdims=True)

    def turn_of(t, resting, moving):
        ground = ground_of(resting, t)
        pieces = [functools.partial(rotate, resting, t, ground, [jl]) for jl in range(EIGHT)]
        product = forward(field.at[moving], w_forward, twiddle, pieces[:3])
        binned(moving, jnp.maximum(t - 1, 0) if resting == 0 else t)
        product = inverse(product, w_inverse, spread, pieces[3:6])
        for piece in pieces[6:]:
            piece()
        leave(back.at[moving], product, twiddle)

    def last_turn(t, resting, before):
        rotate(resting, t, ground_of(resting, t), range(EIGHT))
        binned(before, t)

    def step(t, carry):
        for half in range(halves):
            turn_of(t, half, (half + 1) % halves)
        return carry

    power[...] = jnp.zeros_like(power)
    back[0] = launched[...]
    for half in range(1, halves):
        field[half] = entered[half - 1]
    energy[...] = jnp.zeros_like(energy)
    whole_steps = steps - 1 if last else steps
    lax.fori_loop(0, whole_steps // 2, lambda i, carry: step(2 * i + 1, step(2 * i, carry)), 0)
    if whole_steps % 2:
        step(whole_steps - 1, 0)
    if last:
        for half in range(halves - 1):
            turn_of(whole_steps, half, half + 1)
        last_turn(whole_steps, halves - 1, halves - 2)
    binned(halves - 1, steps - 1)
    if not last:
        left_back[...] = back[0]
        for half in range(1, halves):
            left_field[half - 1] = field[half]

    lane = lax.broadcasted_iota(jnp.int32, (1, LANES), 1)
    fit = LANES // batch
    tile_rows = []
    for t in range(steps):
        row = cells[(begin + t) // at_once, at_once + (begin + t) % at_once, :].reshape(1, LANES)
        row = pltpu.roll(row, lax.rem(batch * (t % fit) - section[0] * own + LANES, LANES), 1)
        row = jnp.where(lane % batch < own, row, -1)
        if t % fit == 0:
            tile_rows.append(jnp.where(lane < batch, row, -1))
        else:
            tile_rows[-1] = jnp.where(lane // batch == t % fit, row, tile_rows[-1])
    tile_row = jnp.concatenate(tile_rows, axis=1)
    tiles, cell_count = totals.shape[0], tile_row.shape[1]
    hot = (lax.broadcasted_iota(jnp.int32, (tiles, cell_count), 0) == tile_row).astype(F32).astype(BF16)
    value = power[...]
    high = value.astype(BF16)
    rest = value - high.astype(F32)
    middle = rest.astype(BF16)
    low = (rest - middle.astype(F32)).astype(BF16)
    gain = jnp.dot(hot, high, preferred_element_type=F32)
    gain += jnp.dot(hot, middle, preferred_element_type=F32)
    gain += jnp.dot(hot, low, preferred_element_type=F32)
    totals[...] = gain if begin == 0 else totals_in[...] + gain


def march(section, begin, steps, received, cells, state, totals, consts, tiles, own, last):
    batch = received.shape[1] // steps
    halves = batch // SUB
    vmem = pl.BlockSpec(memory_space=pltpu.VMEM)
    smem = pl.BlockSpec(memory_space=pltpu.SMEM)
    outputs = [jax.ShapeDtypeStruct((tiles, BINS), F32)]
    if not last:
        outputs += [jax.ShapeDtypeStruct(part.shape, F32) for part in state]
    call = pl.pallas_call(
        functools.partial(march_kernel, begin, steps, own, last),
        out_shape=outputs,
        in_specs=[vmem] * (11 + len(totals)) + [smem],
        out_specs=[vmem] * len(outputs),
        scratch_shapes=[
            pltpu.VMEM((halves, 2, ROWS, SUB, LANES), F32),
            pltpu.VMEM((halves, 2, ROWS, SUB, LANES), F32),
            pltpu.VMEM((halves, ROWS * SUB, 2 * LANES), BF16),
            pltpu.VMEM((-(-steps * batch // LANES) * LANES, BINS), F32),
        ] + [pltpu.VMEM((*table.shape[:-1], SUB, LANES), F32) for table in consts[2:6]],
        compiler_params=pltpu.CompilerParams(vmem_limit_bytes=12 * 1024 * 1024),
        cost_estimate=pl.CostEstimate(
            flops=steps * 1_600_000_000, bytes_accessed=4 * 1024 * 1024, transcendentals=0
        ),
        input_output_aliases={4: 0} if last else {2: 1, 3: 2},
        name="march",
    )
    return call(received, cells, *state, *totals, *consts, section)


def turn_steps(block, rows, begin, end, out):
    own, steps, heights = block.shape
    batch = out.shape[0] // (end - begin)
    for c in range(heights // LANES):
        column = slice(c * LANES, (c + 1) * LANES)
        for b in range(own):
            rows[c, b * steps : (b + 1) * steps, :] = block[b, :, column].astype(F32)
        for t in range(begin, end):
            taken = rows[c, pl.ds(t, own, stride=steps), :].astype(BF16)
            if own < batch:
                taken = jnp.pad(taken, ((0, batch - own), (0, 0)))
            out[(t - begin) * batch : (t - begin + 1) * batch, column] = taken


def fill_slabs(begin, end, own, batch, owners, levels, slabs, blocks, turned, rows, sems):
    arrive = [
        pltpu.make_async_copy(levels.at[pl.ds(owner * own, own)], blocks.at[i], sems.at[0, i])
        for i, owner in enumerate(owners)
    ]
    leave = [pltpu.make_async_copy(turned.at[i], slab, sems.at[1, i]) for i, slab in enumerate(slabs)]
    for copy in arrive:
        copy.start()
    for i in range(len(slabs)):
        arrive[i].wait()
        turn_steps(blocks.at[i], rows, begin, end, turned.at[i])
        leave[i].start()
    for copy in leave:
        copy.wait()


def slab_scratch(number, own, steps, heights, count):
    return [
        pltpu.VMEM((number, own, steps, heights), BF16),
        pltpu.VMEM((number, count, heights), BF16),
        pltpu.VMEM((heights // LANES, own * steps, LANES), F32),
        pltpu.SemaphoreType.DMA((2, number)),
    ]


def deal(levels, begin, end, sections, own, batch):
    steps, heights = levels.shape[1:]
    count = (end - begin) * batch
    anywhere = pl.BlockSpec(memory_space=pl.ANY)

    def kernel(levels, out, *scratch):
        places = [out.at[i] for i in range(sections)]
        fill_slabs(begin, end, own, batch, range(sections), levels, places, *scratch)

    return pl.pallas_call(
        kernel,
        out_shape=jax.ShapeDtypeStruct((sections, count, heights), BF16),
        in_specs=[anywhere],
        out_specs=anywhere,
        scratch_shapes=slab_scratch(sections, own, steps, heights, count),
        compiler_params=pltpu.CompilerParams(vmem_limit_bytes=58 * 1024 * 1024),
        cost_estimate=pl.CostEstimate(flops=1_000_000_000, bytes_accessed=4 * 1024 * 1024, transcendentals=0),
        name="deal",
    )(levels)


def gather_small(value):
    radial, sections = lax.axis_index("radial"), lax.axis_size("range")
    other = lax.ppermute(value, "radial", [(0, 1), (1, 0)])
    pair = jnp.stack([jnp.where(radial == 0, value, other), jnp.where(radial == 0, other, value)])
    section = lax.axis_index("range")
    next_pair = lax.ppermute(pair, "range", [(i, i ^ 1) for i in range(sections)])
    even = section % 2 == 0
    both = jnp.stack([jnp.where(even, pair, next_pair), jnp.where(even, next_pair, pair)])
    held = jnp.zeros((sections, *pair.shape), pair.dtype)
    for d in range(0, sections, 2):
        part = lax.ppermute(both, "range", [(i, i ^ d) for i in range(sections)]) if d else both
        held = lax.dynamic_update_slice_in_dim(held, part, (section ^ d) // 2 * 2, 0)
    return held


def local(refractivity, source, terrain, tile_map):
    sections = lax.axis_size("range")
    owners = sections * lax.axis_size("radial")
    radials, steps, heights = refractivity.shape
    own = radials // sections
    batch = -(-own // 16) * 16
    section = lax.axis_index("range").astype(jnp.int32).reshape(1)

    middle = round(EARLY_SHARE * steps)
    dealt = deal(refractivity, 0, middle, sections, own, batch)
    refractivity, dealt = lax.optimization_barrier((refractivity, dealt))
    early = lax.all_to_all(dealt, "range", 0, 0, tiled=True)
    late = lax.all_to_all(deal(refractivity, middle, steps, sections, own, batch), "range", 0, 0, tiled=True)
    everyone = gather_small(jnp.concatenate([terrain.T, tile_map.T]))
    cells = lax.dynamic_index_in_dim(everyone, lax.axis_index("radial"), 1, keepdims=False)
    consts = [jnp.asarray(v) for v in tables()]
    launched, entered = launch(source.reshape(2, ROWS, LANES), consts)
    state = (launched, jnp.stack([entered] * (batch // SUB - 1)))
    tiles = TILE_DEV * owners
    totals, *state = march(section, 0, middle, early, cells, state, [], consts, tiles, own, False)
    (totals,) = march(section, middle, steps - middle, late, cells, state, [totals], consts, tiles, own, True)

    everyone, totals = lax.optimization_barrier((everyone, totals))
    sent = lax.all_to_all(
        totals.reshape(owners, TILE_DEV, BINS), ("range", "radial"), 0, 0, tiled=True
    )
    ids = (lax.axis_index("range") * lax.axis_size("radial") + lax.axis_index("radial")) * TILE_DEV
    ids = ids + jnp.arange(TILE_DEV, dtype=jnp.int32)
    counts = jnp.sum((ids[:, None] == everyone[:, :, terrain.shape[1] :].reshape(1, -1)).astype(F32), axis=1)
    return jnp.sum(sent, axis=0) / counts[:, None]


def solution(mesh):
    in_specs = (
        P(("region", "radial"), None, "range"),
        P(None, "region"),
        P(("region", "radial"), "range"),
        P(("region", "radial"), "range"),
    )
    out_specs = P(("region", "range", "radial"), None)
    return jax.shard_map(local, mesh=mesh, in_specs=in_specs, out_specs=out_specs, check_vma=False)
```

```python
import functools
import math

import jax
import jax.numpy as jnp
import ml_dtypes
import numpy as np
from jax import lax
from jax.experimental import pallas as pl
from jax.experimental.pallas import tpu as pltpu
from jax.sharding import PartitionSpec as P

H = 4096
BIN = 32
LANES = 128
ROWS = H // LANES
FOUR = 4
EIGHT = 8
BINS = H // BIN
TILE_DEV = 16
TILT_SLOPE = 2.0
SPREAD_RATE = 0.5
ABSORB_RATE = 0.05
TERRAIN_ROWS = 4
SUB = 8
EARLY_SHARE = 0.6875

F32 = jnp.float32
BF16 = jnp.bfloat16


def split_np(table):
    high = table.astype(np.float32).astype(ml_dtypes.bfloat16)
    low = (table - high.astype(np.float64)).astype(ml_dtypes.bfloat16)
    return high, low


def tables():
    n = np.arange(LANES)
    angle = -2.0 * np.pi / LANES * (n[:, None] * n[None, :] % LANES)
    c, s = np.cos(angle), np.sin(angle)
    high, low = split_np(np.block([[c, s], [-s, c]]))
    weights = np.stack([high, low])
    q = np.arange(ROWS)
    angle = -2.0 * np.pi / H * (q[:, None] * n[None, :])
    twiddle = np.stack([np.cos(angle), -np.sin(angle)]).astype(np.float32)
    frequency = q[:, None] + ROWS * n[None, :]
    signed = np.where(frequency >= H // 2, frequency - H, frequency)
    turning = -SPREAD_RATE * (2.0 * np.pi / H * signed) ** 2
    spread = (np.stack([np.cos(turning), -np.sin(turning)]) / H).astype(np.float32)
    rel = np.arange(H).reshape(ROWS, LANES) / H
    tilt = (TILT_SLOPE * rel - 1.0).astype(np.float32)
    depth = np.maximum(rel - 0.75, 0.0) * 4.0
    absorb = np.exp(-ABSORB_RATE * depth * depth).astype(np.float32)
    bins = np.zeros((2 * LANES, BINS), np.float64)
    for lane in range(2 * LANES):
        bins[lane, (lane % LANES) // BIN :: LANES // BIN] = 1.0 / BIN
    return weights, twiddle, spread, tilt, absorb, bins.astype(ml_dtypes.bfloat16)


def phase_polynomials():
    root = 2.0 ** 0.25
    sin_scale = root * math.sqrt(2.0)
    cos_scale = 2.0 * math.sqrt(2.0) / sin_scale
    limit = 7.001
    nodes = 0.5 * limit * limit * (1.0 + np.cos(np.pi * (np.arange(64) + 0.5) / 64))
    phi = np.sqrt(nodes)
    sine = np.polynomial.chebyshev.Chebyshev.fit(
        nodes, sin_scale * np.sin(phi / 4) / phi, 4, domain=[0, limit * limit]
    ).convert(kind=np.polynomial.Polynomial)
    cosine = np.polynomial.chebyshev.Chebyshev.fit(
        nodes, cos_scale * np.cos(phi / 4), 4, domain=[0, limit * limit]
    ).convert(kind=np.polynomial.Polynomial)
    return [float(v) for v in sine.coef], [float(v) for v in cosine.coef]


def unit(number, extent):
    angle = -2.0 * math.pi * (number % extent) / extent
    return math.cos(angle), math.sin(angle)


def cmul_const(value, factor):
    re, im = value
    c, s = factor
    if abs(s) < 1e-12 and c > 0:
        return value
    if abs(c) < 1e-12:
        return (im, -re) if s < 0 else (-im, re)
    return re * c - im * s, re * s + im * c


def add(a, b):
    return a[0] + b[0], a[1] + b[1]


def sub(a, b):
    return a[0] - b[0], a[1] - b[1]


def add_turned(a, b, sign):
    if sign < 0:
        return a[0] + b[1], a[1] - b[0]
    return a[0] - b[1], a[1] + b[0]


def dft4(x, sign):
    a, b = add(x[0], x[2]), sub(x[0], x[2])
    c, d = add(x[1], x[3]), sub(x[1], x[3])
    return [add(a, c), add_turned(b, d, sign), sub(a, c), add_turned(b, d, -sign)]


def eighth(a, sign):
    h = math.sqrt(0.5)
    re, im = a
    if sign < 0:
        return (re + im) * h, (im - re) * h
    return (re - im) * h, (re + im) * h


def dft8(x, sign):
    even = dft4(x[0::2], sign)
    odd = dft4(x[1::2], sign)
    odd[1], odd[3] = eighth(odd[1], sign), eighth(odd[3], sign)
    low = [add(even[0], odd[0]), add(even[1], odd[1]), add_turned(even[2], odd[2], sign), add_turned(even[3], odd[3], sign)]
    high = [sub(even[0], odd[0]), sub(even[1], odd[1]), add_turned(even[2], odd[2], -sign), add_turned(even[3], odd[3], -sign)]
    return low + high


def split(value):
    high = value.astype(BF16)
    low = (value - high.astype(F32)).astype(BF16)
    return high, low


def enter(field, columns, jl):
    parts = dft4(columns, -1)
    for ql in range(FOUR):
        re, im = cmul_const(parts[ql], unit(ql * jl, ROWS))
        field[0, ql * EIGHT + jl] = re
        field[1, ql * EIGHT + jl] = im


def joined(pieces):
    re_high, re_low = split(jnp.concatenate([p[0] for p in pieces], axis=0))
    im_high, im_low = split(jnp.concatenate([p[1] for p in pieces], axis=0))
    return jnp.concatenate([re_high, im_high, re_low, im_low, re_high, im_high], axis=1)


def weighted(left, weights, between=()):
    product = jnp.dot(
        left, jnp.concatenate([weights[0], weights[0], weights[1]]), preferred_element_type=F32
    )
    for work in between:
        work()
    return product


def spread_rows(table, wide):
    for index in np.ndindex(table.shape[:-2]):
        for row in range(table.shape[-2]):
            place = (*index, row)
            wide[place] = jnp.broadcast_to(table[(*index, pl.ds(row, 1))], (SUB, LANES))


def parted(product):
    return [(product[i * SUB : (i + 1) * SUB, :LANES], product[i * SUB : (i + 1) * SUB, LANES:]) for i in range(ROWS)]


Q_ROWS = [ql + FOUR * qh for ql in range(FOUR) for qh in range(EIGHT)]


def forward(field, weights, twiddle, between=()):
    pieces = []
    for ql in range(FOUR):
        column = [(field[0, ql * EIGHT + jl], field[1, ql * EIGHT + jl]) for jl in range(EIGHT)]
        for qh, (re, im) in enumerate(dft8(column, -1)):
            q = ql + FOUR * qh
            c, s = twiddle[0, q], twiddle[1, q]
            pieces.append((re * c + im * s, im * c - re * s))
    return weighted(joined(pieces), weights, between)


def inverse(product, weights, spread, between=()):
    pieces = []
    for q, (re, im) in zip(Q_ROWS, parted(product)):
        c, s = spread[0, q], spread[1, q]
        pieces.append((re * c + im * s, re * s - im * c))
    return weighted(joined(pieces), weights, between)


def leave(back, product, twiddle):
    pieces = []
    for q, (re, im) in zip(Q_ROWS, parted(product)):
        c, s = twiddle[0, q], twiddle[1, q]
        pieces.append((re * c + im * s, re * s - im * c))
    for ql in range(FOUR):
        column = dft8(pieces[ql * EIGHT : (ql + 1) * EIGHT], 1)
        for jl in range(EIGHT):
            back[0, ql * EIGHT + jl] = column[jl][0]
            back[1, ql * EIGHT + jl] = column[jl][1]


def enter_source(field, start):
    for jl in range(EIGHT):
        columns = []
        for jh in range(FOUR):
            j = EIGHT * jh + jl
            columns.append(tuple(jnp.broadcast_to(start[k, j : j + 1, :], (SUB, LANES)) for k in range(2)))
        enter(field, columns, jl)


def launch_kernel(start, weights, twiddle_table, spread_table, back, field, twiddle, spread):
    spread_rows(twiddle_table, twiddle)
    spread_rows(spread_table, spread)
    enter_source(field, start)
    product = inverse(forward(field, weights, twiddle), weights, spread)
    leave(back, product, twiddle)


def launch(start, consts):
    vmem = pl.BlockSpec(memory_space=pltpu.VMEM)
    return pl.pallas_call(
        launch_kernel,
        out_shape=jax.ShapeDtypeStruct((2, ROWS, SUB, LANES), F32),
        in_specs=[vmem] * 4,
        out_specs=vmem,
        scratch_shapes=[pltpu.VMEM((2, ROWS, SUB, LANES), F32)] * 3,
        compiler_params=pltpu.CompilerParams(vmem_limit_bytes=8 * 1024 * 1024),
        cost_estimate=pl.CostEstimate(flops=1_000_000_000, bytes_accessed=1024 * 1024, transcendentals=0),
        name="launch",
    )(start, *consts[:3])


def march_kernel(begin, steps, own, last, levels, cells, launched, entered, *refs):
    if begin > 0:
        totals_in, refs = refs[0], refs[1:]
    weights, refs = refs[0], refs[1:]
    tables, (bins, section, totals), refs = refs[:4], refs[4:7], refs[7:]
    if not last:
        (left_back, left_field), refs = refs[:2], refs[2:]
    (field, back, energy, power), wide_tables = refs[:4], refs[4:]
    for table, place in zip(tables, wide_tables):
        spread_rows(table, place)
    twiddle, spread, tilt, absorb = wide_tables
    sine, cosine = phase_polynomials()
    heights = levels.shape[2]
    batch = levels.shape[1] // steps
    halves = batch // SUB
    lane = lax.broadcasted_iota(jnp.int32, (SUB, LANES), 1)
    radial = lax.broadcasted_iota(jnp.int32, (SUB, LANES), 0)
    at_once = cells.shape[1] // 2

    def rotate(half, t, ground, jls, onward=True):
        for jl in jls:
            column = []
            for ql in range(FOUR):
                c, s = unit(ql * jl, ROWS)
                column.append(
                    cmul_const((back[half, 0, ql * EIGHT + jl], back[half, 1, ql * EIGHT + jl]), (c, -s))
                )
            column = dft4(column, 1)
            moved, value = [], []
            for jh in range(FOUR):
                j = EIGHT * jh + jl
                place = j * LANES
                raw = levels[
                    place // heights, pl.ds(pl.multiple_of(t * batch, batch), batch),
                    place % heights : place % heights + LANES,
                ]
                phi = raw.astype(F32)[half * SUB : (half + 1) * SUB] + tilt[j]
                u = phi * phi
                sin_poly, cos_poly = sine[-1], cosine[-1]
                for a, b in zip(sine[-2::-1], cosine[-2::-1]):
                    sin_poly = sin_poly * u + a
                    cos_poly = cos_poly * u + b
                small = sin_poly * phi
                double = small * cos_poly
                turned_c = 1.0 - double * double
                turned_s = double * (math.sqrt(2.0) - small * small)
                re, im = column[jh]
                if (j + 1) * LANES > 3 * H // 4:
                    loss = absorb[j]
                    re, im = re * loss, im * loss
                re, im = re * turned_c - im * turned_s, re * turned_s + im * turned_c
                if j < TERRAIN_ROWS:
                    open_air = lane + j * LANES >= ground
                    re, im = jnp.where(open_air, re, 0.0), jnp.where(open_air, im, 0.0)
                value.append(re * re + im * im)
                moved.append((re, im))
            if onward:
                enter(field.at[half], moved, jl)
            place = FOUR * jl * SUB
            energy[half, place : place + FOUR * SUB, :] = jnp.concatenate(split(jnp.concatenate(value)), axis=1)

    def binned(half, t):
        summed = jnp.dot(energy[half], bins[...], preferred_element_type=F32)
        row = summed[:SUB]
        for i in range(1, ROWS):
            j = i // FOUR + EIGHT * (i % FOUR)
            row = jnp.where(lane // (LANES // BIN) == j, summed[i * SUB : (i + 1) * SUB], row)
        power[pl.ds(pl.multiple_of(t * batch + half * SUB, SUB), SUB), :] = row

    def ground_of(half, t):
        row = cells[(begin + t) // at_once, pl.ds((begin + t) % at_once, 1), :]
        my_lane = lane == section[0] * own + half * SUB + radial
        return jnp.sum(jnp.where(my_lane, row, 0), axis=1, keepdims=True)

    def turn_of(t, resting, moving):
        ground = ground_of(resting, t)
        pieces = [functools.partial(rotate, resting, t, ground, [jl]) for jl in range(EIGHT)]
        product = forward(field.at[moving], weights, twiddle, pieces[:3])
        binned(moving, jnp.maximum(t - 1, 0) if resting == 0 else t)
        product = inverse(product, weights, spread, pieces[3:6])
        for piece in pieces[6:]:
            piece()
        leave(back.at[moving], product, twiddle)

    def last_turn(t, resting, before):
        rotate(resting, t, ground_of(resting, t), range(EIGHT), False)
        binned(before, t)

    def step(t, carry):
        for half in range(halves):
            turn_of(t, half, (half + 1) % halves)
        return carry

    power[...] = jnp.zeros_like(power)
    back[0] = launched[...]
    for half in range(1, halves):
        if begin == 0:
            enter_source(field.at[half], entered)
        else:
            field[half] = entered[half - 1]
    energy[...] = jnp.zeros_like(energy)
    whole_steps = steps - 1 if last else steps
    lax.fori_loop(0, whole_steps, step, 0)
    if last:
        for half in range(halves - 1):
            turn_of(whole_steps, half, half + 1)
        last_turn(whole_steps, halves - 1, halves - 2)
    binned(halves - 1, steps - 1)
    if not last:
        left_back[...] = back[0]
        for half in range(1, halves):
            left_field[half - 1] = field[half]

    lane = lax.broadcasted_iota(jnp.int32, (1, LANES), 1)
    fit = LANES // batch
    tile_rows = []
    for t in range(steps):
        row = cells[(begin + t) // at_once, at_once + (begin + t) % at_once, :].reshape(1, LANES)
        row = pltpu.roll(row, lax.rem(batch * (t % fit) - section[0] * own + LANES, LANES), 1)
        row = jnp.where(lane % batch < own, row, -1)
        if t % fit == 0:
            tile_rows.append(jnp.where(lane < batch, row, -1))
        else:
            tile_rows[-1] = jnp.where(lane // batch == t % fit, row, tile_rows[-1])
    tile_row = jnp.concatenate(tile_rows, axis=1)
    tiles, cell_count = totals.shape[0], tile_row.shape[1]
    hot = (lax.broadcasted_iota(jnp.int32, (tiles, cell_count), 0) == tile_row).astype(F32).astype(BF16)
    value = power[...]
    high = value.astype(BF16)
    rest = value - high.astype(F32)
    middle = rest.astype(BF16)
    low = (rest - middle.astype(F32)).astype(BF16)
    gain = jnp.dot(hot, high, preferred_element_type=F32)
    gain += jnp.dot(hot, middle, preferred_element_type=F32)
    gain += jnp.dot(hot, low, preferred_element_type=F32)
    totals[...] = gain if begin == 0 else totals_in[...] + gain


def march(section, begin, steps, received, cells, state, totals, consts, tiles, own, last):
    batch = received.shape[1] // steps
    halves = batch // SUB
    vmem = pl.BlockSpec(memory_space=pltpu.VMEM)
    smem = pl.BlockSpec(memory_space=pltpu.SMEM)
    outputs = [jax.ShapeDtypeStruct((tiles, BINS), F32)]
    if not last:
        outputs += [jax.ShapeDtypeStruct((*lead, 2, ROWS, SUB, LANES), F32) for lead in ((), (halves - 1,))]
    call = pl.pallas_call(
        functools.partial(march_kernel, begin, steps, own, last),
        out_shape=outputs,
        in_specs=[vmem] * (10 + len(totals)) + [smem],
        out_specs=[vmem] * len(outputs),
        scratch_shapes=[
            pltpu.VMEM((halves, 2, ROWS, SUB, LANES), F32),
            pltpu.VMEM((halves, 2, ROWS, SUB, LANES), F32),
            pltpu.VMEM((halves, ROWS * SUB, 2 * LANES), BF16),
            pltpu.VMEM((-(-steps * batch // LANES) * LANES, BINS), F32),
        ] + [pltpu.VMEM((*table.shape[:-1], SUB, LANES), F32) for table in consts[1:5]],
        compiler_params=pltpu.CompilerParams(vmem_limit_bytes=12 * 1024 * 1024),
        cost_estimate=pl.CostEstimate(
            flops=steps * 1_600_000_000, bytes_accessed=4 * 1024 * 1024, transcendentals=0
        ),
        name="march",
    )
    return call(received, cells, *state, *totals, *consts, section)


def turn_steps(block, rows, begin, end, out):
    own, steps, heights = block.shape
    batch = out.shape[0] // (end - begin)
    for c in range(heights // LANES):
        column = slice(c * LANES, (c + 1) * LANES)
        for b in range(own):
            rows[c, b * steps : (b + 1) * steps, :] = block[b, :, column].astype(F32)
        for t in range(begin, end):
            taken = rows[c, pl.ds(t, own, stride=steps), :].astype(BF16)
            if own < batch:
                taken = jnp.pad(taken, ((0, batch - own), (0, 0)))
            out[(t - begin) * batch : (t - begin + 1) * batch, column] = taken


def fill_slabs(begin, end, own, batch, owners, levels, slabs, blocks, turned, rows, sems):
    arrive = [
        pltpu.make_async_copy(levels.at[pl.ds(owner * own, own)], blocks.at[i], sems.at[0, i])
        for i, owner in enumerate(owners)
    ]
    leave = [pltpu.make_async_copy(turned.at[i], slab, sems.at[1, i]) for i, slab in enumerate(slabs)]
    for copy in arrive:
        copy.start()
    for i in range(len(slabs)):
        arrive[i].wait()
        turn_steps(blocks.at[i], rows, begin, end, turned.at[i])
        leave[i].start()
    for copy in leave:
        copy.wait()


def slab_scratch(number, own, steps, heights, count):
    return [
        pltpu.VMEM((number, own, steps, heights), BF16),
        pltpu.VMEM((number, count, heights), BF16),
        pltpu.VMEM((heights // LANES, own * steps, LANES), F32),
        pltpu.SemaphoreType.DMA((2, number)),
    ]


def deal(levels, begin, end, sections, own, batch):
    steps, heights = levels.shape[1:]
    count = (end - begin) * batch
    anywhere = pl.BlockSpec(memory_space=pl.ANY)

    def kernel(levels, out, *scratch):
        places = [out.at[i] for i in range(sections)]
        fill_slabs(begin, end, own, batch, range(sections), levels, places, *scratch)

    return pl.pallas_call(
        kernel,
        out_shape=jax.ShapeDtypeStruct((sections, count, heights), BF16),
        in_specs=[anywhere],
        out_specs=anywhere,
        scratch_shapes=slab_scratch(sections, own, steps, heights, count),
        compiler_params=pltpu.CompilerParams(vmem_limit_bytes=58 * 1024 * 1024),
        cost_estimate=pl.CostEstimate(flops=1_000_000_000, bytes_accessed=4 * 1024 * 1024, transcendentals=0),
        name="deal",
    )(levels)


def gather_small(value):
    radial, sections = lax.axis_index("radial"), lax.axis_size("range")
    other = lax.ppermute(value, "radial", [(0, 1), (1, 0)])
    pair = jnp.stack([jnp.where(radial == 0, value, other), jnp.where(radial == 0, other, value)])
    section = lax.axis_index("range")
    next_pair = lax.ppermute(pair, "range", [(i, i ^ 1) for i in range(sections)])
    even = section % 2 == 0
    both = jnp.stack([jnp.where(even, pair, next_pair), jnp.where(even, next_pair, pair)])
    held = jnp.zeros((sections, *pair.shape), pair.dtype)
    for d in range(0, sections, 2):
        part = lax.ppermute(both, "range", [(i, i ^ d) for i in range(sections)]) if d else both
        held = lax.dynamic_update_slice_in_dim(held, part, (section ^ d) // 2 * 2, 0)
    return held


def local(refractivity, source, terrain, tile_map):
    sections = lax.axis_size("range")
    owners = sections * lax.axis_size("radial")
    radials, steps, heights = refractivity.shape
    own = radials // sections
    batch = -(-own // 16) * 16
    section = lax.axis_index("range").astype(jnp.int32).reshape(1)

    middle = round(EARLY_SHARE * steps)
    dealt = deal(refractivity, 0, middle, sections, own, batch)
    refractivity, dealt = lax.optimization_barrier((refractivity, dealt))
    early = lax.all_to_all(dealt, "range", 0, 0, tiled=True)
    late = lax.all_to_all(deal(refractivity, middle, steps, sections, own, batch), "range", 0, 0, tiled=True)
    everyone = gather_small(jnp.concatenate([terrain.T, tile_map.T]))
    cells = lax.dynamic_index_in_dim(everyone, lax.axis_index("radial"), 1, keepdims=False)
    consts = [jnp.asarray(v) for v in tables()]
    start = source.reshape(2, ROWS, LANES)
    state = (launch(start, consts), start)
    tiles = TILE_DEV * owners
    totals, *state = march(section, 0, middle, early, cells, state, [], consts, tiles, own, False)
    (totals,) = march(section, middle, steps - middle, late, cells, state, [totals], consts, tiles, own, True)

    everyone, totals = lax.optimization_barrier((everyone, totals))
    sent = lax.all_to_all(
        totals.reshape(owners, TILE_DEV, BINS), ("range", "radial"), 0, 0, tiled=True
    )
    ids = (lax.axis_index("range") * lax.axis_size("radial") + lax.axis_index("radial")) * TILE_DEV
    ids = ids + jnp.arange(TILE_DEV, dtype=jnp.int32)
    counts = jnp.sum((ids[:, None] == everyone[:, :, terrain.shape[1] :].reshape(1, -1)).astype(F32), axis=1)
    return jnp.sum(sent, axis=0) / counts[:, None]


def solution(mesh):
    in_specs = (
        P(("region", "radial"), None, "range"),
        P(None, "region"),
        P(("region", "radial"), "range"),
        P(("region", "radial"), "range"),
    )
    out_specs = P(("region", "range", "radial"), None)
    return jax.shard_map(local, mesh=mesh, in_specs=in_specs, out_specs=out_specs, check_vma=False)
```

```python
import functools
import math

import jax
import jax.numpy as jnp
import ml_dtypes
import numpy as np
from jax import lax
from jax.experimental import pallas as pl
from jax.experimental.pallas import tpu as pltpu
from jax.sharding import PartitionSpec as P

H = 4096
BIN = 32
LANES = 128
ROWS = H // LANES
FOUR = 4
EIGHT = 8
BINS = H // BIN
TILE_DEV = 16
TILT_SLOPE = 2.0
SPREAD_RATE = 0.5
ABSORB_RATE = 0.05
TERRAIN_ROWS = 4
SUB = 8
EARLY_SHARE = 0.75

F32 = jnp.float32
BF16 = jnp.bfloat16


def split_np(table):
    high = table.astype(np.float32).astype(ml_dtypes.bfloat16)
    low = (table - high.astype(np.float64)).astype(ml_dtypes.bfloat16)
    return high, low


def tables():
    n = np.arange(LANES)
    angle = -2.0 * np.pi / LANES * (n[:, None] * n[None, :] % LANES)
    c, s = np.cos(angle), np.sin(angle)
    high, low = split_np(np.block([[c, s], [-s, c]]))
    weights = np.stack([high, low])
    q = np.arange(ROWS)
    angle = -2.0 * np.pi / H * (q[:, None] * n[None, :])
    twiddle = np.stack([np.cos(angle), -np.sin(angle)]).astype(np.float32)
    frequency = q[:, None] + ROWS * n[None, :]
    signed = np.where(frequency >= H // 2, frequency - H, frequency)
    turning = -SPREAD_RATE * (2.0 * np.pi / H * signed) ** 2
    spread = (np.stack([np.cos(turning), -np.sin(turning)]) / H).astype(np.float32)
    rel = np.arange(H).reshape(ROWS, LANES) / H
    tilt = (TILT_SLOPE * rel - 1.0).astype(np.float32)
    depth = np.maximum(rel - 0.75, 0.0) * 4.0
    absorb = np.exp(-ABSORB_RATE * depth * depth).astype(np.float32)
    bins = np.zeros((2 * LANES, BINS), np.float64)
    for lane in range(2 * LANES):
        bins[lane, (lane % LANES) // BIN :: LANES // BIN] = 1.0 / BIN
    return weights, twiddle, spread, tilt, absorb, bins.astype(ml_dtypes.bfloat16)


def phase_polynomials():
    root = 2.0 ** 0.25
    sin_scale = root * math.sqrt(2.0)
    cos_scale = 2.0 * math.sqrt(2.0) / sin_scale
    limit = 7.001
    nodes = 0.5 * limit * limit * (1.0 + np.cos(np.pi * (np.arange(64) + 0.5) / 64))
    phi = np.sqrt(nodes)
    sine = np.polynomial.chebyshev.Chebyshev.fit(
        nodes, sin_scale * np.sin(phi / 4) / phi, 4, domain=[0, limit * limit]
    ).convert(kind=np.polynomial.Polynomial)
    cosine = np.polynomial.chebyshev.Chebyshev.fit(
        nodes, cos_scale * np.cos(phi / 4), 4, domain=[0, limit * limit]
    ).convert(kind=np.polynomial.Polynomial)
    return [float(v) for v in sine.coef], [float(v) for v in cosine.coef]


def unit(number, extent):
    angle = -2.0 * math.pi * (number % extent) / extent
    return math.cos(angle), math.sin(angle)


def cmul_const(value, factor):
    re, im = value
    c, s = factor
    if abs(s) < 1e-12 and c > 0:
        return value
    if abs(c) < 1e-12:
        return (im, -re) if s < 0 else (-im, re)
    return re * c - im * s, re * s + im * c


def add(a, b):
    return a[0] + b[0], a[1] + b[1]


def sub(a, b):
    return a[0] - b[0], a[1] - b[1]


def add_turned(a, b, sign):
    if sign < 0:
        return a[0] + b[1], a[1] - b[0]
    return a[0] - b[1], a[1] + b[0]


def dft4(x, sign):
    a, b = add(x[0], x[2]), sub(x[0], x[2])
    c, d = add(x[1], x[3]), sub(x[1], x[3])
    return [add(a, c), add_turned(b, d, sign), sub(a, c), add_turned(b, d, -sign)]


def eighth(a, sign):
    h = math.sqrt(0.5)
    re, im = a
    if sign < 0:
        return (re + im) * h, (im - re) * h
    return (re - im) * h, (re + im) * h


def dft8(x, sign):
    even = dft4(x[0::2], sign)
    odd = dft4(x[1::2], sign)
    odd[1], odd[3] = eighth(odd[1], sign), eighth(odd[3], sign)
    low = [add(even[0], odd[0]), add(even[1], odd[1]), add_turned(even[2], odd[2], sign), add_turned(even[3], odd[3], sign)]
    high = [sub(even[0], odd[0]), sub(even[1], odd[1]), add_turned(even[2], odd[2], -sign), add_turned(even[3], odd[3], -sign)]
    return low + high


def split(value):
    high = value.astype(BF16)
    low = (value - high.astype(F32)).astype(BF16)
    return high, low


def enter(field, columns, jl):
    parts = dft4(columns, -1)
    for ql in range(FOUR):
        re, im = cmul_const(parts[ql], unit(ql * jl, ROWS))
        field[0, ql * EIGHT + jl] = re
        field[1, ql * EIGHT + jl] = im


def joined(pieces):
    re_high, re_low = split(jnp.concatenate([p[0] for p in pieces], axis=0))
    im_high, im_low = split(jnp.concatenate([p[1] for p in pieces], axis=0))
    return jnp.concatenate([re_high, im_high, re_low, im_low, re_high, im_high], axis=1)


def weighted(left, weights, between=()):
    product = jnp.dot(
        left, jnp.concatenate([weights[0], weights[0], weights[1]]), preferred_element_type=F32
    )
    for work in between:
        work()
    return product


def spread_rows(table, wide):
    for index in np.ndindex(table.shape[:-2]):
        for row in range(table.shape[-2]):
            place = (*index, row)
            wide[place] = jnp.broadcast_to(table[(*index, pl.ds(row, 1))], (SUB, LANES))


def parted(product):
    return [(product[i * SUB : (i + 1) * SUB, :LANES], product[i * SUB : (i + 1) * SUB, LANES:]) for i in range(ROWS)]


Q_ROWS = [ql + FOUR * qh for ql in range(FOUR) for qh in range(EIGHT)]


def forward(field, weights, twiddle, between=()):
    pieces = []
    for ql in range(FOUR):
        column = [(field[0, ql * EIGHT + jl], field[1, ql * EIGHT + jl]) for jl in range(EIGHT)]
        for qh, (re, im) in enumerate(dft8(column, -1)):
            q = ql + FOUR * qh
            c, s = twiddle[0, q], twiddle[1, q]
            pieces.append((re * c + im * s, im * c - re * s))
    return weighted(joined(pieces), weights, between)


def inverse(product, weights, spread, between=()):
    pieces = []
    for q, (re, im) in zip(Q_ROWS, parted(product)):
        c, s = spread[0, q], spread[1, q]
        pieces.append((re * c + im * s, re * s - im * c))
    return weighted(joined(pieces), weights, between)


def leave(back, product, twiddle):
    pieces = []
    for q, (re, im) in zip(Q_ROWS, parted(product)):
        c, s = twiddle[0, q], twiddle[1, q]
        pieces.append((re * c + im * s, re * s - im * c))
    for ql in range(FOUR):
        column = dft8(pieces[ql * EIGHT : (ql + 1) * EIGHT], 1)
        for jl in range(EIGHT):
            back[0, ql * EIGHT + jl] = column[jl][0]
            back[1, ql * EIGHT + jl] = column[jl][1]


def enter_source(field, start):
    for jl in range(EIGHT):
        columns = []
        for jh in range(FOUR):
            j = EIGHT * jh + jl
            columns.append(tuple(jnp.broadcast_to(start[k, j : j + 1, :], (SUB, LANES)) for k in range(2)))
        enter(field, columns, jl)


def launch_kernel(start, weights, twiddle_table, spread_table, back, field, twiddle, spread):
    spread_rows(twiddle_table, twiddle)
    spread_rows(spread_table, spread)
    enter_source(field, start)
    product = inverse(forward(field, weights, twiddle), weights, spread)
    leave(back, product, twiddle)


def launch(start, consts):
    vmem = pl.BlockSpec(memory_space=pltpu.VMEM)
    return pl.pallas_call(
        launch_kernel,
        out_shape=jax.ShapeDtypeStruct((2, ROWS, SUB, LANES), F32),
        in_specs=[vmem] * 4,
        out_specs=vmem,
        scratch_shapes=[pltpu.VMEM((2, ROWS, SUB, LANES), F32)] * 3,
        compiler_params=pltpu.CompilerParams(vmem_limit_bytes=8 * 1024 * 1024),
        cost_estimate=pl.CostEstimate(flops=1_000_000_000, bytes_accessed=1024 * 1024, transcendentals=0),
        name="launch",
    )(start, *consts[:3])


def march_kernel(begin, steps, own, last, levels, cells, launched, entered, *refs):
    if begin > 0:
        totals_in, refs = refs[0], refs[1:]
    weights, refs = refs[0], refs[1:]
    tables, (bins, section, totals), refs = refs[:4], refs[4:7], refs[7:]
    if not last:
        (left_back, left_field), refs = refs[:2], refs[2:]
    (field, back, energy, power), wide_tables = refs[:4], refs[4:]
    for table, place in zip(tables, wide_tables):
        spread_rows(table, place)
    twiddle, spread, tilt, absorb = wide_tables
    sine, cosine = phase_polynomials()
    heights = levels.shape[2]
    batch = levels.shape[1] // steps
    halves = batch // SUB
    lane = lax.broadcasted_iota(jnp.int32, (SUB, LANES), 1)
    radial = lax.broadcasted_iota(jnp.int32, (SUB, LANES), 0)
    at_once = cells.shape[1] // 2

    def rotate(half, t, ground, jls, onward=True):
        for jl in jls:
            column = []
            for ql in range(FOUR):
                c, s = unit(ql * jl, ROWS)
                column.append(
                    cmul_const((back[half, 0, ql * EIGHT + jl], back[half, 1, ql * EIGHT + jl]), (c, -s))
                )
            column = dft4(column, 1)
            moved, value = [], []
            for jh in range(FOUR):
                j = EIGHT * jh + jl
                place = j * LANES
                raw = levels[
                    place // heights, pl.ds(pl.multiple_of(t * batch, batch), batch),
                    place % heights : place % heights + LANES,
                ]
                phi = raw.astype(F32)[half * SUB : (half + 1) * SUB] + tilt[j]
                u = phi * phi
                sin_poly, cos_poly = sine[-1], cosine[-1]
                for a, b in zip(sine[-2::-1], cosine[-2::-1]):
                    sin_poly = sin_poly * u + a
                    cos_poly = cos_poly * u + b
                small = sin_poly * phi
                double = small * cos_poly
                turned_c = 1.0 - double * double
                turned_s = double * (math.sqrt(2.0) - small * small)
                re, im = column[jh]
                if (j + 1) * LANES > 3 * H // 4:
                    loss = absorb[j]
                    re, im = re * loss, im * loss
                re, im = re * turned_c - im * turned_s, re * turned_s + im * turned_c
                if j < TERRAIN_ROWS:
                    open_air = lane + j * LANES >= ground
                    re, im = jnp.where(open_air, re, 0.0), jnp.where(open_air, im, 0.0)
                value.append(re * re + im * im)
                moved.append((re, im))
            if onward:
                enter(field.at[half], moved, jl)
            place = FOUR * jl * SUB
            energy[half, place : place + FOUR * SUB, :] = jnp.concatenate(split(jnp.concatenate(value)), axis=1)

    def binned(half, t):
        summed = jnp.dot(energy[half], bins[...], preferred_element_type=F32)
        row = summed[:SUB]
        for i in range(1, ROWS):
            j = i // FOUR + EIGHT * (i % FOUR)
            row = jnp.where(lane // (LANES // BIN) == j, summed[i * SUB : (i + 1) * SUB], row)
        power[pl.ds(pl.multiple_of(t * batch + half * SUB, SUB), SUB), :] = row

    def ground_of(half, t):
        row = cells[(begin + t) // at_once, pl.ds((begin + t) % at_once, 1), :]
        my_lane = lane == section[0] * own + half * SUB + radial
        return jnp.sum(jnp.where(my_lane, row, 0), axis=1, keepdims=True)

    def turn_of(t, resting, moving):
        ground = ground_of(resting, t)
        pieces = [functools.partial(rotate, resting, t, ground, [jl]) for jl in range(EIGHT)]
        product = forward(field.at[moving], weights, twiddle, pieces[:3])
        binned(moving, jnp.maximum(t - 1, 0) if resting == 0 else t)
        product = inverse(product, weights, spread, pieces[3:6])
        for piece in pieces[6:]:
            piece()
        leave(back.at[moving], product, twiddle)

    def last_turn(t, resting, before):
        rotate(resting, t, ground_of(resting, t), range(EIGHT), False)
        binned(before, t)

    def step(t, carry):
        for half in range(halves):
            turn_of(t, half, (half + 1) % halves)
        return carry

    power[...] = jnp.zeros_like(power)
    back[0] = launched[...]
    for half in range(1, halves):
        if begin == 0:
            enter_source(field.at[half], entered)
        else:
            field[half] = entered[half - 1]
    energy[...] = jnp.zeros_like(energy)
    whole_steps = steps - 1 if last else steps
    lax.fori_loop(0, whole_steps, step, 0)
    if last:
        for half in range(halves - 1):
            turn_of(whole_steps, half, half + 1)
        last_turn(whole_steps, halves - 1, halves - 2)
    binned(halves - 1, steps - 1)
    if not last:
        left_back[...] = back[0]
        for half in range(1, halves):
            left_field[half - 1] = field[half]

    lane = lax.broadcasted_iota(jnp.int32, (1, LANES), 1)
    fit = LANES // batch
    tile_rows = []
    for t in range(steps):
        row = cells[(begin + t) // at_once, at_once + (begin + t) % at_once, :].reshape(1, LANES)
        row = pltpu.roll(row, lax.rem(batch * (t % fit) - section[0] * own + LANES, LANES), 1)
        row = jnp.where(lane % batch < own, row, -1)
        if t % fit == 0:
            tile_rows.append(jnp.where(lane < batch, row, -1))
        else:
            tile_rows[-1] = jnp.where(lane // batch == t % fit, row, tile_rows[-1])
    tile_row = jnp.concatenate(tile_rows, axis=1)
    tiles, cell_count = totals.shape[0], tile_row.shape[1]
    hot = (lax.broadcasted_iota(jnp.int32, (tiles, cell_count), 0) == tile_row).astype(F32).astype(BF16)
    value = power[...]
    high = value.astype(BF16)
    rest = value - high.astype(F32)
    middle = rest.astype(BF16)
    low = (rest - middle.astype(F32)).astype(BF16)
    gain = jnp.dot(hot, high, preferred_element_type=F32)
    gain += jnp.dot(hot, middle, preferred_element_type=F32)
    gain += jnp.dot(hot, low, preferred_element_type=F32)
    totals[...] = gain if begin == 0 else totals_in[...] + gain


def march(section, begin, steps, received, cells, state, totals, consts, tiles, own, last):
    batch = received.shape[1] // steps
    halves = batch // SUB
    vmem = pl.BlockSpec(memory_space=pltpu.VMEM)
    smem = pl.BlockSpec(memory_space=pltpu.SMEM)
    outputs = [jax.ShapeDtypeStruct((tiles, BINS), F32)]
    if not last:
        outputs += [jax.ShapeDtypeStruct((*lead, 2, ROWS, SUB, LANES), F32) for lead in ((), (halves - 1,))]
    call = pl.pallas_call(
        functools.partial(march_kernel, begin, steps, own, last),
        out_shape=outputs,
        in_specs=[vmem] * (10 + len(totals)) + [smem],
        out_specs=[vmem] * len(outputs),
        scratch_shapes=[
            pltpu.VMEM((halves, 2, ROWS, SUB, LANES), F32),
            pltpu.VMEM((halves, 2, ROWS, SUB, LANES), F32),
            pltpu.VMEM((halves, ROWS * SUB, 2 * LANES), BF16),
            pltpu.VMEM((-(-steps * batch // LANES) * LANES, BINS), F32),
        ] + [pltpu.VMEM((*table.shape[:-1], SUB, LANES), F32) for table in consts[1:5]],
        compiler_params=pltpu.CompilerParams(vmem_limit_bytes=12 * 1024 * 1024),
        cost_estimate=pl.CostEstimate(
            flops=steps * 1_600_000_000, bytes_accessed=4 * 1024 * 1024, transcendentals=0
        ),
        name="march",
    )
    return call(received, cells, *state, *totals, *consts, section)


def turn_steps(block, rows, begin, end, out):
    own, steps, heights = block.shape
    batch = out.shape[0] // (end - begin)
    for c in range(heights // LANES):
        column = slice(c * LANES, (c + 1) * LANES)
        for b in range(own):
            rows[c, b * steps : (b + 1) * steps, :] = block[b, :, column].astype(F32)
        for t in range(begin, end):
            taken = rows[c, pl.ds(t, own, stride=steps), :].astype(BF16)
            if own < batch:
                taken = jnp.pad(taken, ((0, batch - own), (0, 0)))
            out[(t - begin) * batch : (t - begin + 1) * batch, column] = taken


def fill_slabs(begin, end, own, batch, owners, levels, slabs, blocks, turned, rows, sems):
    arrive = [
        pltpu.make_async_copy(levels.at[pl.ds(owner * own, own)], blocks.at[i], sems.at[0, i])
        for i, owner in enumerate(owners)
    ]
    leave = [pltpu.make_async_copy(turned.at[i], slab, sems.at[1, i]) for i, slab in enumerate(slabs)]
    for copy in arrive:
        copy.start()
    for i in range(len(slabs)):
        arrive[i].wait()
        turn_steps(blocks.at[i], rows, begin, end, turned.at[i])
        leave[i].start()
    for copy in leave:
        copy.wait()


def slab_scratch(number, own, steps, heights, count):
    return [
        pltpu.VMEM((number, own, steps, heights), BF16),
        pltpu.VMEM((number, count, heights), BF16),
        pltpu.VMEM((heights // LANES, own * steps, LANES), F32),
        pltpu.SemaphoreType.DMA((2, number)),
    ]


def deal(levels, begin, end, sections, own, batch):
    steps, heights = levels.shape[1:]
    count = (end - begin) * batch
    anywhere = pl.BlockSpec(memory_space=pl.ANY)

    def kernel(levels, out, *scratch):
        places = [out.at[i] for i in range(sections)]
        fill_slabs(begin, end, own, batch, range(sections), levels, places, *scratch)

    return pl.pallas_call(
        kernel,
        out_shape=jax.ShapeDtypeStruct((sections, count, heights), BF16),
        in_specs=[anywhere],
        out_specs=anywhere,
        scratch_shapes=slab_scratch(sections, own, steps, heights, count),
        compiler_params=pltpu.CompilerParams(vmem_limit_bytes=58 * 1024 * 1024),
        cost_estimate=pl.CostEstimate(flops=1_000_000_000, bytes_accessed=4 * 1024 * 1024, transcendentals=0),
        name="deal",
    )(levels)


def gather_small(value):
    radial, sections = lax.axis_index("radial"), lax.axis_size("range")
    other = lax.ppermute(value, "radial", [(0, 1), (1, 0)])
    pair = jnp.stack([jnp.where(radial == 0, value, other), jnp.where(radial == 0, other, value)])
    section = lax.axis_index("range")
    next_pair = lax.ppermute(pair, "range", [(i, i ^ 1) for i in range(sections)])
    even = section % 2 == 0
    both = jnp.stack([jnp.where(even, pair, next_pair), jnp.where(even, next_pair, pair)])
    held = jnp.zeros((sections, *pair.shape), pair.dtype)
    for d in range(0, sections, 2):
        part = lax.ppermute(both, "range", [(i, i ^ d) for i in range(sections)]) if d else both
        held = lax.dynamic_update_slice_in_dim(held, part, (section ^ d) // 2 * 2, 0)
    return held


def local(refractivity, source, terrain, tile_map):
    sections = lax.axis_size("range")
    owners = sections * lax.axis_size("radial")
    radials, steps, heights = refractivity.shape
    own = radials // sections
    batch = -(-own // 16) * 16
    section = lax.axis_index("range").astype(jnp.int32).reshape(1)

    middle = round(EARLY_SHARE * steps)
    dealt = deal(refractivity, 0, middle, sections, own, batch)
    refractivity, dealt = lax.optimization_barrier((refractivity, dealt))
    early = lax.all_to_all(dealt, "range", 0, 0, tiled=True)
    late = lax.all_to_all(deal(refractivity, middle, steps, sections, own, batch), "range", 0, 0, tiled=True)
    everyone = gather_small(jnp.concatenate([terrain.T, tile_map.T]))
    cells = lax.dynamic_index_in_dim(everyone, lax.axis_index("radial"), 1, keepdims=False)
    consts = [jnp.asarray(v) for v in tables()]
    start = source.reshape(2, ROWS, LANES)
    state = (launch(start, consts), start)
    tiles = TILE_DEV * owners
    totals, *state = march(section, 0, middle, early, cells, state, [], consts, tiles, own, False)
    (totals,) = march(section, middle, steps - middle, late, cells, state, [totals], consts, tiles, own, True)

    everyone, totals = lax.optimization_barrier((everyone, totals))
    sent = lax.all_to_all(
        totals.reshape(owners, TILE_DEV, BINS), ("range", "radial"), 0, 0, tiled=True
    )
    ids = (lax.axis_index("range") * lax.axis_size("radial") + lax.axis_index("radial")) * TILE_DEV
    ids = ids + jnp.arange(TILE_DEV, dtype=jnp.int32)
    counts = jnp.sum((ids[:, None] == everyone[:, :, terrain.shape[1] :].reshape(1, -1)).astype(F32), axis=1)
    return jnp.sum(sent, axis=0) / counts[:, None]


def solution(mesh):
    in_specs = (
        P(("region", "radial"), None, "range"),
        P(None, "region"),
        P(("region", "radial"), "range"),
        P(("region", "radial"), "range"),
    )
    out_specs = P(("region", "range", "radial"), None)
    return jax.shard_map(local, mesh=mesh, in_specs=in_specs, out_specs=out_specs, check_vma=False)
```

```python
import functools
import math

import jax
import jax.numpy as jnp
import ml_dtypes
import numpy as np
from jax import lax
from jax.experimental import pallas as pl
from jax.experimental.pallas import tpu as pltpu
from jax.sharding import PartitionSpec as P

H = 4096
BIN = 32
LANES = 128
ROWS = H // LANES
FOUR = 4
EIGHT = 8
BINS = H // BIN
TILE_DEV = 16
TILT_SLOPE = 2.0
SPREAD_RATE = 0.5
ABSORB_RATE = 0.05
TERRAIN_ROWS = 4
SUB = 8
EARLY_SHARE = 0.6875

F32 = jnp.float32
BF16 = jnp.bfloat16


def split_np(table):
    high = table.astype(np.float32).astype(ml_dtypes.bfloat16)
    low = (table - high.astype(np.float64)).astype(ml_dtypes.bfloat16)
    return high, low


def tables():
    n = np.arange(LANES)
    angle = -2.0 * np.pi / LANES * (n[:, None] * n[None, :] % LANES)
    c, s = np.cos(angle), np.sin(angle)
    high, low = split_np(np.block([[c, s], [-s, c]]))
    weights = np.stack([high, low])
    q = np.arange(ROWS)
    angle = -2.0 * np.pi / H * (q[:, None] * n[None, :])
    twiddle = np.stack([np.cos(angle), -np.sin(angle)]).astype(np.float32)
    frequency = q[:, None] + ROWS * n[None, :]
    signed = np.where(frequency >= H // 2, frequency - H, frequency)
    turning = -SPREAD_RATE * (2.0 * np.pi / H * signed) ** 2
    spread = (np.stack([np.cos(turning), -np.sin(turning)]) / H).astype(np.float32)
    rel = np.arange(H).reshape(ROWS, LANES) / H
    tilt = (TILT_SLOPE * rel - 1.0).astype(np.float32)
    depth = np.maximum(rel - 0.75, 0.0) * 4.0
    absorb = np.exp(-ABSORB_RATE * depth * depth).astype(np.float32)
    bins = np.zeros((2 * LANES, BINS), np.float64)
    for lane in range(2 * LANES):
        bins[lane, (lane % LANES) // BIN :: LANES // BIN] = 1.0 / BIN
    return weights, twiddle, spread, tilt, absorb, bins.astype(ml_dtypes.bfloat16)


def phase_polynomials():
    root = 2.0 ** 0.25
    sin_scale = root * math.sqrt(2.0)
    cos_scale = 2.0 * math.sqrt(2.0) / sin_scale
    limit = 7.001
    nodes = 0.5 * limit * limit * (1.0 + np.cos(np.pi * (np.arange(64) + 0.5) / 64))
    phi = np.sqrt(nodes)
    sine = np.polynomial.chebyshev.Chebyshev.fit(
        nodes, sin_scale * np.sin(phi / 4) / phi, 4, domain=[0, limit * limit]
    ).convert(kind=np.polynomial.Polynomial)
    cosine = np.polynomial.chebyshev.Chebyshev.fit(
        nodes, cos_scale * np.cos(phi / 4), 4, domain=[0, limit * limit]
    ).convert(kind=np.polynomial.Polynomial)
    return [float(v) for v in sine.coef], [float(v) for v in cosine.coef]


def unit(number, extent):
    angle = -2.0 * math.pi * (number % extent) / extent
    return math.cos(angle), math.sin(angle)


def cmul_const(value, factor):
    re, im = value
    c, s = factor
    if abs(s) < 1e-12 and c > 0:
        return value
    if abs(c) < 1e-12:
        return (im, -re) if s < 0 else (-im, re)
    return re * c - im * s, re * s + im * c


def add(a, b):
    return a[0] + b[0], a[1] + b[1]


def sub(a, b):
    return a[0] - b[0], a[1] - b[1]


def add_turned(a, b, sign):
    if sign < 0:
        return a[0] + b[1], a[1] - b[0]
    return a[0] - b[1], a[1] + b[0]


def dft4(x, sign):
    a, b = add(x[0], x[2]), sub(x[0], x[2])
    c, d = add(x[1], x[3]), sub(x[1], x[3])
    return [add(a, c), add_turned(b, d, sign), sub(a, c), add_turned(b, d, -sign)]


def eighth(a, sign):
    h = math.sqrt(0.5)
    re, im = a
    if sign < 0:
        return (re + im) * h, (im - re) * h
    return (re - im) * h, (re + im) * h


def dft8(x, sign):
    even = dft4(x[0::2], sign)
    odd = dft4(x[1::2], sign)
    odd[1], odd[3] = eighth(odd[1], sign), eighth(odd[3], sign)
    low = [add(even[0], odd[0]), add(even[1], odd[1]), add_turned(even[2], odd[2], sign), add_turned(even[3], odd[3], sign)]
    high = [sub(even[0], odd[0]), sub(even[1], odd[1]), add_turned(even[2], odd[2], -sign), add_turned(even[3], odd[3], -sign)]
    return low + high


def split(value):
    high = value.astype(BF16)
    low = (value - high.astype(F32)).astype(BF16)
    return high, low


def enter(field, columns, jl):
    parts = dft4(columns, -1)
    for ql in range(FOUR):
        re, im = cmul_const(parts[ql], unit(ql * jl, ROWS))
        field[0, ql * EIGHT + jl] = re
        field[1, ql * EIGHT + jl] = im


def joined(pieces):
    re_high, re_low = split(jnp.concatenate([p[0] for p in pieces], axis=0))
    im_high, im_low = split(jnp.concatenate([p[1] for p in pieces], axis=0))
    return jnp.concatenate([re_high, im_high, re_low, im_low, re_high, im_high], axis=1)


def weighted(left, weights, between=()):
    product = jnp.dot(
        left, jnp.concatenate([weights[0], weights[0], weights[1]]), preferred_element_type=F32
    )
    for work in between:
        work()
    return product


def spread_rows(table, wide):
    for index in np.ndindex(table.shape[:-2]):
        for row in range(table.shape[-2]):
            place = (*index, row)
            wide[place] = jnp.broadcast_to(table[(*index, pl.ds(row, 1))], (SUB, LANES))


def parted(product):
    return [(product[i * SUB : (i + 1) * SUB, :LANES], product[i * SUB : (i + 1) * SUB, LANES:]) for i in range(ROWS)]


Q_ROWS = [ql + FOUR * qh for ql in range(FOUR) for qh in range(EIGHT)]


def forward(field, weights, twiddle, between=()):
    pieces = []
    for ql in range(FOUR):
        column = [(field[0, ql * EIGHT + jl], field[1, ql * EIGHT + jl]) for jl in range(EIGHT)]
        for qh, (re, im) in enumerate(dft8(column, -1)):
            q = ql + FOUR * qh
            c, s = twiddle[0, q], twiddle[1, q]
            pieces.append((re * c + im * s, im * c - re * s))
    return weighted(joined(pieces), weights, between)


def inverse(product, weights, spread, between=()):
    pieces = []
    for q, (re, im) in zip(Q_ROWS, parted(product)):
        c, s = spread[0, q], spread[1, q]
        pieces.append((re * c + im * s, re * s - im * c))
    return weighted(joined(pieces), weights, between)


def leave(back, product, twiddle):
    pieces = []
    for q, (re, im) in zip(Q_ROWS, parted(product)):
        c, s = twiddle[0, q], twiddle[1, q]
        pieces.append((re * c + im * s, re * s - im * c))
    for ql in range(FOUR):
        column = dft8(pieces[ql * EIGHT : (ql + 1) * EIGHT], 1)
        for jl in range(EIGHT):
            back[0, ql * EIGHT + jl] = column[jl][0]
            back[1, ql * EIGHT + jl] = column[jl][1]


def enter_source(field, start):
    for jl in range(EIGHT):
        columns = []
        for jh in range(FOUR):
            j = EIGHT * jh + jl
            columns.append(tuple(jnp.broadcast_to(start[k, j : j + 1, :], (SUB, LANES)) for k in range(2)))
        enter(field, columns, jl)


def launch_kernel(start, weights, twiddle_table, spread_table, back, field, twiddle, spread):
    spread_rows(twiddle_table, twiddle)
    spread_rows(spread_table, spread)
    enter_source(field, start)
    product = inverse(forward(field, weights, twiddle), weights, spread)
    leave(back, product, twiddle)


def launch(start, consts):
    vmem = pl.BlockSpec(memory_space=pltpu.VMEM)
    return pl.pallas_call(
        launch_kernel,
        out_shape=jax.ShapeDtypeStruct((2, ROWS, SUB, LANES), F32),
        in_specs=[vmem] * 4,
        out_specs=vmem,
        scratch_shapes=[pltpu.VMEM((2, ROWS, SUB, LANES), F32)] * 3,
        compiler_params=pltpu.CompilerParams(vmem_limit_bytes=8 * 1024 * 1024),
        cost_estimate=pl.CostEstimate(flops=1_000_000_000, bytes_accessed=1024 * 1024, transcendentals=0),
        name="launch",
    )(start, *consts[:3])


def march_kernel(begin, steps, own, last, levels, cells, launched, entered, *refs):
    if begin > 0:
        totals_in, refs = refs[0], refs[1:]
    weights, refs = refs[0], refs[1:]
    tables, (bins, section, totals), refs = refs[:4], refs[4:7], refs[7:]
    if not last:
        (left_back, left_field), refs = refs[:2], refs[2:]
    (field, back, energy, power), wide_tables = refs[:4], refs[4:]
    for table, place in zip(tables, wide_tables):
        spread_rows(table, place)
    twiddle, spread, tilt, absorb = wide_tables
    sine, cosine = phase_polynomials()
    heights = levels.shape[2]
    batch = levels.shape[1] // steps
    halves = batch // SUB
    lane = lax.broadcasted_iota(jnp.int32, (SUB, LANES), 1)
    radial = lax.broadcasted_iota(jnp.int32, (SUB, LANES), 0)
    at_once = cells.shape[1] // 2

    def rotate(half, t, ground, jls, onward=True):
        for jl in jls:
            column = []
            for ql in range(FOUR):
                c, s = unit(ql * jl, ROWS)
                column.append(
                    cmul_const((back[half, 0, ql * EIGHT + jl], back[half, 1, ql * EIGHT + jl]), (c, -s))
                )
            column = dft4(column, 1)
            moved, value = [], []
            for jh in range(FOUR):
                j = EIGHT * jh + jl
                place = j * LANES
                raw = levels[
                    place // heights, pl.ds(pl.multiple_of(t * batch, batch), batch),
                    place % heights : place % heights + LANES,
                ]
                phi = raw.astype(F32)[half * SUB : (half + 1) * SUB] + tilt[j]
                u = phi * phi
                sin_poly, cos_poly = sine[-1], cosine[-1]
                for a, b in zip(sine[-2::-1], cosine[-2::-1]):
                    sin_poly = sin_poly * u + a
                    cos_poly = cos_poly * u + b
                small = sin_poly * phi
                double = small * cos_poly
                turned_c = 1.0 - double * double
                turned_s = double * (math.sqrt(2.0) - small * small)
                re, im = column[jh]
                if (j + 1) * LANES > 3 * H // 4:
                    loss = absorb[j]
                    re, im = re * loss, im * loss
                re, im = re * turned_c - im * turned_s, re * turned_s + im * turned_c
                if j < TERRAIN_ROWS:
                    open_air = lane + j * LANES >= ground
                    re, im = jnp.where(open_air, re, 0.0), jnp.where(open_air, im, 0.0)
                value.append(re * re + im * im)
                moved.append((re, im))
            if onward:
                enter(field.at[half], moved, jl)
            place = FOUR * jl * SUB
            energy[half, place : place + FOUR * SUB, :] = jnp.concatenate(split(jnp.concatenate(value)), axis=1)

    def binned(half, t):
        summed = jnp.dot(energy[half], bins[...], preferred_element_type=F32)
        row = summed[:SUB]
        for i in range(1, ROWS):
            j = i // FOUR + EIGHT * (i % FOUR)
            row = jnp.where(lane // (LANES // BIN) == j, summed[i * SUB : (i + 1) * SUB], row)
        power[pl.ds(pl.multiple_of(t * batch + half * SUB, SUB), SUB), :] = row

    def ground_of(half, t):
        row = cells[(begin + t) // at_once, pl.ds((begin + t) % at_once, 1), :]
        my_lane = lane == section[0] * own + half * SUB + radial
        return jnp.sum(jnp.where(my_lane, row, 0), axis=1, keepdims=True)

    def turn_of(t, resting, moving):
        ground = ground_of(resting, t)
        pieces = [functools.partial(rotate, resting, t, ground, [jl]) for jl in range(EIGHT)]
        product = forward(field.at[moving], weights, twiddle, pieces[:4])
        binned(moving, jnp.maximum(t - 1, 0) if resting == 0 else t)
        product = inverse(product, weights, spread, pieces[4:])
        leave(back.at[moving], product, twiddle)

    def last_turn(t, resting, before):
        rotate(resting, t, ground_of(resting, t), range(EIGHT), False)
        binned(before, t)

    def step(t, carry):
        for half in range(halves):
            turn_of(t, half, (half + 1) % halves)
        return carry

    power[...] = jnp.zeros_like(power)
    back[0] = launched[...]
    for half in range(1, halves):
        if begin == 0:
            enter_source(field.at[half], entered)
        else:
            field[half] = entered[half - 1]
    energy[...] = jnp.zeros_like(energy)
    whole_steps = steps - 1 if last else steps
    lax.fori_loop(0, whole_steps, step, 0)
    if last:
        for half in range(halves - 1):
            turn_of(whole_steps, half, half + 1)
        last_turn(whole_steps, halves - 1, halves - 2)
    binned(halves - 1, steps - 1)
    if not last:
        left_back[...] = back[0]
        for half in range(1, halves):
            left_field[half - 1] = field[half]

    lane = lax.broadcasted_iota(jnp.int32, (1, LANES), 1)
    fit = LANES // batch
    tile_rows = []
    for t in range(steps):
        row = cells[(begin + t) // at_once, at_once + (begin + t) % at_once, :].reshape(1, LANES)
        row = pltpu.roll(row, lax.rem(batch * (t % fit) - section[0] * own + LANES, LANES), 1)
        row = jnp.where(lane % batch < own, row, -1)
        if t % fit == 0:
            tile_rows.append(jnp.where(lane < batch, row, -1))
        else:
            tile_rows[-1] = jnp.where(lane // batch == t % fit, row, tile_rows[-1])
    tile_row = jnp.concatenate(tile_rows, axis=1)
    tiles, cell_count = totals.shape[0], tile_row.shape[1]
    hot = (lax.broadcasted_iota(jnp.int32, (tiles, cell_count), 0) == tile_row).astype(F32).astype(BF16)
    value = power[...]
    high = value.astype(BF16)
    rest = value - high.astype(F32)
    middle = rest.astype(BF16)
    low = (rest - middle.astype(F32)).astype(BF16)
    gain = jnp.dot(hot, high, preferred_element_type=F32)
    gain += jnp.dot(hot, middle, preferred_element_type=F32)
    gain += jnp.dot(hot, low, preferred_element_type=F32)
    totals[...] = gain if begin == 0 else totals_in[...] + gain


def march(section, begin, steps, received, cells, state, totals, consts, tiles, own, last):
    batch = received.shape[1] // steps
    halves = batch // SUB
    vmem = pl.BlockSpec(memory_space=pltpu.VMEM)
    smem = pl.BlockSpec(memory_space=pltpu.SMEM)
    outputs = [jax.ShapeDtypeStruct((tiles, BINS), F32)]
    if not last:
        outputs += [jax.ShapeDtypeStruct((*lead, 2, ROWS, SUB, LANES), F32) for lead in ((), (halves - 1,))]
    call = pl.pallas_call(
        functools.partial(march_kernel, begin, steps, own, last),
        out_shape=outputs,
        in_specs=[vmem] * (10 + len(totals)) + [smem],
        out_specs=[vmem] * len(outputs),
        scratch_shapes=[
            pltpu.VMEM((halves, 2, ROWS, SUB, LANES), F32),
            pltpu.VMEM((halves, 2, ROWS, SUB, LANES), F32),
            pltpu.VMEM((halves, ROWS * SUB, 2 * LANES), BF16),
            pltpu.VMEM((-(-steps * batch // LANES) * LANES, BINS), F32),
        ] + [pltpu.VMEM((*table.shape[:-1], SUB, LANES), F32) for table in consts[1:5]],
        compiler_params=pltpu.CompilerParams(vmem_limit_bytes=12 * 1024 * 1024),
        cost_estimate=pl.CostEstimate(
            flops=steps * 1_600_000_000, bytes_accessed=4 * 1024 * 1024, transcendentals=0
        ),
        name="march",
    )
    return call(received, cells, *state, *totals, *consts, section)


def turn_steps(block, rows, begin, end, out):
    own, steps, heights = block.shape
    batch = out.shape[0] // (end - begin)
    for c in range(heights // LANES):
        column = slice(c * LANES, (c + 1) * LANES)
        for b in range(own):
            rows[c, b * steps : (b + 1) * steps, :] = block[b, :, column].astype(F32)
        for t in range(begin, end):
            taken = rows[c, pl.ds(t, own, stride=steps), :].astype(BF16)
            if own < batch:
                taken = jnp.pad(taken, ((0, batch - own), (0, 0)))
            out[(t - begin) * batch : (t - begin + 1) * batch, column] = taken


def fill_slabs(begin, end, own, batch, owners, levels, slabs, blocks, turned, rows, sems):
    arrive = [
        pltpu.make_async_copy(levels.at[pl.ds(owner * own, own)], blocks.at[i], sems.at[0, i])
        for i, owner in enumerate(owners)
    ]
    leave = [pltpu.make_async_copy(turned.at[i], slab, sems.at[1, i]) for i, slab in enumerate(slabs)]
    for copy in arrive:
        copy.start()
    for i in range(len(slabs)):
        arrive[i].wait()
        turn_steps(blocks.at[i], rows.at[i % 2], begin, end, turned.at[i])
        leave[i].start()
    for copy in leave:
        copy.wait()


def slab_scratch(number, own, steps, heights, count):
    return [
        pltpu.VMEM((number, own, steps, heights), BF16),
        pltpu.VMEM((number, count, heights), BF16),
        pltpu.VMEM((2, heights // LANES, own * steps, LANES), F32),
        pltpu.SemaphoreType.DMA((2, number)),
    ]


def deal(levels, begin, end, sections, own, batch):
    steps, heights = levels.shape[1:]
    count = (end - begin) * batch
    anywhere = pl.BlockSpec(memory_space=pl.ANY)

    def kernel(levels, out, *scratch):
        places = [out.at[i] for i in range(sections)]
        fill_slabs(begin, end, own, batch, range(sections), levels, places, *scratch)

    return pl.pallas_call(
        kernel,
        out_shape=jax.ShapeDtypeStruct((sections, count, heights), BF16),
        in_specs=[anywhere],
        out_specs=anywhere,
        scratch_shapes=slab_scratch(sections, own, steps, heights, count),
        compiler_params=pltpu.CompilerParams(vmem_limit_bytes=58 * 1024 * 1024),
        cost_estimate=pl.CostEstimate(flops=1_000_000_000, bytes_accessed=4 * 1024 * 1024, transcendentals=0),
        name="deal",
    )(levels)


def gather_small(value):
    radial, sections = lax.axis_index("radial"), lax.axis_size("range")
    other = lax.ppermute(value, "radial", [(0, 1), (1, 0)])
    pair = jnp.stack([jnp.where(radial == 0, value, other), jnp.where(radial == 0, other, value)])
    section = lax.axis_index("range")
    next_pair = lax.ppermute(pair, "range", [(i, i ^ 1) for i in range(sections)])
    even = section % 2 == 0
    both = jnp.stack([jnp.where(even, pair, next_pair), jnp.where(even, next_pair, pair)])
    held = jnp.zeros((sections, *pair.shape), pair.dtype)
    for d in range(0, sections, 2):
        part = lax.ppermute(both, "range", [(i, i ^ d) for i in range(sections)]) if d else both
        held = lax.dynamic_update_slice_in_dim(held, part, (section ^ d) // 2 * 2, 0)
    return held


def local(refractivity, source, terrain, tile_map):
    sections = lax.axis_size("range")
    owners = sections * lax.axis_size("radial")
    radials, steps, heights = refractivity.shape
    own = radials // sections
    batch = -(-own // 16) * 16
    section = lax.axis_index("range").astype(jnp.int32).reshape(1)

    middle = round(EARLY_SHARE * steps)
    dealt = deal(refractivity, 0, middle, sections, own, batch)
    refractivity, dealt = lax.optimization_barrier((refractivity, dealt))
    early = lax.all_to_all(dealt, "range", 0, 0, tiled=True)
    late = lax.all_to_all(deal(refractivity, middle, steps, sections, own, batch), "range", 0, 0, tiled=True)
    everyone = gather_small(jnp.concatenate([terrain.T, tile_map.T]))
    cells = lax.dynamic_index_in_dim(everyone, lax.axis_index("radial"), 1, keepdims=False)
    consts = [jnp.asarray(v) for v in tables()]
    start = source.reshape(2, ROWS, LANES)
    state = (launch(start, consts), start)
    tiles = TILE_DEV * owners
    totals, *state = march(section, 0, middle, early, cells, state, [], consts, tiles, own, False)
    (totals,) = march(section, middle, steps - middle, late, cells, state, [totals], consts, tiles, own, True)

    everyone, totals = lax.optimization_barrier((everyone, totals))
    sent = lax.all_to_all(
        totals.reshape(owners, TILE_DEV, BINS), ("range", "radial"), 0, 0, tiled=True
    )
    ids = (lax.axis_index("range") * lax.axis_size("radial") + lax.axis_index("radial")) * TILE_DEV
    ids = ids + jnp.arange(TILE_DEV, dtype=jnp.int32)
    counts = jnp.sum((ids[:, None] == everyone[:, :, terrain.shape[1] :].reshape(1, -1)).astype(F32), axis=1)
    return jnp.sum(sent, axis=0) / counts[:, None]


def solution(mesh):
    in_specs = (
        P(("region", "radial"), None, "range"),
        P(None, "region"),
        P(("region", "radial"), "range"),
        P(("region", "radial"), "range"),
    )
    out_specs = P(("region", "range", "radial"), None)
    return jax.shard_map(local, mesh=mesh, in_specs=in_specs, out_specs=out_specs, check_vma=False)
```

```python
import functools
import math

import jax
import jax.numpy as jnp
import ml_dtypes
import numpy as np
from jax import lax
from jax.experimental import pallas as pl
from jax.experimental.pallas import tpu as pltpu
from jax.sharding import PartitionSpec as P

H = 4096
BIN = 32
LANES = 128
ROWS = H // LANES
FOUR = 4
EIGHT = 8
BINS = H // BIN
TILE_DEV = 16
TILT_SLOPE = 2.0
SPREAD_RATE = 0.5
ABSORB_RATE = 0.05
TERRAIN_ROWS = 4
SUB = 8
EARLY_SHARE = 0.6875

F32 = jnp.float32
BF16 = jnp.bfloat16


def split_np(table):
    high = table.astype(np.float32).astype(ml_dtypes.bfloat16)
    low = (table - high.astype(np.float64)).astype(ml_dtypes.bfloat16)
    return high, low


def tables():
    n = np.arange(LANES)
    angle = -2.0 * np.pi / LANES * (n[:, None] * n[None, :] % LANES)
    c, s = np.cos(angle), np.sin(angle)
    high, low = split_np(np.block([[c, s], [-s, c]]))
    weights = np.stack([high, low])
    q = np.arange(ROWS)
    angle = -2.0 * np.pi / H * (q[:, None] * n[None, :])
    twiddle = np.stack([np.cos(angle), -np.sin(angle)]).astype(np.float32)
    frequency = q[:, None] + ROWS * n[None, :]
    signed = np.where(frequency >= H // 2, frequency - H, frequency)
    turning = -SPREAD_RATE * (2.0 * np.pi / H * signed) ** 2
    spread = (np.stack([np.cos(turning), -np.sin(turning)]) / H).astype(np.float32)
    rel = np.arange(H).reshape(ROWS, LANES) / H
    tilt = (TILT_SLOPE * rel - 1.0).astype(np.float32)
    depth = np.maximum(rel - 0.75, 0.0) * 4.0
    absorb = np.exp(-ABSORB_RATE * depth * depth).astype(np.float32)
    bins = np.zeros((2 * LANES, BINS), np.float64)
    for lane in range(2 * LANES):
        bins[lane, (lane % LANES) // BIN :: LANES // BIN] = 1.0 / BIN
    return weights, twiddle, spread, tilt, absorb, bins.astype(ml_dtypes.bfloat16)


def phase_polynomials():
    root = 2.0 ** 0.25
    sin_scale = root * math.sqrt(2.0)
    cos_scale = 2.0 * math.sqrt(2.0) / sin_scale
    limit = 7.001
    nodes = 0.5 * limit * limit * (1.0 + np.cos(np.pi * (np.arange(64) + 0.5) / 64))
    phi = np.sqrt(nodes)
    sine = np.polynomial.chebyshev.Chebyshev.fit(
        nodes, sin_scale * np.sin(phi / 4) / phi, 4, domain=[0, limit * limit]
    ).convert(kind=np.polynomial.Polynomial)
    cosine = np.polynomial.chebyshev.Chebyshev.fit(
        nodes, cos_scale * np.cos(phi / 4), 4, domain=[0, limit * limit]
    ).convert(kind=np.polynomial.Polynomial)
    return [float(v) for v in sine.coef], [float(v) for v in cosine.coef]


def unit(number, extent):
    angle = -2.0 * math.pi * (number % extent) / extent
    return math.cos(angle), math.sin(angle)


def cmul_const(value, factor):
    re, im = value
    c, s = factor
    if abs(s) < 1e-12 and c > 0:
        return value
    if abs(c) < 1e-12:
        return (im, -re) if s < 0 else (-im, re)
    return re * c - im * s, re * s + im * c


def add(a, b):
    return a[0] + b[0], a[1] + b[1]


def sub(a, b):
    return a[0] - b[0], a[1] - b[1]


def add_turned(a, b, sign):
    if sign < 0:
        return a[0] + b[1], a[1] - b[0]
    return a[0] - b[1], a[1] + b[0]


def dft4(x, sign):
    a, b = add(x[0], x[2]), sub(x[0], x[2])
    c, d = add(x[1], x[3]), sub(x[1], x[3])
    return [add(a, c), add_turned(b, d, sign), sub(a, c), add_turned(b, d, -sign)]


def eighth(a, sign):
    h = math.sqrt(0.5)
    re, im = a
    if sign < 0:
        return (re + im) * h, (im - re) * h
    return (re - im) * h, (re + im) * h


def dft8(x, sign):
    even = dft4(x[0::2], sign)
    odd = dft4(x[1::2], sign)
    odd[1], odd[3] = eighth(odd[1], sign), eighth(odd[3], sign)
    low = [add(even[0], odd[0]), add(even[1], odd[1]), add_turned(even[2], odd[2], sign), add_turned(even[3], odd[3], sign)]
    high = [sub(even[0], odd[0]), sub(even[1], odd[1]), add_turned(even[2], odd[2], -sign), add_turned(even[3], odd[3], -sign)]
    return low + high


def split(value):
    high = value.astype(BF16)
    low = (value - high.astype(F32)).astype(BF16)
    return high, low


def enter(field, columns, jl):
    parts = dft4(columns, -1)
    for ql in range(FOUR):
        re, im = cmul_const(parts[ql], unit(ql * jl, ROWS))
        field[0, ql * EIGHT + jl] = re
        field[1, ql * EIGHT + jl] = im


def joined(pieces):
    re_high, re_low = split(jnp.concatenate([p[0] for p in pieces], axis=0))
    im_high, im_low = split(jnp.concatenate([p[1] for p in pieces], axis=0))
    return jnp.concatenate([re_high, im_high, re_low, im_low, re_high, im_high], axis=1)


def weighted(left, weights, between=()):
    product = jnp.dot(
        left, jnp.concatenate([weights[0], weights[0], weights[1]]), preferred_element_type=F32
    )
    for work in between:
        work()
    return product


def spread_rows(table, wide):
    for index in np.ndindex(table.shape[:-2]):
        for row in range(table.shape[-2]):
            place = (*index, row)
            wide[place] = jnp.broadcast_to(table[(*index, pl.ds(row, 1))], (SUB, LANES))


def parted(product):
    return [(product[i * SUB : (i + 1) * SUB, :LANES], product[i * SUB : (i + 1) * SUB, LANES:]) for i in range(ROWS)]


Q_ROWS = [ql + FOUR * qh for ql in range(FOUR) for qh in range(EIGHT)]


def forward(field, weights, twiddle, between=()):
    pieces = []
    for ql in range(FOUR):
        column = [(field[0, ql * EIGHT + jl], field[1, ql * EIGHT + jl]) for jl in range(EIGHT)]
        for qh, (re, im) in enumerate(dft8(column, -1)):
            q = ql + FOUR * qh
            c, s = twiddle[0, q], twiddle[1, q]
            pieces.append((re * c + im * s, im * c - re * s))
    return weighted(joined(pieces), weights, between)


def inverse(product, weights, spread, between=()):
    pieces = []
    for q, (re, im) in zip(Q_ROWS, parted(product)):
        c, s = spread[0, q], spread[1, q]
        pieces.append((re * c + im * s, re * s - im * c))
    return weighted(joined(pieces), weights, between)


def leave(back, product, twiddle):
    pieces = []
    for q, (re, im) in zip(Q_ROWS, parted(product)):
        c, s = twiddle[0, q], twiddle[1, q]
        pieces.append((re * c + im * s, re * s - im * c))
    for ql in range(FOUR):
        column = dft8(pieces[ql * EIGHT : (ql + 1) * EIGHT], 1)
        for jl in range(EIGHT):
            back[0, ql * EIGHT + jl] = column[jl][0]
            back[1, ql * EIGHT + jl] = column[jl][1]


def enter_source(field, start):
    for jl in range(EIGHT):
        columns = []
        for jh in range(FOUR):
            j = EIGHT * jh + jl
            columns.append(tuple(jnp.broadcast_to(start[k, j : j + 1, :], (SUB, LANES)) for k in range(2)))
        enter(field, columns, jl)


def launch_kernel(start, weights, twiddle_table, spread_table, back, field, twiddle, spread):
    spread_rows(twiddle_table, twiddle)
    spread_rows(spread_table, spread)
    enter_source(field, start)
    product = inverse(forward(field, weights, twiddle), weights, spread)
    leave(back, product, twiddle)


def launch(start, consts):
    vmem = pl.BlockSpec(memory_space=pltpu.VMEM)
    return pl.pallas_call(
        launch_kernel,
        out_shape=jax.ShapeDtypeStruct((2, ROWS, SUB, LANES), F32),
        in_specs=[vmem] * 4,
        out_specs=vmem,
        scratch_shapes=[pltpu.VMEM((2, ROWS, SUB, LANES), F32)] * 3,
        compiler_params=pltpu.CompilerParams(vmem_limit_bytes=8 * 1024 * 1024),
        cost_estimate=pl.CostEstimate(flops=1_000_000_000, bytes_accessed=1024 * 1024, transcendentals=0),
        name="launch",
    )(start, *consts[:3])


def march_kernel(begin, steps, own, last, levels, cells, launched, entered, *refs):
    if begin > 0:
        totals_in, refs = refs[0], refs[1:]
    weights, refs = refs[0], refs[1:]
    tables, (bins, section, totals), refs = refs[:4], refs[4:7], refs[7:]
    if not last:
        (left_back, left_field), refs = refs[:2], refs[2:]
    (field, back, energy, power), wide_tables = refs[:4], refs[4:]
    for table, place in zip(tables, wide_tables):
        spread_rows(table, place)
    twiddle, spread, tilt, absorb = wide_tables
    sine, cosine = phase_polynomials()
    heights = levels.shape[2]
    batch = levels.shape[1] // steps
    halves = batch // SUB
    lane = lax.broadcasted_iota(jnp.int32, (SUB, LANES), 1)
    radial = lax.broadcasted_iota(jnp.int32, (SUB, LANES), 0)
    at_once = cells.shape[1] // 2

    def rotate(half, t, ground, jls, onward=True):
        for jl in jls:
            column = []
            for ql in range(FOUR):
                c, s = unit(ql * jl, ROWS)
                column.append(
                    cmul_const((back[half, 0, ql * EIGHT + jl], back[half, 1, ql * EIGHT + jl]), (c, -s))
                )
            column = dft4(column, 1)
            moved, value = [], []
            for jh in range(FOUR):
                j = EIGHT * jh + jl
                place = j * LANES
                raw = levels[
                    place // heights, pl.ds(pl.multiple_of(t * batch, batch), batch),
                    place % heights : place % heights + LANES,
                ]
                phi = raw.astype(F32)[half * SUB : (half + 1) * SUB] + tilt[j]
                u = phi * phi
                sin_poly, cos_poly = sine[-1], cosine[-1]
                for a, b in zip(sine[-2::-1], cosine[-2::-1]):
                    sin_poly = sin_poly * u + a
                    cos_poly = cos_poly * u + b
                small = sin_poly * phi
                double = small * cos_poly
                turned_c = 1.0 - double * double
                turned_s = double * (math.sqrt(2.0) - small * small)
                re, im = column[jh]
                if (j + 1) * LANES > 3 * H // 4:
                    loss = absorb[j]
                    re, im = re * loss, im * loss
                re, im = re * turned_c - im * turned_s, re * turned_s + im * turned_c
                if j < TERRAIN_ROWS:
                    open_air = lane + j * LANES >= ground
                    re, im = jnp.where(open_air, re, 0.0), jnp.where(open_air, im, 0.0)
                value.append(re * re + im * im)
                moved.append((re, im))
            if onward:
                enter(field.at[half], moved, jl)
            place = FOUR * jl * SUB
            energy[half, place : place + FOUR * SUB, :] = jnp.concatenate(split(jnp.concatenate(value)), axis=1)

    def binned(half, t):
        summed = jnp.dot(energy[half], bins[...], preferred_element_type=F32)
        row = summed[:SUB]
        for i in range(1, ROWS):
            j = i // FOUR + EIGHT * (i % FOUR)
            row = jnp.where(lane // (LANES // BIN) == j, summed[i * SUB : (i + 1) * SUB], row)
        power[pl.ds(pl.multiple_of(t * batch + half * SUB, SUB), SUB), :] = row

    def ground_of(half, t):
        row = cells[(begin + t) // at_once, pl.ds((begin + t) % at_once, 1), :]
        my_lane = lane == section[0] * own + half * SUB + radial
        return jnp.sum(jnp.where(my_lane, row, 0), axis=1, keepdims=True)

    def turn_of(t, resting, moving):
        ground = ground_of(resting, t)
        pieces = [functools.partial(rotate, resting, t, ground, [jl]) for jl in range(EIGHT)]
        product = forward(field.at[moving], weights, twiddle, pieces[:3])
        binned(moving, jnp.maximum(t - 1, 0) if resting == 0 else t)
        product = inverse(product, weights, spread, pieces[3:6])
        for piece in pieces[6:]:
            piece()
        leave(back.at[moving], product, twiddle)

    def last_turn(t, resting, before):
        rotate(resting, t, ground_of(resting, t), range(EIGHT), False)
        binned(before, t)

    def step(t, carry):
        for half in range(halves):
            turn_of(t, half, (half + 1) % halves)
        return carry

    power[...] = jnp.zeros_like(power)
    back[0] = launched[...]
    for half in range(1, halves):
        if begin == 0:
            enter_source(field.at[half], entered)
        else:
            field[half] = entered[half - 1]
    energy[...] = jnp.zeros_like(energy)
    whole_steps = steps - 1 if last else steps
    lax.fori_loop(0, whole_steps, step, 0)
    if last:
        for half in range(halves - 1):
            turn_of(whole_steps, half, half + 1)
        last_turn(whole_steps, halves - 1, halves - 2)
    binned(halves - 1, steps - 1)
    if not last:
        left_back[...] = back[0]
        for half in range(1, halves):
            left_field[half - 1] = field[half]

    lane = lax.broadcasted_iota(jnp.int32, (1, LANES), 1)
    fit = LANES // batch
    tile_rows = []
    for t in range(steps):
        row = cells[(begin + t) // at_once, at_once + (begin + t) % at_once, :].reshape(1, LANES)
        row = pltpu.roll(row, lax.rem(batch * (t % fit) - section[0] * own + LANES, LANES), 1)
        row = jnp.where(lane % batch < own, row, -1)
        if t % fit == 0:
            tile_rows.append(jnp.where(lane < batch, row, -1))
        else:
            tile_rows[-1] = jnp.where(lane // batch == t % fit, row, tile_rows[-1])
    tile_row = jnp.concatenate(tile_rows, axis=1)
    tiles, cell_count = totals.shape[0], tile_row.shape[1]
    hot = (lax.broadcasted_iota(jnp.int32, (tiles, cell_count), 0) == tile_row).astype(F32).astype(BF16)
    value = power[...]
    high = value.astype(BF16)
    rest = value - high.astype(F32)
    middle = rest.astype(BF16)
    low = (rest - middle.astype(F32)).astype(BF16)
    gain = jnp.dot(hot, high, preferred_element_type=F32)
    gain += jnp.dot(hot, middle, preferred_element_type=F32)
    gain += jnp.dot(hot, low, preferred_element_type=F32)
    totals[...] = gain if begin == 0 else totals_in[...] + gain


def march(section, begin, steps, received, cells, state, totals, consts, tiles, own, last):
    batch = received.shape[1] // steps
    halves = batch // SUB
    vmem = pl.BlockSpec(memory_space=pltpu.VMEM)
    smem = pl.BlockSpec(memory_space=pltpu.SMEM)
    outputs = [jax.ShapeDtypeStruct((tiles, BINS), F32)]
    if not last:
        outputs += [jax.ShapeDtypeStruct((*lead, 2, ROWS, SUB, LANES), F32) for lead in ((), (halves - 1,))]
    call = pl.pallas_call(
        functools.partial(march_kernel, begin, steps, own, last),
        out_shape=outputs,
        in_specs=[vmem] * (10 + len(totals)) + [smem],
        out_specs=[vmem] * len(outputs),
        scratch_shapes=[
            pltpu.VMEM((halves, 2, ROWS, SUB, LANES), F32),
            pltpu.VMEM((halves, 2, ROWS, SUB, LANES), F32),
            pltpu.VMEM((halves, ROWS * SUB, 2 * LANES), BF16),
            pltpu.VMEM((-(-steps * batch // LANES) * LANES, BINS), F32),
        ] + [pltpu.VMEM((*table.shape[:-1], SUB, LANES), F32) for table in consts[1:5]],
        compiler_params=pltpu.CompilerParams(vmem_limit_bytes=12 * 1024 * 1024),
        cost_estimate=pl.CostEstimate(
            flops=steps * 1_600_000_000, bytes_accessed=4 * 1024 * 1024, transcendentals=0
        ),
        name="march",
    )
    return call(received, cells, *state, *totals, *consts, section)


def turn_steps(block, rows, begin, end, out):
    own, steps, heights = block.shape
    batch = out.shape[0] // (end - begin)
    for c in range(heights // LANES):
        column = slice(c * LANES, (c + 1) * LANES)
        for b in range(own):
            rows[c, b * steps : (b + 1) * steps, :] = block[b, :, column].astype(F32)
        for t in range(begin, end):
            taken = rows[c, pl.ds(t, own, stride=steps), :].astype(BF16)
            if own < batch:
                taken = jnp.pad(taken, ((0, batch - own), (0, 0)))
            out[(t - begin) * batch : (t - begin + 1) * batch, column] = taken


def fill_slabs(begin, end, own, batch, owners, levels, slabs, blocks, turned, rows, sems):
    arrive = [
        pltpu.make_async_copy(levels.at[pl.ds(owner * own, own)], blocks.at[i], sems.at[0, i])
        for i, owner in enumerate(owners)
    ]
    leave = [pltpu.make_async_copy(turned.at[i], slab, sems.at[1, i]) for i, slab in enumerate(slabs)]
    for copy in arrive:
        copy.start()
    for i in range(len(slabs)):
        arrive[i].wait()
        turn_steps(blocks.at[i], rows.at[i % 2], begin, end, turned.at[i])
        leave[i].start()
    for copy in leave:
        copy.wait()


def slab_scratch(number, own, steps, heights, count):
    return [
        pltpu.VMEM((number, own, steps, heights), BF16),
        pltpu.VMEM((number, count, heights), BF16),
        pltpu.VMEM((2, heights // LANES, own * steps, LANES), F32),
        pltpu.SemaphoreType.DMA((2, number)),
    ]


def deal(levels, begin, end, sections, own, batch):
    steps, heights = levels.shape[1:]
    count = (end - begin) * batch
    anywhere = pl.BlockSpec(memory_space=pl.ANY)

    def kernel(levels, out, *scratch):
        places = [out.at[i] for i in range(sections)]
        fill_slabs(begin, end, own, batch, range(sections), levels, places, *scratch)

    return pl.pallas_call(
        kernel,
        out_shape=jax.ShapeDtypeStruct((sections, count, heights), BF16),
        in_specs=[anywhere],
        out_specs=anywhere,
        scratch_shapes=slab_scratch(sections, own, steps, heights, count),
        compiler_params=pltpu.CompilerParams(vmem_limit_bytes=58 * 1024 * 1024),
        cost_estimate=pl.CostEstimate(flops=1_000_000_000, bytes_accessed=4 * 1024 * 1024, transcendentals=0),
        name="deal",
    )(levels)


def gather_small(value):
    radial, sections = lax.axis_index("radial"), lax.axis_size("range")
    other = lax.ppermute(value, "radial", [(0, 1), (1, 0)])
    pair = jnp.stack([jnp.where(radial == 0, value, other), jnp.where(radial == 0, other, value)])
    section = lax.axis_index("range")
    next_pair = lax.ppermute(pair, "range", [(i, i ^ 1) for i in range(sections)])
    even = section % 2 == 0
    both = jnp.stack([jnp.where(even, pair, next_pair), jnp.where(even, next_pair, pair)])
    held = jnp.zeros((sections, *pair.shape), pair.dtype)
    for d in range(0, sections, 2):
        part = lax.ppermute(both, "range", [(i, i ^ d) for i in range(sections)]) if d else both
        held = lax.dynamic_update_slice_in_dim(held, part, (section ^ d) // 2 * 2, 0)
    return held


def local(refractivity, source, terrain, tile_map):
    sections = lax.axis_size("range")
    owners = sections * lax.axis_size("radial")
    radials, steps, heights = refractivity.shape
    own = radials // sections
    batch = -(-own // 16) * 16
    section = lax.axis_index("range").astype(jnp.int32).reshape(1)

    middle = round(EARLY_SHARE * steps)
    dealt = deal(refractivity, 0, middle, sections, own, batch)
    refractivity, dealt = lax.optimization_barrier((refractivity, dealt))
    early = lax.all_to_all(dealt, "range", 0, 0, tiled=True)
    late = lax.all_to_all(deal(refractivity, middle, steps, sections, own, batch), "range", 0, 0, tiled=True)
    everyone = gather_small(jnp.concatenate([terrain.T, tile_map.T]))
    cells = lax.dynamic_index_in_dim(everyone, lax.axis_index("radial"), 1, keepdims=False)
    consts = [jnp.asarray(v) for v in tables()]
    start = source.reshape(2, ROWS, LANES)
    state = (launch(start, consts), start)
    tiles = TILE_DEV * owners
    totals, *state = march(section, 0, middle, early, cells, state, [], consts, tiles, own, False)
    (totals,) = march(section, middle, steps - middle, late, cells, state, [totals], consts, tiles, own, True)

    everyone, totals = lax.optimization_barrier((everyone, totals))
    sent = lax.all_to_all(
        totals.reshape(owners, TILE_DEV, BINS), ("range", "radial"), 0, 0, tiled=True
    )
    ids = (lax.axis_index("range") * lax.axis_size("radial") + lax.axis_index("radial")) * TILE_DEV
    ids = ids + jnp.arange(TILE_DEV, dtype=jnp.int32)
    counts = jnp.sum((ids[:, None] == everyone[:, :, terrain.shape[1] :].reshape(1, -1)).astype(F32), axis=1)
    return jnp.sum(sent, axis=0) / counts[:, None]


def solution(mesh):
    in_specs = (
        P(("region", "radial"), None, "range"),
        P(None, "region"),
        P(("region", "radial"), "range"),
        P(("region", "radial"), "range"),
    )
    out_specs = P(("region", "range", "radial"), None)
    return jax.shard_map(local, mesh=mesh, in_specs=in_specs, out_specs=out_specs, check_vma=False)
```
